32 devices in a mesh: grid: 4 (over y, x), strip: 8 (over z, core).
Axes of the slice: x: 2, y: 2, z: 4, core: 2. Of those that a mesh axis runs over, the one named last changes fastest.
Arguments:
- features: bfloat16 [4, 96, 72, 128], P('grid', 'strip'), may hold values from -6 to 6
- cell_frame: int32 [4, 96, 72], P('grid', 'strip'), may hold values from 0 to 3, as said below
- cotangent: bfloat16 [4, 96, 72, 128], P('grid', 'strip'), may hold values from -12 to 12
- attend_weight: float32 [2, 128, 384], replicated, may hold values from -0.5 to 0.5
- output_weight: float32 [2, 128, 128], replicated, may hold values from -1.5 to 1.5
- expand_weight: float32 [2, 128, 256], replicated, may hold values from -0.5 to 0.5
- reduce_weight: float32 [2, 256, 128], replicated, may hold values from -0.375 to 0.375
- position_table: float32 [2, 144, 128], replicated, may hold values from -4 to 4
- norm_params: float32 [2, 4, 128], replicated, may hold values from -0.75 to 1.75, as said below
- attend_first: float32 [2, 128, 384], replicated, may hold values from -0.0029296875 to 0.0029296875
- output_first: float32 [2, 128, 128], replicated, may hold values from -0.0029296875 to 0.0029296875
- expand_first: float32 [2, 128, 256], replicated, may hold values from -0.0029296875 to 0.0029296875
- reduce_first: float32 [2, 256, 128], replicated, may hold values from -0.0029296875 to 0.0029296875
- position_first: float32 [2, 144, 128], replicated, may hold values from -0.00024414062 to 0.00024414062
- norms_first: float32 [2, 4, 128], replicated, may hold values from -0.0078125 to 0.0078125
- attend_second: float32 [2, 128, 384], replicated, may hold values from 3.332978e-09 to 1.3331912e-08
- output_second: float32 [2, 128, 128], replicated, may hold values from 3.332978e-09 to 1.3331912e-08
- expand_second: float32 [2, 128, 256], replicated, may hold values from 3.332978e-09 to 1.3331912e-08
- reduce_second: float32 [2, 256, 128], replicated, may hold values from 3.332978e-09 to 1.3331912e-08
- position_second: float32 [2, 144, 128], replicated, may hold values from 2.314568e-11 to 9.258272e-11
- norms_second: float32 [2, 4, 128], replicated, may hold values from 2.6663823e-08 to 1.0665529e-07
Outputs:
- block_output: bfloat16 [4, 96, 72, 128], P('grid', 'strip')
- input_grad: float32 [4, 96, 72, 128], P('grid', 'strip')
- attend_updated: float32 [2, 128, 384], replicated
- output_updated: float32 [2, 128, 128], replicated
- expand_updated: float32 [2, 128, 256], replicated
- reduce_updated: float32 [2, 256, 128], replicated
- position_updated: float32 [2, 144, 128], replicated
- norms_updated: float32 [2, 4, 128], replicated
- attend_moment: float32 [2, 128, 384], replicated
- output_moment: float32 [2, 128, 128], replicated
- expand_moment: float32 [2, 128, 256], replicated
- reduce_moment: float32 [2, 256, 128], replicated
- position_moment: float32 [2, 144, 128], replicated
- norms_moment: float32 [2, 4, 128], replicated
- attend_squares: float32 [2, 128, 384], replicated
- output_squares: float32 [2, 128, 128], replicated
- expand_squares: float32 [2, 128, 256], replicated
- reduce_squares: float32 [2, 256, 128], replicated
- position_squares: float32 [2, 144, 128], replicated
- norms_squares: float32 [2, 4, 128], replicated
- clip_norm: float32 [], replicated
- tensor_norms: float32 [2, 9, 2], replicated
The draws below stay inside these ranges and needn't reach their ends.
Inputs may be any that keep to these rules, and one draw needn't show every extreme that they name: `cell_frame`: 0 marks an empty cell; the frames 1 to 3 are bands of whole columns over all 96 rows of a grid. `norm_params`: rows 0 and 2 of each layer are gains near one, rows 1 and 3 biases near zero.
All inputs are finite; a program needn't handle non-finite values.
Results may differ from the reference program's by a relative error of at most 0.02.
The reference program's roundings to bfloat16 on the way count: a program that leaves them out, or rounds other values in their place, can miss the bound.
Values may be sent and summed in bfloat16 or wider, within the bound.
A program may use at most 128 MiB of HBM per device.

```python
import math
from functools import reduce
import jax
import jax.numpy as jnp
from jax import lax

D = 128
HEADS = 8
HEAD = 16
FF = 256
WIN = 12
SC = 72
STEP = 10
NGRID = 4
NR = 96
PARAMS = 300032


def draw_cell_frame(key, part):
    key = jax.random.fold_in(key, 11)
    first_key, second_key, third_key = jax.random.split(key, 3)
    cut_low = jax.random.randint(first_key, (NGRID, 1, 1), 1, SC // 2)
    cut_high = jax.random.randint(second_key, (NGRID, 1, 1), SC // 2, SC)
    column = jnp.arange(SC, dtype=jnp.int32)[None, None, :]
    frame = 1 + (column >= cut_low).astype(jnp.int32) + (column >= cut_high).astype(jnp.int32)
    row = jnp.arange(NR, dtype=jnp.int32)[None, :, None]
    share = 30 + 60 * row // NR
    dice = jax.random.randint(third_key, (NGRID, NR, SC), 0, 100)
    return jnp.where(dice < share, frame, 0).astype(jnp.int32)


def draw_cotangent(key, part):
    key = jax.random.fold_in(key, 23)
    row = jnp.arange(NR, dtype=jnp.float32)[None, :, None, None] / NR
    noise = jnp.clip(jax.random.normal(key, (NGRID, NR, SC, D), jnp.float32), -4.0, 4.0)
    return (noise * (1.0 + 2.0 * row)).astype(jnp.bfloat16)


def draw_norm_params(key, part):
    key = jax.random.fold_in(key, 37)
    gains = (jnp.arange(4) % 2 == 0)[None, :, None]
    noise = jnp.clip(jax.random.normal(key, (2, 4, D), jnp.float32), -2.5, 2.5)
    return jnp.where(gains, 1.0 + 0.3 * noise, 0.3 * noise)


def levels(stream_key, shape, cuts, smallest, largest):
    def one(dim, shards_of):
        draws = jax.random.uniform(jax.random.fold_in(jax.random.fold_in(stream_key, 6), dim), (shards_of,), jnp.float32, smallest / len(cuts), largest / len(cuts))
        return jnp.repeat(jnp.exp(draws), shape[dim] // shards_of).reshape((-1,) + (1,) * (len(shape) - dim - 1))

    factor_of = one(*cuts[0])
    for cut in cuts[1:]:
        factor_of = factor_of * one(*cut)
    return factor_of


def centred(rng, dims, scale, reach, cuts=(), held_as=jnp.bfloat16):
    loudness = levels(rng, dims, cuts, -0.22, 0.18) if cuts else 1.0
    drawn = jax.random.normal(rng, dims, jnp.float32) * scale * loudness
    return jnp.minimum(jnp.maximum(drawn, -reach), reach).astype(held_as)


def setup_inputs(seed: int = 0) -> dict:
    splits = jax.random.split(jax.random.key(seed), 22)
    features = centred(splits[0], (NGRID, NR, SC, D), 1.0, 6.0, ((0, 4), (1, 8)))
    cell_frame = draw_cell_frame(jax.random.fold_in(splits[21], 71), 0)
    cotangent = draw_cotangent(jax.random.fold_in(splits[21], 71), 0)
    attend_weight = centred(splits[3], (2, D, 3 * D), D ** -0.5, 0.5, (), jnp.float32)
    output_weight = centred(splits[4], (2, D, D), (D // 8) ** -0.5, 1.5, (), jnp.float32)
    expand_weight = centred(splits[5], (2, D, FF), D ** -0.5, 0.5, (), jnp.float32)
    reduce_weight = centred(splits[6], (2, FF, D), FF ** -0.5, 0.375, (), jnp.float32)
    position_table = centred(splits[7], (2, WIN * WIN, D), 1.0, 4.0, (), jnp.float32)
    norm_params = draw_norm_params(jax.random.fold_in(splits[21], 71), 0)
    attend_first = centred(splits[9], (2, D, 3 * D), (0.111 / PARAMS ** 0.5), 0.0029296875, (), jnp.float32)
    output_first = centred(splits[10], (2, D, D), (0.111 / PARAMS ** 0.5), 0.0029296875, (), jnp.float32)
    expand_first = centred(splits[11], (2, D, FF), (0.111 / PARAMS ** 0.5), 0.0029296875, (), jnp.float32)
    reduce_first = centred(splits[12], (2, FF, D), (0.111 / PARAMS ** 0.5), 0.0029296875, (), jnp.float32)
    position_first = centred(splits[13], (2, WIN * WIN, D), (0.111 / (WIN * PARAMS ** 0.5)), 0.00024414062, (), jnp.float32)
    norms_first = centred(splits[14], (2, 4, D), (0.3 / PARAMS ** 0.5), 0.0078125, (), jnp.float32)
    attend_second = jnp.clip(jnp.exp(jax.random.uniform(splits[15], (2, D, 3 * D), jnp.float32, math.log(3.33297789367748e-09), math.log(1.333191157470992e-08))), 3.33297789367748e-09, 1.333191157470992e-08)
    output_second = jnp.clip(jnp.exp(jax.random.uniform(splits[16], (2, D, D), jnp.float32, math.log(3.33297789367748e-09), math.log(1.333191157470992e-08))), 3.33297789367748e-09, 1.333191157470992e-08)
    expand_second = jnp.clip(jnp.exp(jax.random.uniform(splits[17], (2, D, FF), jnp.float32, math.log(3.33297789367748e-09), math.log(1.333191157470992e-08))), 3.33297789367748e-09, 1.333191157470992e-08)
    reduce_second = jnp.clip(jnp.exp(jax.random.uniform(splits[18], (2, FF, D), jnp.float32, math.log(3.33297789367748e-09), math.log(1.333191157470992e-08))), 3.33297789367748e-09, 1.333191157470992e-08)
    position_second = jnp.clip(jnp.exp(jax.random.uniform(splits[19], (2, WIN * WIN, D), jnp.float32, math.log(2.3145679817204723e-11), math.log(9.258271926881889e-11))), 2.3145679817204723e-11, 9.258271926881889e-11)
    norms_second = jnp.clip(jnp.exp(jax.random.uniform(splits[20], (2, 4, D), jnp.float32, math.log(2.666382314941984e-08), math.log(1.0665529259767936e-07))), 2.666382314941984e-08, 1.0665529259767936e-07)
    return {"features": features, "cell_frame": cell_frame, "cotangent": cotangent, "attend_weight": attend_weight, "output_weight": output_weight, "expand_weight": expand_weight, "reduce_weight": reduce_weight, "position_table": position_table, "norm_params": norm_params, "attend_first": attend_first, "output_first": output_first, "expand_first": expand_first, "reduce_first": reduce_first, "position_first": position_first, "norms_first": norms_first, "attend_second": attend_second, "output_second": output_second, "expand_second": expand_second, "reduce_second": reduce_second, "position_second": position_second, "norms_second": norms_second}


@jax.custom_vjp
def low(v):
    return lax.optimization_barrier(v.astype(jnp.bfloat16)).astype(jnp.float32)

@jax.custom_vjp
def low_back(v):
    return v

def low_keep(v):
    return (low(v), None)

def low_pass(kept, grad):
    return (grad,)

def back_keep(v):
    return (v, None)

def back_low(kept, grad):
    return (low(grad),)
low.defvjp(low_keep, low_pass)
low_back.defvjp(back_keep, back_low)
beta_one = 0.9
beta_two = 0.999
learn_rate = 0.2
weight_decay = 0.01
epsilon = 1e-06
clip_bound = 1.0

def product(left, right):
    return jnp.dot(left, right, precision=lax.Precision.HIGHEST, preferred_element_type=jnp.float32)

def normalize(value, gain, shift):
    centered = value - lax.optimization_barrier(jnp.mean(value, axis=-1, keepdims=True))
    spread = lax.optimization_barrier(jnp.mean(centered * centered, axis=-1, keepdims=True))
    return centered * lax.rsqrt(spread + 1e-05) * gain + shift

def to_windows(field):
    grids, rows, cols = (field.shape[0], field.shape[1], field.shape[2])
    rest = field.shape[3:]
    shaped = field.reshape((grids, rows // WIN, WIN, cols // WIN, WIN) + rest)
    shaped = jnp.swapaxes(shaped, 2, 3)
    return shaped.reshape((grids * (rows // WIN), cols // WIN, WIN * WIN) + rest)

def from_windows(tiles, grids, rows, cols):
    rest = tiles.shape[3:]
    shaped = tiles.reshape((grids, rows // WIN, cols // WIN, WIN, WIN) + rest)
    shaped = jnp.swapaxes(shaped, 2, 3)
    return shaped.reshape((grids, rows, cols) + rest)

def attend(query, keys, values, codes):
    count = query.shape[0]
    shape = (count, WIN * WIN, HEADS, HEAD)
    scores = jnp.einsum('wqhd,wkhd->whqk', query.reshape(shape), keys.reshape(shape), precision=lax.Precision.HIGHEST) * HEAD ** (-0.5)
    scores = low_back(scores)
    allowed = (codes[:, :, None] == codes[:, None, :])[:, None]
    scores = jnp.where(allowed, scores, -1000000000.0)
    top = lax.optimization_barrier(jnp.max(scores, axis=-1, keepdims=True))
    weights = jnp.exp(scores - top)
    probs = weights / lax.optimization_barrier(jnp.sum(weights, axis=-1, keepdims=True))
    mixed = jnp.einsum('whqk,wkhd->wqhd', low(probs), values.reshape(shape), precision=lax.Precision.HIGHEST)
    return mixed.reshape(count, WIN * WIN, HEADS * HEAD)

def layer(field, codes, attend_w, output_w, expand_w, reduce_w, position, rows):
    grids, height, cols, width = field.shape
    tiles = to_windows(field)
    code_tiles = to_windows(codes)
    mixed_in = low(tiles + position)
    query_key = low_back(low(product(mixed_in, low(attend_w[:, :2 * width]))))
    values = low_back(low(product(tiles, low(attend_w[:, 2 * width:]))))
    block_fn = jax.checkpoint(lambda parts: attend(parts[0], parts[1], parts[2], parts[3]))
    mixed = lax.map(block_fn, (query_key[..., :width], query_key[..., width:], values, code_tiles))
    mixed = low_back(low(mixed))
    branch = low_back(product(mixed, low(output_w)))
    first = normalize(tiles + branch, rows[0], rows[1])
    hidden = low_back(product(low(first), low(expand_w)))
    branch_two = low_back(product(low(jax.nn.gelu(hidden)), low(reduce_w)))
    second = normalize(first + branch_two, rows[2], rows[3])
    second = second * (code_tiles > 0).astype(jnp.float32)[..., None]
    return from_windows(second, grids, height, cols)

def forward(field, weights, codes):
    attend_w, output_w, expand_w, reduce_w, position, rows = weights
    half = WIN // 2
    first = layer(field, codes, attend_w[0], output_w[0], expand_w[0], reduce_w[0], position[0], rows[0])
    carried = low_back(low(first))
    rolled = jnp.roll(carried, (-half, -half), axis=(1, 2))
    rolled_codes = jnp.roll(codes, (-half, -half), axis=(1, 2))
    second = layer(rolled, rolled_codes, attend_w[1], output_w[1], expand_w[1], reduce_w[1], position[1], rows[1])
    return low(jnp.roll(second, (half, half), axis=(1, 2)))

def lamb(weights, grads, firsts, seconds):
    total = reduce(lambda acc, grad: acc + jnp.sum(grad * grad), grads, jnp.float32(0.0))
    clip_norm = jnp.sqrt(total)
    factor = clip_bound / jnp.maximum(clip_norm, clip_bound)
    fix_one = 1.0 - beta_one ** STEP
    fix_two = 1.0 - beta_two ** STEP
    updated, moments, squares, weight_norms, step_norms = ([], [], [], [], [])
    for index in range(6):
        grad = grads[index] * factor
        moment = beta_one * firsts[index] + (1.0 - beta_one) * grad
        square = beta_two * seconds[index] + (1.0 - beta_two) * grad * grad
        direction = moment / fix_one / (jnp.sqrt(square / fix_two) + epsilon)
        if index < 5:
            direction = direction + weight_decay * weights[index]
            axes = (1, 2)
        else:
            axes = (2,)
        weight_norm = jnp.sqrt(lax.optimization_barrier(jnp.sum(weights[index] * weights[index], axis=axes, keepdims=True)))
        step_norm = jnp.sqrt(lax.optimization_barrier(jnp.sum(direction * direction, axis=axes, keepdims=True)))
        updated.append(weights[index] - learn_rate * weight_norm / (step_norm + epsilon) * direction)
        moments.append(moment)
        squares.append(square)
        weight_norms.append(weight_norm.reshape(2, -1))
        step_norms.append(step_norm.reshape(2, -1))
    norms = jnp.stack([jnp.concatenate(weight_norms, axis=1), jnp.concatenate(step_norms, axis=1)], axis=-1)
    return (updated, moments, squares, clip_norm, norms)

def reference(features, cell_frame, cotangent, attend_weight, output_weight, expand_weight, reduce_weight, position_table, norm_params, attend_first, output_first, expand_first, reduce_first, position_first, norms_first, attend_second, output_second, expand_second, reduce_second, position_second, norms_second):
    weights = (attend_weight, output_weight, expand_weight, reduce_weight, position_table, norm_params)
    field = features.astype(jnp.float32)
    result, pullback = jax.vjp(lambda value, params: forward(value, params, cell_frame), field, weights)
    input_grad, grads = pullback(cotangent.astype(jnp.float32))
    firsts = (attend_first, output_first, expand_first, reduce_first, position_first, norms_first)
    seconds = (attend_second, output_second, expand_second, reduce_second, position_second, norms_second)
    updated, moments, squares, clip_norm, norms = lamb(weights, grads, firsts, seconds)
    return (result.astype(jnp.bfloat16), input_grad, updated[0], updated[1], updated[2], updated[3], updated[4], updated[5], moments[0], moments[1], moments[2], moments[3], moments[4], moments[5], squares[0], squares[1], squares[2], squares[3], squares[4], squares[5], clip_norm, norms)
```

```python
import functools

import jax
import jax.numpy as jnp
import numpy as np
from jax import lax
from jax.experimental import pallas as pl
from jax.experimental.pallas import tpu as pltpu
from jax.sharding import PartitionSpec as P

bf16 = jnp.bfloat16
f32 = jnp.float32
MESH = pl.DeviceIdType.MESH

HEADS = 8
HEAD = 16
D = 128
FF = 256
WIN = 12
SLOTS = WIN * WIN
LANES = HEADS * SLOTS
STEP = 10
beta_one = 0.9
beta_two = 0.999
learn_rate = 0.2
weight_decay = 0.01
epsilon = 1e-06
clip_bound = 1.0

Q0, K0, V0, O0, E0, R0, P0, N0 = 0, 128, 256, 384, 512, 768, 1024, 1168
ROWS = 1176
TOTAL = 2432

TILES = ((0, 256), (256, 512), (512, 768), (768, 1024), (1024, 1152))


def nt(a, b):
    return lax.dot_general(a, b, (((1,), (1,)), ((), ())), preferred_element_type=f32)


def tn(a, b):
    return lax.dot_general(a, b, (((0,), (0,)), ((), ())), preferred_element_type=f32)


def nn(a, b):
    return jnp.dot(a, b, preferred_element_type=f32)


def head_blocks(block):
    lane = lax.broadcasted_iota(jnp.int32, block.shape, 1)
    parts = []
    for h in range(HEADS):
        keep = (lane >= h * HEAD) & (lane < (h + 1) * HEAD)
        parts.append(jnp.where(keep, block, jnp.zeros_like(block)))
    return jnp.concatenate(parts, axis=0)


def diagonal(full):
    return jnp.concatenate(
        [full[h * HEAD : (h + 1) * HEAD, h * SLOTS : (h + 1) * SLOTS] for h in range(HEADS)], axis=0
    )


def main_kernel(
    strips,
    windows,
    feat,
    codes_in,
    cot,
    attend_w,
    output_w,
    expand_w,
    reduce_w,
    position,
    norms,
    block_out,
    input_grad,
    grads_out,
    wa,
    wo,
    we,
    wr,
    xt,
    mi,
    qs,
    ks,
    vs,
    probs,
    att,
    first_b,
    xh1,
    rs1,
    act,
    dgelu,
    xh2,
    rs2,
    crow,
    ccol,
    ctab,
    field,
    wide,
    tmp,
    d_br2,
    d_hid,
    d_br,
    d_att,
    d_res,
    ds_s,
    d_q,
    d_k,
    d_v,
    csend,
    crecv,
    hsend,
    hrecv,
    osend,
    orecv,
    grecv,
    bsend,
    brecv,
    g,
    s1,
    r1,
    hsum,
    s2,
    r2,
    s3,
    r3,
    half_b,
    all_b,
    send_sem,
    recv_sem,
):
    T = windows * SLOTS
    cols = windows * WIN
    stride = cols + 8
    hw = WIN // 2
    hs = hw * WIN
    gi = lax.axis_index("grid")
    si = lax.axis_index("strip")
    n_grid = lax.axis_size("grid")
    core = lax.rem(si, 2)
    zi = lax.div(si, 2)
    n_z = strips // 2
    prev = lax.rem(si + strips - 1, strips)
    nxt = lax.rem(si + 1, strips)
    sib = si + 1 - 2 * core

    grid_peers = [lax.rem(gi + d, n_grid) for d in range(1, n_grid)]
    z_peers = [lax.rem(zi + d, n_z) * 2 + core for d in range(1, n_z)]
    peers = [(gi, prev), (gi, nxt), (gi, sib)]
    peers += [(p, si) for p in grid_peers] + [(gi, p) for p in z_peers]

    barrier = pltpu.get_barrier_semaphore()
    for peer in peers:
        pl.semaphore_signal(barrier, inc=1, device_id=peer, device_id_type=MESH)
    pl.semaphore_wait(barrier, len(peers))

    def remote(src, dst, index, device):
        return pltpu.make_async_remote_copy(
            src_ref=src,
            dst_ref=dst,
            send_sem=send_sem.at[index],
            recv_sem=recv_sem.at[index],
            device_id=device,
            device_id_type=MESH,
        )

    csend[...] = jnp.zeros((16, 128), f32)
    csend[0:WIN, 0:cols] = codes_in[...].astype(f32)
    codes_copy = remote(csend, crecv, 0, (gi, prev))
    codes_copy.start()
    cot_copy = remote(cot.at[pl.ds(0, hw)], grecv, 1, (gi, prev))
    cot_copy.start()

    for l in range(2):
        wa[l] = attend_w[l].astype(bf16)
        wo[l] = output_w[l].astype(bf16)
        we[l] = expand_w[l].astype(bf16)
        wr[l] = reduce_w[l].astype(bf16)

    def code_tables(l, table):
        low = table.astype(bf16)
        lane = lax.broadcasted_iota(jnp.int32, (16, LANES), 1).astype(f32)
        row = lax.broadcasted_iota(jnp.int32, (16, LANES), 0).astype(f32)
        slot = lane - SLOTS * jnp.floor((lane + 0.5) * (1.0 / SLOTS))
        slot_r = jnp.floor((slot + 0.5) * (1.0 / WIN))
        slot_c = slot - WIN * slot_r
        pick_r = (slot_r == row).astype(bf16)
        ctab[...] = tn(low, pick_r)
        pick_c = (slot_c == row).astype(f32)[0:WIN]
        for w in range(windows):
            part = ctab[w * WIN : (w + 1) * WIN, :]
            crow[l, w] = jnp.sum(part * pick_c, axis=0, keepdims=True)
        token = lax.broadcasted_iota(jnp.int32, (SLOTS, 128), 0).astype(f32)
        place = lax.broadcasted_iota(jnp.int32, (SLOTS, 128), 1).astype(f32)
        token_r = jnp.floor((token + 0.5) * (1.0 / WIN))
        token_c = token - WIN * token_r
        row_of = (token_r == place).astype(bf16)[:, 0:16]
        spread = nn(row_of, low)
        for w in range(windows):
            chosen = jnp.where(place == token_c + w * WIN, spread, 0.0)
            value = jnp.sum(chosen, axis=1, keepdims=True)
            ccol[l, w * SLOTS : (w + 1) * SLOTS] = jnp.broadcast_to(value, (SLOTS, 128))

    code_tables(0, csend[...])

    def attention_forward(l):
        def one(w, carry):
            off = pl.multiple_of(w * SLOTS, SLOTS)
            rows = pl.ds(off, SLOTS)
            q = qs[l, rows]
            k = ks[l, rows]
            v_t = vs[l, rows].T
            qb = head_blocks(q)
            cc = ccol[l, rows]
            cr = crow[l, w]
            for a, b in TILES:
                scores = nt(k, qb[a:b])
                same = jnp.concatenate([cc] * ((b - a) // 128), axis=1) == cr[:, a:b]
                scores = jnp.where(same, scores, -1000000000.0)
                top = jnp.max(scores, axis=0, keepdims=True)
                weights = jnp.exp(scores - top)
                total = jnp.sum(weights, axis=0, keepdims=True)
                p = (weights * (1.0 / total)).astype(bf16)
                probs[l, rows, a:b] = p
                tmp[:, a:b] = nn(v_t, p)
            att[l, rows] = diagonal(tmp[...]).T.astype(bf16)
            return carry

        lax.fori_loop(0, windows, one, 0)

    def layer_forward(l, finish):
        def first_part(w, carry):
            rows = pl.ds(pl.multiple_of(w * SLOTS, SLOTS), SLOTS)
            x = xt[l, rows]
            m = (x.astype(f32) + position[l]).astype(bf16)
            mi[l, rows] = m
            qk = nn(m, wa[l, :, 0 : 2 * D])
            qs[l, rows] = (qk[:, 0:D] * HEAD ** (-0.5)).astype(bf16)
            ks[l, rows] = qk[:, D : 2 * D].astype(bf16)
            vs[l, rows] = nn(x, wa[l, :, 2 * D : 3 * D]).astype(bf16)
            return carry

        lax.fori_loop(0, windows, first_part, 0)
        attention_forward(l)

        def second_part(w, carry):
            rows = pl.ds(pl.multiple_of(w * SLOTS, SLOTS), SLOTS)
            r = xt[l, rows].astype(f32) + nn(att[l, rows], wo[l])
            c = r - jnp.mean(r, axis=1, keepdims=True)
            s = lax.rsqrt(jnp.mean(c * c, axis=1, keepdims=True) + 1e-05)
            n = c * s
            xh1[l, rows] = n
            rs1[l, rows] = jnp.broadcast_to(s, (SLOTS, D))
            first = n * norms[l, 0:1] + norms[l, 1:2]
            fb = first.astype(bf16)
            first_b[l, rows] = fb
            h = nn(fb, we[l])
            h2 = h * h
            t = jnp.tanh(0.7978845608028654 * h * (1.0 + 0.044715 * h2))
            act_b = (0.5 * h * (1.0 + t)).astype(bf16)
            act[l, rows] = act_b
            dgelu[l, rows] = 0.5 * (1.0 + t) + 0.5 * h * (1.0 - t * t) * (
                0.7978845608028654 * (1.0 + 3.0 * 0.044715 * h2)
            )
            r = first + nn(act_b, wr[l])
            c = r - jnp.mean(r, axis=1, keepdims=True)
            s = lax.rsqrt(jnp.mean(c * c, axis=1, keepdims=True) + 1e-05)
            n = c * s
            xh2[l, rows] = n
            rs2[l, rows] = jnp.broadcast_to(s, (SLOTS, D))
            second = n * norms[l, 2:3] + norms[l, 3:4]
            second = jnp.where(ccol[l, rows] > 0.0, second, 0.0)
            wide[rows] = second.astype(bf16).astype(f32)
            return carry

        lax.fori_loop(0, windows, second_part, 0)

    def norm_back(d, gain, n, s):
        dn = d * gain
        m1 = jnp.mean(dn, axis=1, keepdims=True)
        m2 = jnp.mean(dn * n, axis=1, keepdims=True)
        return s * (dn - m1 - n * m2)

    def layer_backward(l):
        base = l * ROWS
        zero = jnp.zeros((1, D), f32)

        def dense(w, sums):
            rows = pl.ds(pl.multiple_of(w * SLOTS, SLOTS), SLOTS)
            d = jnp.where(ccol[l, rows] > 0.0, wide[rows], 0.0)
            n2 = xh2[l, rows]
            bias2 = jnp.sum(d, axis=0, keepdims=True)
            gain2 = jnp.sum(d * n2, axis=0, keepdims=True)
            d2 = norm_back(d, norms[l, 2:3], n2, rs2[l, rows])
            b2 = d2.astype(bf16)
            d_br2[rows] = b2
            dh = (nt(b2, wr[l]) * dgelu[l, rows]).astype(bf16)
            d_hid[rows] = dh
            d1 = d2 + nt(dh, we[l])
            n1 = xh1[l, rows]
            bias1 = jnp.sum(d1, axis=0, keepdims=True)
            gain1 = jnp.sum(d1 * n1, axis=0, keepdims=True)
            dr = norm_back(d1, norms[l, 0:1], n1, rs1[l, rows])
            d_res[rows] = dr
            b1 = dr.astype(bf16)
            d_br[rows] = b1
            d_att[rows] = nt(b1, wo[l]).astype(bf16)
            return tuple(a + b for a, b in zip(sums, (gain1, bias1, gain2, bias2)))

        sums = lax.fori_loop(0, windows, dense, (zero,) * 4)
        g[base + N0 : base + N0 + 8] = jnp.concatenate(list(sums) + [jnp.zeros((4, D), f32)], axis=0)
        g[base + R0 : base + R0 + FF] = tn(act[l], d_br2[...])
        d_expand = tn(first_b[l], d_hid[...])
        g[base + E0 : base + E0 + D] = d_expand[:, 0:D]
        g[base + E0 + D : base + E0 + 2 * D] = d_expand[:, D : 2 * D]
        g[base + O0 : base + O0 + D] = tn(att[l], d_br[...])

        def one(w, carry):
            rows = pl.ds(pl.multiple_of(w * SLOTS, SLOTS), SLOTS)
            v = vs[l, rows]
            k_t = ks[l, rows].T
            qb = head_blocks(qs[l, rows])
            db = head_blocks(d_att[rows])
            for a, b in TILES:
                dp = nt(v, db[a:b])
                p = probs[l, rows, a:b].astype(f32)
                ds = p * (dp - jnp.sum(dp * p, axis=0, keepdims=True))
                ds = ds.astype(bf16)
                ds_s[:, a:b] = ds
                tmp[:, a:b] = nn(k_t, ds)
            d_v[rows] = nn(probs[l, rows], db).astype(bf16)
            d_k[rows] = nn(ds_s[...], qb).astype(bf16)
            d_q[rows] = (diagonal(tmp[...]).T * HEAD ** (-0.5)).astype(bf16)
            return carry

        lax.fori_loop(0, windows, one, 0)
        g[base + Q0 : base + Q0 + D] = tn(mi[l], d_q[...])
        g[base + K0 : base + K0 + D] = tn(mi[l], d_k[...])
        g[base + V0 : base + V0 + D] = tn(xt[l], d_v[...])

        def last(w, d_pos):
            rows = pl.ds(pl.multiple_of(w * SLOTS, SLOTS), SLOTS)
            dm = nt(d_q[rows], wa[l, :, 0:D]) + nt(d_k[rows], wa[l, :, D : 2 * D])
            wide[rows] = d_res[rows] + dm + nt(d_v[rows], wa[l, :, 2 * D : 3 * D])
            return d_pos + dm

        d_pos = lax.fori_loop(0, windows, last, jnp.zeros((SLOTS, D), f32))
        g[base + P0 : base + P0 + SLOTS] = d_pos

    for r in range(WIN):
        field[r * stride : r * stride + cols] = feat[r].astype(f32)
    for w in range(windows):
        for r in range(WIN):
            a = w * SLOTS + r * WIN
            wide[a : a + WIN] = field[r * stride + w * WIN : r * stride + (w + 1) * WIN]
    xt[0] = wide[...].astype(bf16)
    layer_forward(0, None)

    for w in range(windows):
        hsend[w * hs : (w + 1) * hs] = wide[w * SLOTS : w * SLOTS + hs].astype(bf16)
    halo_copy = remote(hsend, hrecv, 2, (gi, prev))
    halo_copy.start()
    codes_copy.wait()
    own = csend[...]
    other = crecv[...]
    table = jnp.concatenate([own[hw:WIN], other[0:hw], jnp.zeros((4, 128), f32)], axis=0)
    table = jnp.concatenate(
        [table[:, hw:cols], table[:, 0:hw], jnp.zeros((16, 128 - cols), f32)], axis=1
    )
    code_tables(1, table)

    def to_shifted():
        for w in range(windows):
            for r in range(WIN):
                a = w * SLOTS + r * WIN
                b = r * stride + w * WIN + hw
                wide[a : a + WIN] = field[b : b + WIN]

    for w in range(windows):
        for r in range(hw):
            a = w * SLOTS + (r + hw) * WIN
            field[r * stride + w * WIN : r * stride + (w + 1) * WIN] = wide[a : a + WIN]
    halo_copy.wait()
    wide[0 : windows * hs] = hrecv[...].astype(f32)
    for w in range(windows):
        for r in range(hw):
            a = w * hs + r * WIN
            b = (r + hw) * stride
            field[b + w * WIN : b + (w + 1) * WIN] = wide[a : a + WIN]
    for r in range(WIN):
        field[r * stride + cols : r * stride + cols + hw] = field[r * stride : r * stride + hw]
    to_shifted()
    xt[1] = wide[...].astype(bf16)
    layer_forward(1, None)

    for w in range(windows):
        osend[w * hs : (w + 1) * hs] = wide[w * SLOTS + hs : (w + 1) * SLOTS].astype(bf16)
    out_copy = remote(osend, orecv, 3, (gi, nxt))
    out_copy.start()

    def from_shifted(source, source_rows, first_row):
        for w in range(windows):
            for r in range(hw):
                a = w * source_rows + r * WIN
                b = (r + first_row) * stride + w * WIN + hw
                field[b : b + WIN] = source[a : a + WIN]
        for r in range(first_row, first_row + hw):
            field[r * stride : r * stride + hw] = field[r * stride + cols : r * stride + cols + hw]

    from_shifted(wide, SLOTS, hw)
    for r in range(hw, WIN):
        block_out[r] = field[r * stride : r * stride + cols].astype(bf16)

    cot_copy.wait()
    for r in range(hw):
        field[r * stride : r * stride + cols] = cot[r + hw].astype(f32)
        field[(r + hw) * stride : (r + hw) * stride + cols] = grecv[r].astype(f32)
    for r in range(WIN):
        field[r * stride + cols : r * stride + cols + hw] = field[r * stride : r * stride + hw]
    to_shifted()
    layer_backward(1)

    for w in range(windows):
        bsend[w * hs : (w + 1) * hs] = wide[w * SLOTS + hs : (w + 1) * SLOTS].astype(bf16)
    back_copy = remote(bsend, brecv, 4, (gi, nxt))
    back_copy.start()
    from_shifted(wide, SLOTS, hw)
    back_copy.wait()
    wide[0 : windows * hs] = brecv[...].astype(f32)
    from_shifted(wide, hs, 0)
    for w in range(windows):
        for r in range(WIN):
            a = w * SLOTS + r * WIN
            wide[a : a + WIN] = field[r * stride + w * WIN : r * stride + (w + 1) * WIN]
    wide[...] = wide[...].astype(bf16).astype(f32)
    layer_backward(0)
    for w in range(windows):
        for r in range(WIN):
            a = w * SLOTS + r * WIN
            field[r * stride + w * WIN : r * stride + (w + 1) * WIN] = wide[a : a + WIN]
    for r in range(WIN):
        input_grad[r] = field[r * stride : r * stride + cols]
    out_copy.wait()
    wide[0 : windows * hs] = orecv[...].astype(f32)
    from_shifted(wide, hs, 0)
    for r in range(hw):
        block_out[r] = field[r * stride : r * stride + cols].astype(bf16)

    half = TOTAL // 2
    quarter = half // n_grid
    g[2 * ROWS : TOTAL] = jnp.zeros((TOTAL - 2 * ROWS, D), f32)
    s1[...] = g[pl.ds(pl.multiple_of((1 - core) * half, 16), half)].astype(bf16)
    copy = remote(s1, r1, 5, (gi, sib))
    copy.start()
    copy.wait()
    hsum[...] = g[pl.ds(pl.multiple_of(core * half, 16), half)] + r1[...].astype(f32)
    s2[...] = hsum[...].astype(bf16)
    index = 6
    copies = []
    for d, p in enumerate(grid_peers):
        part = pl.ds(pl.multiple_of(p * quarter, 16), quarter)
        copies.append(remote(s2.at[part], r2.at[d], index, (p, si)))
        copies[-1].start()
        index += 1
    for copy in copies:
        copy.wait()
    mine = pl.ds(pl.multiple_of(gi * quarter, 16), quarter)
    total = hsum[mine]
    for d in range(n_grid - 1):
        total = total + r2[d].astype(f32)
    s3[...] = total.astype(bf16)
    copies = []
    for p in z_peers:
        copies.append(remote(s3, r3.at[zi], index, (gi, p)))
        copies[-1].start()
        index += 1
    r3[zi] = s3[...]
    for copy in copies:
        copy.wait()
    total = r3[0].astype(f32)
    for d in range(1, n_z):
        total = total + r3[d].astype(f32)
    half_b[mine] = total.astype(bf16)
    copies = []
    for p in grid_peers:
        copies.append(remote(half_b.at[mine], half_b.at[mine], index, (p, si)))
        copies[-1].start()
        index += 1
    for copy in copies:
        copy.wait()
    own_half = pl.ds(pl.multiple_of(core * half, 16), half)
    copy = remote(half_b, all_b.at[own_half], index, (gi, sib))
    copy.start()
    all_b[own_half] = half_b[...]
    copy.wait()
    grads_out[...] = all_b[...].astype(f32)


def main_call(strips, windows, cols, n_grid):
    T = windows * SLOTS
    hw = WIN // 2
    half = TOTAL // 2
    quarter = half // n_grid
    n_z = strips // 2
    vm = pltpu.VMEM
    hs = windows * hw * WIN
    copies = 5 + 1 + 2 * (n_grid - 1) + (n_z - 1) + 1
    scratch = [
        vm((2, D, 3 * D), bf16),
        vm((2, D, D), bf16),
        vm((2, D, FF), bf16),
        vm((2, FF, D), bf16),
        vm((2, T, D), bf16),
        vm((2, T, D), bf16),
        vm((2, T, D), bf16),
        vm((2, T, D), bf16),
        vm((2, T, D), bf16),
        vm((2, T, LANES), bf16),
        vm((2, T, D), bf16),
        vm((2, T, D), bf16),
        vm((2, T, D), f32),
        vm((2, T, D), f32),
        vm((2, T, FF), bf16),
        vm((2, T, FF), f32),
        vm((2, T, D), f32),
        vm((2, T, D), f32),
        vm((2, windows, 1, LANES), f32),
        vm((2, T, D), f32),
        vm((128, LANES), f32),
        vm((WIN * (cols + 8), D), f32),
        vm((T, D), f32),
        vm((D, LANES), f32),
        vm((T, D), bf16),
        vm((T, FF), bf16),
        vm((T, D), bf16),
        vm((T, D), bf16),
        vm((T, D), f32),
        vm((SLOTS, LANES), bf16),
        vm((T, D), bf16),
        vm((T, D), bf16),
        vm((T, D), bf16),
        vm((16, 128), f32),
        vm((16, 128), f32),
        vm((hs, D), bf16),
        vm((hs, D), bf16),
        vm((hs, D), bf16),
        vm((hs, D), bf16),
        vm((hw, cols, D), bf16),
        vm((hs, D), bf16),
        vm((hs, D), bf16),
        vm((TOTAL, D), f32),
        vm((half, D), bf16),
        vm((half, D), bf16),
        vm((half, D), f32),
        vm((half, D), bf16),
        vm((n_grid - 1, quarter, D), bf16),
        vm((quarter, D), bf16),
        vm((n_z, quarter, D), bf16),
        vm((half, D), bf16),
        vm((TOTAL, D), bf16),
        pltpu.SemaphoreType.DMA((copies,)),
        pltpu.SemaphoreType.DMA((copies,)),
    ]
    whole = pl.BlockSpec(memory_space=pltpu.VMEM)
    return pl.pallas_call(
        functools.partial(main_kernel, strips, windows),
        out_shape=(
            jax.ShapeDtypeStruct((WIN, cols, D), bf16),
            jax.ShapeDtypeStruct((WIN, cols, D), f32),
            jax.ShapeDtypeStruct((TOTAL, D), f32),
        ),
        in_specs=[whole] * 9,
        out_specs=(whole,) * 3,
        scratch_shapes=scratch,
        compiler_params=pltpu.CompilerParams(
            collective_id=0, has_side_effects=True, vmem_limit_bytes=56 * 1024 * 1024
        ),
    )


def lamb_kernel(*refs):
    grads, block_in, input_in = refs[0:3]
    weights = refs[3:9]
    firsts = refs[9:15]
    seconds = refs[15:21]
    block_out, input_out = refs[21:23]
    updated = refs[23:29]
    moments = refs[29:35]
    squares = refs[35:41]
    clip_out, norms_out = refs[41:43]
    sems = refs[43]
    moves = [
        pltpu.make_async_copy(block_in, block_out, sems.at[0]),
        pltpu.make_async_copy(input_in, input_out, sems.at[1]),
    ]
    for move in moves:
        move.start()
    every = grads[...]
    clip_norm = jnp.sqrt(jnp.sum(every * every, keepdims=True))
    clip_out[...] = clip_norm
    factor = clip_bound / jnp.maximum(clip_norm, clip_bound)
    fix_one = 1.0 / (1.0 - beta_one**STEP)
    fix_two = 1.0 / (1.0 - beta_two**STEP)

    def step(index, where, grad, decay):
        grad = grad * factor
        old = weights[index][where]
        moment = beta_one * firsts[index][where] + (1.0 - beta_one) * grad
        square = beta_two * seconds[index][where] + (1.0 - beta_two) * grad * grad
        moments[index][where] = moment
        squares[index][where] = square
        direction = moment * fix_one / (jnp.sqrt(square * fix_two) + epsilon)
        if decay:
            direction = direction + weight_decay * old
        return old, direction

    for l in range(2):
        base = l * ROWS
        found = []
        for index, first_row, blocks, height in (
            (0, Q0, 3, D),
            (1, O0, 1, D),
            (2, E0, 2, D),
            (3, R0, 1, FF),
            (4, P0, 1, SLOTS),
        ):
            parts = []
            for b in range(blocks):
                where = (l, slice(None), slice(b * D, (b + 1) * D))
                start = base + first_row + b * height
                parts.append((where,) + step(index, where, grads[start : start + height], True))
            weight_norm = jnp.sqrt(sum(jnp.sum(old * old, keepdims=True) for _, old, _ in parts))
            step_norm = jnp.sqrt(sum(jnp.sum(d * d, keepdims=True) for _, _, d in parts))
            scale = learn_rate * weight_norm / (step_norm + epsilon)
            for where, old, direction in parts:
                updated[index][where] = old - scale * direction
            found.append((weight_norm, step_norm))
        old, direction = step(5, (l,), grads[base + N0 : base + N0 + 4], False)
        weight_norm = jnp.sqrt(jnp.sum(old * old, axis=1, keepdims=True))
        step_norm = jnp.sqrt(jnp.sum(direction * direction, axis=1, keepdims=True))
        updated[5][l] = old - learn_rate * weight_norm / (step_norm + epsilon) * direction
        for r in range(4):
            found.append((weight_norm[r : r + 1], step_norm[r : r + 1]))
        row = lax.broadcasted_iota(jnp.int32, (9, 2), 0)
        lane = lax.broadcasted_iota(jnp.int32, (9, 2), 1)
        table = jnp.zeros((9, 2), f32)
        for t, pair in enumerate(found):
            for j in range(2):
                value = jnp.broadcast_to(pair[j], (9, 2))
                table = jnp.where((row == t) & (lane == j), value, table)
        norms_out[l] = table
    for move in moves:
        move.wait()


def lamb_call(grads, block_output, input_grad, weights, firsts, seconds):
    whole = pl.BlockSpec(memory_space=pltpu.VMEM)
    far = pl.BlockSpec(memory_space=pl.ANY)
    like = lambda a: jax.ShapeDtypeStruct(a.shape, a.dtype)
    out = [like(block_output), like(input_grad)]
    out += [like(a) for a in weights] * 3
    out += [jax.ShapeDtypeStruct((1, 1), f32), jax.ShapeDtypeStruct((2, 9, 2), f32)]
    return pl.pallas_call(
        lamb_kernel,
        out_shape=out,
        in_specs=[whole, far, far] + [whole] * 18,
        out_specs=[far, far] + [whole] * 20,
        scratch_shapes=[pltpu.SemaphoreType.DMA((2,))],
        compiler_params=pltpu.CompilerParams(vmem_limit_bytes=48 * 1024 * 1024),
    )(grads, block_output, input_grad, *weights, *firsts, *seconds)


def body(mesh, features, cell_frame, cotangent, *rest):
    weights, firsts, seconds = rest[0:6], rest[6:12], rest[12:18]
    cols = features.shape[2]
    call = main_call(mesh.shape["strip"], cols // WIN, cols, mesh.shape["grid"])
    block_output, input_grad, grads = call(features[0], cell_frame[0], cotangent[0], *weights)
    out = lamb_call(grads, block_output, input_grad, weights, firsts, seconds)
    return (out[0][None], out[1][None], *out[2:20], out[20].reshape(()), out[21])


def solution(mesh):
    cells = P("grid", "strip", None, None)
    return jax.shard_map(
        functools.partial(body, mesh),
        mesh=mesh,
        in_specs=(cells, P("grid", "strip", None), cells) + (P(),) * 18,
        out_specs=(cells, cells) + (P(),) * 20,
        check_vma=False,
    )
```

```python
import functools

import jax
import jax.numpy as jnp
import numpy as np
from jax import lax
from jax.experimental import pallas as pl
from jax.experimental.pallas import tpu as pltpu
from jax.sharding import PartitionSpec as P

bf16 = jnp.bfloat16
f32 = jnp.float32
MESH = pl.DeviceIdType.MESH

HEADS = 8
HEAD = 16
D = 128
FF = 256
WIN = 12
SLOTS = WIN * WIN
LANES = HEADS * SLOTS
STEP = 10
beta_one = 0.9
beta_two = 0.999
learn_rate = 0.2
weight_decay = 0.01
epsilon = 1e-06
clip_bound = 1.0

L1 = dict(q=0, k=128, v=256, o=384, e=512, r=768, p=1024, n=1168)
L0_FF = dict(e=0, r=256)
L0_REST = dict(q=0, k=128, v=256, o=384, p=512, n=656)
SET_ROWS = (1176, 512, 664)

TILES = tuple((a, a + 128) for a in range(0, LANES, 128))


def nt(a, b):
    return lax.dot_general(a, b, (((1,), (1,)), ((), ())), preferred_element_type=f32)


def tn(a, b):
    return lax.dot_general(a, b, (((0,), (0,)), ((), ())), preferred_element_type=f32)


def nn(a, b):
    return jnp.dot(a, b, preferred_element_type=f32)


def head_blocks(block):
    lane = lax.broadcasted_iota(jnp.int32, block.shape, 1)
    parts = []
    for h in range(HEADS):
        keep = (lane >= h * HEAD) & (lane < (h + 1) * HEAD)
        parts.append(jnp.where(keep, block, jnp.zeros_like(block)))
    return jnp.concatenate(parts, axis=0)


def merged(full):
    lane = lax.broadcasted_iota(jnp.int32, (SLOTS, D), 1)
    block = full[0:SLOTS]
    for h in range(1, HEADS):
        block = jnp.where(lane >= h * HEAD, full[h * SLOTS : (h + 1) * SLOTS], block)
    return block


def diagonal(full):
    return jnp.concatenate(
        [full[h * HEAD : (h + 1) * HEAD, h * SLOTS : (h + 1) * SLOTS] for h in range(HEADS)], axis=0
    )


def chunk_rows(rows, parts):
    return (-(-rows // parts) + 7) // 8 * 8


def main_kernel(
    strips,
    windows,
    n_grid,
    feat_in,
    codes_in,
    cot_in,
    attend_in,
    output_in,
    expand_in,
    reduce_in,
    position_in,
    norms_in,
    block_out,
    input_grad,
    grads_one,
    grads_ff,
    grads_rest,
    feat,
    codes_v,
    cot,
    attend_w,
    output_w,
    expand_w,
    reduce_w,
    position,
    norms,
    wa,
    wo,
    we,
    wr,
    xt,
    mi,
    qs,
    ks,
    vs,
    probs,
    att,
    first_b,
    xh1,
    rs1,
    act,
    dgelu,
    xh2,
    rs2,
    crow,
    ccol,
    ctab,
    field,
    wide,
    shifted,
    scores_s,
    d_br2,
    d_hid,
    d_br,
    d_att,
    d_res,
    ds_s,
    d_q,
    d_k,
    d_v,
    csend,
    crecv,
    hsend,
    hrecv,
    osend,
    orecv,
    grecv,
    bsend,
    brecv,
    block_v,
    input_v,
    *sums_and_sems,
):
    send_sem, recv_sem, in_sem, out_sem = sums_and_sems[-4:]
    T = windows * SLOTS
    cols = windows * WIN
    stride = cols + 8
    hw = WIN // 2
    hs = hw * WIN
    gi = lax.axis_index("grid")
    si = lax.axis_index("strip")
    core = lax.rem(si, 2)
    zi = lax.div(si, 2)
    n_z = strips // 2
    chips = n_grid * n_z
    chip = gi * n_z + zi
    prev = lax.rem(si + strips - 1, strips)
    nxt = lax.rem(si + 1, strips)
    sib = si + 1 - 2 * core
    others = []
    for dz in range(n_z):
        for dg in range(n_grid):
            if (dz, dg) != (0, 0):
                g_p, z_p = lax.rem(gi + dg, n_grid), lax.rem(zi + dz, n_z)
                others.append((g_p * n_z + z_p, (g_p, z_p * 2 + core)))

    loads = {}
    for i, (src, dst) in enumerate(
        (
            (feat_in, feat),
            (codes_in, codes_v),
            (attend_in, attend_w),
            (position_in, position),
            (output_in, output_w),
            (expand_in, expand_w),
            (reduce_in, reduce_w),
            (norms_in, norms),
            (cot_in, cot),
        )
    ):
        loads[i] = pltpu.make_async_copy(src, dst, in_sem.at[i])
        loads[i].start()

    barrier = pltpu.get_barrier_semaphore()
    peers = [(gi, prev), (gi, nxt), (gi, sib)] + [device for _, device in others]
    for peer in peers:
        pl.semaphore_signal(barrier, inc=1, device_id=peer, device_id_type=MESH)
    pl.semaphore_wait(barrier, len(peers))

    def remote(src, dst, index, device):
        return pltpu.make_async_remote_copy(
            src_ref=src,
            dst_ref=dst,
            send_sem=send_sem.at[index],
            recv_sem=recv_sem.at[index],
            device_id=device,
            device_id_type=MESH,
        )

    class Total:
        def __init__(self, number):
            self.g, self.s1, self.r1, self.s2, self.r2, self.out = sums_and_sems[
                number * 6 : number * 6 + 6
            ]
            self.c = chunk_rows(SET_ROWS[number], 2 * chips)
            self.sem = 5 + number * 2 * chips

        def rows(self, half, j):
            return pl.ds(pl.multiple_of((half * chips + j) * self.c, 8), self.c)

        def to_sibling(self):
            used = SET_ROWS[number_of(self)]
            if used < 2 * chips * self.c:
                self.g[used:] = jnp.zeros((2 * chips * self.c - used, D), f32)
            for j in range(chips):
                self.s1[j] = self.g[self.rows(1 - core, j)].astype(bf16)
            self.first = remote(self.s1, self.r1, self.sem, (gi, sib))
            self.first.start()

        def to_chips(self):
            self.first.wait()
            for j in range(chips):
                both = self.g[self.rows(core, j)] + self.r1[j].astype(f32)
                self.s2[j] = both.astype(bf16)
            self.copies = []
            for i, (number, device) in enumerate(others):
                copy = remote(self.s2.at[number], self.r2.at[chip], self.sem + 1 + i, device)
                copy.start()
                self.copies.append(copy)
            self.r2[chip] = self.s2[chip]

        def spread(self):
            for copy in self.copies:
                copy.wait()
            total = self.r2[0].astype(f32)
            for j in range(1, chips):
                total = total + self.r2[j].astype(f32)
            self.out[core, chip] = total.astype(bf16)
            self.copies = []
            for i, (number, device) in enumerate(others):
                mine = self.out.at[core, chip]
                copy = remote(mine, mine, self.sem + chips + i, device)
                copy.start()
                self.copies.append(copy)

        def share(self):
            for copy in self.copies:
                copy.wait()
            mine = self.out.at[core]
            self.last = remote(mine, mine, self.sem + 2 * chips - 1, (gi, sib))
            self.last.start()

        def done(self):
            self.last.wait()

    totals = [Total(n) for n in range(3)]
    number_of = totals.index
    homes = (
        {"e": (totals[1], L0_FF), "r": (totals[1], L0_FF)},
        {},
    )

    def put(l, name, value, rows):
        total, table = homes[l].get(name, (totals[2], L0_REST) if l == 0 else (totals[0], L1))
        total.g[table[name] : table[name] + rows] = value

    cot_copy = remote(cot_in.at[pl.ds(0, hw)], grecv, 1, (gi, prev))
    cot_copy.start()
    loads[1].wait()
    csend[...] = jnp.zeros((16, 128), f32)
    for r in range(WIN):
        csend[r : r + 1, 0:cols] = codes_v[r].astype(f32)
    codes_copy = remote(csend, crecv, 0, (gi, prev))
    codes_copy.start()

    def code_tables(l, table):
        low = table.astype(bf16)
        lane = lax.broadcasted_iota(jnp.int32, (16, LANES), 1).astype(f32)
        row = lax.broadcasted_iota(jnp.int32, (16, LANES), 0).astype(f32)
        slot = lane - SLOTS * jnp.floor((lane + 0.5) * (1.0 / SLOTS))
        slot_r = jnp.floor((slot + 0.5) * (1.0 / WIN))
        slot_c = slot - WIN * slot_r
        pick_r = (slot_r == row).astype(bf16)
        ctab[...] = tn(low, pick_r)
        pick_c = (slot_c == row).astype(f32)[0:WIN]
        for w in range(windows):
            part = ctab[w * WIN : (w + 1) * WIN, :]
            crow[l, w] = jnp.sum(part * pick_c, axis=0, keepdims=True)
        token = lax.broadcasted_iota(jnp.int32, (SLOTS, 128), 0).astype(f32)
        place = lax.broadcasted_iota(jnp.int32, (SLOTS, 128), 1).astype(f32)
        token_r = jnp.floor((token + 0.5) * (1.0 / WIN))
        token_c = token - WIN * token_r
        row_of = (token_r == place).astype(bf16)[:, 0:16]
        spread = nn(row_of, low)
        for w in range(windows):
            chosen = jnp.where(place == token_c + w * WIN, spread, 0.0)
            value = jnp.sum(chosen, axis=1, keepdims=True)
            ccol[l, w * SLOTS : (w + 1) * SLOTS] = jnp.broadcast_to(value, (SLOTS, 128))

    def window_rows(w):
        return slice(w * SLOTS, (w + 1) * SLOTS)

    def layer_forward(l):
        x = xt[l]
        m = (x.astype(f32) + jnp.concatenate([position[l]] * windows, axis=0)).astype(bf16)
        mi[l] = m
        qk = nn(m, wa[l, :, 0 : 2 * D])
        qs[l] = (qk[:, 0:D] * HEAD ** (-0.5)).astype(bf16)
        ks[l] = qk[:, D : 2 * D].astype(bf16)
        vs[l] = nn(x, wa[l, :, 2 * D : 3 * D]).astype(bf16)

        for w in range(windows):
            rows = window_rows(w)
            qb = head_blocks(qs[l, rows])
            scores_s[...] = nt(ks[l, rows], qb)
            cc = ccol[l, rows]
            cr = crow[l, w]
            for a, b in TILES:
                scores = jnp.where(cc == cr[:, a:b], scores_s[:, a:b], -1000000000.0)
                top = jnp.max(scores, axis=0, keepdims=True)
                weights = jnp.exp(scores - top)
                total = jnp.sum(weights, axis=0, keepdims=True)
                probs[l, rows, a:b] = (weights * (1.0 / total)).astype(bf16)
            att[l, rows] = merged(tn(probs[l, rows], vs[l, rows])).astype(bf16)

        r = xt[l].astype(f32) + nn(att[l], wo[l])
        c = r - jnp.mean(r, axis=1, keepdims=True)
        s = lax.rsqrt(jnp.mean(c * c, axis=1, keepdims=True) + 1e-05)
        n = c * s
        xh1[l] = n
        rs1[l] = jnp.broadcast_to(s, n.shape)
        first = n * norms[l, 0:1] + norms[l, 1:2]
        fb = first.astype(bf16)
        first_b[l] = fb
        h = nn(fb, we[l])
        h2 = h * h
        t = jnp.tanh(0.7978845608028654 * h * (1.0 + 0.044715 * h2))
        act_b = (0.5 * h * (1.0 + t)).astype(bf16)
        act[l] = act_b
        dgelu[l] = 0.5 * (1.0 + t) + 0.5 * h * (1.0 - t * t) * (
            0.7978845608028654 * (1.0 + 3.0 * 0.044715 * h2)
        )
        r = first + nn(act_b, wr[l])
        c = r - jnp.mean(r, axis=1, keepdims=True)
        s = lax.rsqrt(jnp.mean(c * c, axis=1, keepdims=True) + 1e-05)
        n = c * s
        xh2[l] = n
        rs2[l] = jnp.broadcast_to(s, n.shape)
        second = n * norms[l, 2:3] + norms[l, 3:4]
        second = jnp.where(ccol[l] > 0.0, second, 0.0)
        wide[...] = second.astype(bf16).astype(f32)

    def norm_back(d, gain, n, s):
        dn = d * gain
        m1 = jnp.mean(dn, axis=1, keepdims=True)
        m2 = jnp.mean(dn * n, axis=1, keepdims=True)
        return s * (dn - m1 - n * m2)

    def dense_backward(l):
        d = jnp.where(ccol[l] > 0.0, wide[...], 0.0)
        n2 = xh2[l]
        bias2 = jnp.sum(d, axis=0, keepdims=True)
        gain2 = jnp.sum(d * n2, axis=0, keepdims=True)
        d2 = norm_back(d, norms[l, 2:3], n2, rs2[l])
        b2 = d2.astype(bf16)
        d_br2[...] = b2
        dh = (nt(b2, wr[l]) * dgelu[l]).astype(bf16)
        d_hid[...] = dh
        d1 = d2 + nt(dh, we[l])
        n1 = xh1[l]
        bias1 = jnp.sum(d1, axis=0, keepdims=True)
        gain1 = jnp.sum(d1 * n1, axis=0, keepdims=True)
        dr = norm_back(d1, norms[l, 0:1], n1, rs1[l])
        d_res[...] = dr
        b1 = dr.astype(bf16)
        d_br[...] = b1
        d_att[...] = nt(b1, wo[l]).astype(bf16)
        lines = [gain1, bias1, gain2, bias2, jnp.zeros((4, D), f32)]
        put(l, "n", jnp.concatenate(lines, axis=0), 8)

    def feed_forward_grads(l):
        put(l, "r", tn(act[l], d_br2[...]), FF)
        d_expand = tn(first_b[l], d_hid[...])
        put(l, "e", jnp.concatenate([d_expand[:, 0:D], d_expand[:, D : 2 * D]], axis=0), FF)

    def attention_backward(l):
        for w in range(windows):
            rows = window_rows(w)
            db = head_blocks(d_att[rows])
            qb = head_blocks(qs[l, rows])
            d_probs = nt(vs[l, rows], db)
            for a, b in TILES:
                dp = d_probs[:, a:b]
                p = probs[l, rows, a:b].astype(f32)
                ds = p * (dp - jnp.sum(dp * p, axis=0, keepdims=True))
                ds_s[rows, a:b] = ds.astype(bf16)
            d_v[rows] = nn(probs[l, rows], db).astype(bf16)
            ds = ds_s[rows]
            d_k[rows] = nn(ds, qb).astype(bf16)
            full = nn(ks[l, rows].T, ds)
            d_q[rows] = (diagonal(full).T * HEAD ** (-0.5)).astype(bf16)

    def attention_grads(l):
        put(l, "o", tn(att[l], d_br[...]), D)
        put(l, "q", tn(mi[l], d_q[...]), D)
        put(l, "k", tn(mi[l], d_k[...]), D)
        put(l, "v", tn(xt[l], d_v[...]), D)
        d_pos = jnp.zeros((SLOTS, D), f32)
        for part, columns in ((d_q, slice(0, D)), (d_k, slice(D, 2 * D))):
            total = part[0:SLOTS].astype(f32)
            for w in range(1, windows):
                total = total + part[window_rows(w)].astype(f32)
            high = total.astype(bf16)
            low = (total - high.astype(f32)).astype(bf16)
            d_pos = d_pos + nt(high, wa[l, :, columns]) + nt(low, wa[l, :, columns])
        put(l, "p", d_pos, SLOTS)

    def input_gradient(l):
        d = d_res[...] + nt(d_q[...], wa[l, :, 0:D]) + nt(d_k[...], wa[l, :, D : 2 * D])
        wide[...] = d + nt(d_v[...], wa[l, :, 2 * D : 3 * D])

    loads[0].wait()
    for r in range(WIN):
        field[r * stride : r * stride + cols] = feat[r].astype(f32)
    for w in range(windows):
        for r in range(WIN):
            a = w * SLOTS + r * WIN
            wide[a : a + WIN] = field[r * stride + w * WIN : r * stride + (w + 1) * WIN]
    xt[0] = wide[...].astype(bf16)
    code_tables(0, csend[...])
    for i in range(2, 8):
        loads[i].wait()

    def lower(l):
        wa[l] = attend_w[l].astype(bf16)
        wo[l] = output_w[l].astype(bf16)
        we[l] = expand_w[l].astype(bf16)
        wr[l] = reduce_w[l].astype(bf16)

    lower(0)
    layer_forward(0)

    for w in range(windows):
        hsend[w * hs : (w + 1) * hs] = wide[w * SLOTS : w * SLOTS + hs].astype(bf16)
    halo_copy = remote(hsend, hrecv, 2, (gi, prev))
    halo_copy.start()

    def wrap(rows):
        for r in rows:
            field[r * stride + cols : r * stride + cols + hw] = field[r * stride : r * stride + hw]

    def to_shifted(target, rows):
        wrap(rows)
        for w in range(windows):
            for r in rows:
                a = w * SLOTS + r * WIN
                b = r * stride + w * WIN + hw
                target[a : a + WIN] = field[b : b + WIN]

    loads[8].wait()
    cot_copy.wait()
    for r in range(hw):
        field[r * stride : r * stride + cols] = cot[r + hw].astype(f32)
        field[(r + hw) * stride : (r + hw) * stride + cols] = grecv[r].astype(f32)
    to_shifted(shifted, range(WIN))
    lower(1)
    codes_copy.wait()
    own = csend[...]
    other = crecv[...]
    table = jnp.concatenate([own[hw:WIN], other[0:hw], jnp.zeros((4, 128), f32)], axis=0)
    table = jnp.concatenate(
        [table[:, hw:cols], table[:, 0:hw], jnp.zeros((16, 128 - cols), f32)], axis=1
    )
    code_tables(1, table)
    for w in range(windows):
        for r in range(hw):
            a = w * SLOTS + (r + hw) * WIN
            field[r * stride + w * WIN : r * stride + (w + 1) * WIN] = wide[a : a + WIN]
    to_shifted(wide, range(hw))
    halo_copy.wait()
    d_res[0 : windows * hs] = hrecv[...].astype(f32)
    for w in range(windows):
        for r in range(hw):
            a = w * hs + r * WIN
            b = (r + hw) * stride
            field[b + w * WIN : b + (w + 1) * WIN] = d_res[a : a + WIN]
    to_shifted(wide, range(hw, WIN))
    xt[1] = wide[...].astype(bf16)
    layer_forward(1)

    for w in range(windows):
        osend[w * hs : (w + 1) * hs] = wide[w * SLOTS + hs : (w + 1) * SLOTS].astype(bf16)
    out_copy = remote(osend, orecv, 3, (gi, nxt))
    out_copy.start()

    def from_shifted(source, source_rows, first_row):
        for w in range(windows):
            for r in range(hw):
                a = w * source_rows + r * WIN
                b = (r + first_row) * stride + w * WIN + hw
                field[b : b + WIN] = source[a : a + WIN]
        for r in range(first_row, first_row + hw):
            field[r * stride : r * stride + hw] = field[r * stride + cols : r * stride + cols + hw]

    from_shifted(wide, SLOTS, hw)
    for r in range(hw, WIN):
        block_v[r] = field[r * stride : r * stride + cols].astype(bf16)

    wide[...] = shifted[...]
    dense_backward(1)
    attention_backward(1)
    input_gradient(1)

    for w in range(windows):
        bsend[w * hs : (w + 1) * hs] = wide[w * SLOTS + hs : (w + 1) * SLOTS].astype(bf16)
    back_copy = remote(bsend, brecv, 4, (gi, nxt))
    back_copy.start()
    from_shifted(wide, SLOTS, hw)
    feed_forward_grads(1)
    attention_grads(1)
    totals[0].to_sibling()
    back_copy.wait()
    wide[0 : windows * hs] = brecv[...].astype(f32)
    from_shifted(wide, hs, 0)
    for w in range(windows):
        for r in range(WIN):
            a = w * SLOTS + r * WIN
            wide[a : a + WIN] = field[r * stride + w * WIN : r * stride + (w + 1) * WIN]
    wide[...] = wide[...].astype(bf16).astype(f32)

    totals[0].to_chips()
    dense_backward(0)
    feed_forward_grads(0)
    totals[1].to_sibling()
    totals[0].spread()
    totals[1].to_chips()
    attention_backward(0)
    totals[0].share()
    totals[1].spread()
    attention_grads(0)
    totals[2].to_sibling()
    input_gradient(0)
    totals[2].to_chips()
    totals[1].share()
    for w in range(windows):
        for r in range(WIN):
            a = w * SLOTS + r * WIN
            field[r * stride + w * WIN : r * stride + (w + 1) * WIN] = wide[a : a + WIN]
    for r in range(WIN):
        input_v[r] = field[r * stride : r * stride + cols]
    out_copy.wait()
    wide[0 : windows * hs] = orecv[...].astype(f32)
    from_shifted(wide, hs, 0)
    for r in range(hw):
        block_v[r] = field[r * stride : r * stride + cols].astype(bf16)
    stores = [
        pltpu.make_async_copy(block_v, block_out, out_sem.at[0]),
        pltpu.make_async_copy(input_v, input_grad, out_sem.at[1]),
    ]
    for store in stores:
        store.start()
    totals[0].done()
    totals[1].done()
    stores.append(pltpu.make_async_copy(totals[0].out, grads_one, out_sem.at[2]))
    stores.append(pltpu.make_async_copy(totals[1].out, grads_ff, out_sem.at[3]))
    for store in stores[2:]:
        store.start()
    totals[2].spread()
    totals[2].share()
    totals[2].done()
    stores.append(pltpu.make_async_copy(totals[2].out, grads_rest, out_sem.at[4]))
    stores[4].start()
    for store in stores:
        store.wait()


def main_call(strips, windows, cols, n_grid):
    T = windows * SLOTS
    hw = WIN // 2
    chips = n_grid * strips // 2
    vm = pltpu.VMEM
    hs = windows * hw * WIN
    scratch = [
        vm((WIN, cols, D), bf16),
        vm((WIN, 1, cols), jnp.int32),
        vm((WIN, cols, D), bf16),
        vm((2, D, 3 * D), f32),
        vm((2, D, D), f32),
        vm((2, D, FF), f32),
        vm((2, FF, D), f32),
        vm((2, SLOTS, D), f32),
        vm((2, 4, D), f32),
        vm((2, D, 3 * D), bf16),
        vm((2, D, D), bf16),
        vm((2, D, FF), bf16),
        vm((2, FF, D), bf16),
        vm((2, T, D), bf16),
        vm((2, T, D), bf16),
        vm((2, T, D), bf16),
        vm((2, T, D), bf16),
        vm((2, T, D), bf16),
        vm((2, T, LANES), bf16),
        vm((2, T, D), bf16),
        vm((2, T, D), bf16),
        vm((2, T, D), f32),
        vm((2, T, D), f32),
        vm((2, T, FF), bf16),
        vm((2, T, FF), f32),
        vm((2, T, D), f32),
        vm((2, T, D), f32),
        vm((2, windows, 1, LANES), f32),
        vm((2, T, D), f32),
        vm((128, LANES), f32),
        vm((WIN * (cols + 8), D), f32),
        vm((T, D), f32),
        vm((T, D), f32),
        vm((SLOTS, LANES), f32),
        vm((T, D), bf16),
        vm((T, FF), bf16),
        vm((T, D), bf16),
        vm((T, D), bf16),
        vm((T, D), f32),
        vm((T, LANES), bf16),
        vm((T, D), bf16),
        vm((T, D), bf16),
        vm((T, D), bf16),
        vm((16, 128), f32),
        vm((16, 128), f32),
        vm((hs, D), bf16),
        vm((hs, D), bf16),
        vm((hs, D), bf16),
        vm((hs, D), bf16),
        vm((hw, cols, D), bf16),
        vm((hs, D), bf16),
        vm((hs, D), bf16),
        vm((WIN, cols, D), bf16),
        vm((WIN, cols, D), f32),
    ]
    outs = []
    for rows in SET_ROWS:
        c = chunk_rows(rows, 2 * chips)
        scratch += [
            vm((2 * chips * c, D), f32),
            vm((chips, c, D), bf16),
            vm((chips, c, D), bf16),
            vm((chips, c, D), bf16),
            vm((chips, c, D), bf16),
            vm((2, chips, c, D), bf16),
        ]
        outs.append(jax.ShapeDtypeStruct((2, chips, c, D), bf16))
    copies = 5 + 3 * 2 * chips
    scratch += [pltpu.SemaphoreType.DMA((n,)) for n in (copies, copies, 9, 5)]
    far = pl.BlockSpec(memory_space=pl.ANY)
    return pl.pallas_call(
        functools.partial(main_kernel, strips, windows, n_grid),
        out_shape=(
            jax.ShapeDtypeStruct((WIN, cols, D), bf16),
            jax.ShapeDtypeStruct((WIN, cols, D), f32),
            *outs,
        ),
        in_specs=[far] * 9,
        out_specs=(far,) * 5,
        scratch_shapes=scratch,
        compiler_params=pltpu.CompilerParams(
            collective_id=0, has_side_effects=True, vmem_limit_bytes=60 * 1024 * 1024
        ),
    )


def lamb_kernel(*refs):
    grads_far = refs[0:3]
    block_in, input_in = refs[3:5]
    states_far = refs[5:23]
    block_out, input_out = refs[23:25]
    results_far = refs[25:43]
    clip_out, norms_out = refs[43:45]
    grads_near = refs[45:48]
    states = refs[48:66]
    results = refs[66:84]
    block_near, input_near = refs[84:86]
    grad_sem, state_sem, out_sem, cell_sem = refs[86:90]
    cell_loads = [
        pltpu.make_async_copy(block_in, block_near, cell_sem.at[0]),
        pltpu.make_async_copy(input_in, input_near, cell_sem.at[1]),
    ]
    cell_stores = [
        pltpu.make_async_copy(block_near, block_out, cell_sem.at[2]),
        pltpu.make_async_copy(input_near, input_out, cell_sem.at[3]),
    ]
    grad_loads = [
        pltpu.make_async_copy(grads_far[i], grads_near[i], grad_sem.at[i]) for i in range(3)
    ]
    loads = [
        pltpu.make_async_copy(states_far[i], states[i], state_sem.at[i]) for i in range(18)
    ]
    stores = [
        pltpu.make_async_copy(results[i], results_far[i], out_sem.at[i]) for i in range(18)
    ]
    for copy in grad_loads:
        copy.start()
    for index in range(6):
        for kind in range(3):
            loads[6 * kind + index].start()
    for copy in cell_loads:
        copy.start()
    for copy in grad_loads:
        copy.wait()
    grads = [g[...].astype(f32).reshape(-1, D) for g in grads_near]
    clip_norm = jnp.sqrt(sum(jnp.sum(g * g, keepdims=True) for g in grads))
    clip_out[...] = clip_norm
    factor = clip_bound / jnp.maximum(clip_norm, clip_bound)
    fix_one = 1.0 / (1.0 - beta_one**STEP)
    fix_two = 1.0 / (1.0 - beta_two**STEP)

    def grad_rows(l, name, start, rows):
        if l == 1:
            number, table = 0, L1
        elif name in L0_FF:
            number, table = 1, L0_FF
        else:
            number, table = 2, L0_REST
        return grads[number][table[name] + start : table[name] + start + rows]

    def step(index, where, grad, decay):
        grad = grad * factor
        old = states[index][where]
        moment = beta_one * states[6 + index][where] + (1.0 - beta_one) * grad
        square = beta_two * states[12 + index][where] + (1.0 - beta_two) * grad * grad
        results[6 + index][where] = moment
        results[12 + index][where] = square
        direction = moment * fix_one / (jnp.sqrt(square * fix_two) + epsilon)
        if decay:
            direction = direction + weight_decay * old
        return old, direction

    found = {}
    for index, names, height in (
        (0, "qkv", D),
        (1, "o", D),
        (2, "ee", D),
        (3, "r", FF),
        (4, "p", SLOTS),
    ):
        for kind in range(3):
            loads[6 * kind + index].wait()
        for l in range(2):
            parts = []
            for b, name in enumerate(names):
                where = (l, slice(None), slice(b * D, (b + 1) * D))
                grad = grad_rows(l, name, b * D if name == "e" else 0, height)
                parts.append((where,) + step(index, where, grad, True))
            weight_norm = jnp.sqrt(sum(jnp.sum(old * old, keepdims=True) for _, old, _ in parts))
            step_norm = jnp.sqrt(sum(jnp.sum(d * d, keepdims=True) for _, _, d in parts))
            scale = learn_rate * weight_norm / (step_norm + epsilon)
            for where, old, direction in parts:
                results[index][where] = old - scale * direction
            found[l, index] = (weight_norm, step_norm)
        for kind in range(3):
            stores[6 * kind + index].start()
        if index < 2:
            cell_loads[index].wait()
            cell_stores[index].start()
    for kind in range(3):
        loads[6 * kind + 5].wait()
    for l in range(2):
        old, direction = step(5, (l,), grad_rows(l, "n", 0, 4), False)
        weight_norm = jnp.sqrt(jnp.sum(old * old, axis=1, keepdims=True))
        step_norm = jnp.sqrt(jnp.sum(direction * direction, axis=1, keepdims=True))
        results[5][l] = old - learn_rate * weight_norm / (step_norm + epsilon) * direction
        for r in range(4):
            found[l, 5 + r] = (weight_norm[r : r + 1], step_norm[r : r + 1])
        row = lax.broadcasted_iota(jnp.int32, (2, 9), 0)
        lane = lax.broadcasted_iota(jnp.int32, (2, 9), 1)
        table = jnp.zeros((2, 9), f32)
        for t in range(9):
            for j in range(2):
                value = jnp.broadcast_to(found[l, t][j], (2, 9))
                table = jnp.where((row == j) & (lane == t), value, table)
        norms_out[l] = table
    for kind in range(3):
        stores[6 * kind + 5].start()
    for copy in stores + cell_stores:
        copy.wait()


def lamb_call(grads, block_output, input_grad, weights, firsts, seconds):
    whole = pl.BlockSpec(memory_space=pltpu.VMEM)
    far = pl.BlockSpec(memory_space=pl.ANY)
    like = lambda a: jax.ShapeDtypeStruct(a.shape, a.dtype)
    states = [*weights, *firsts, *seconds]
    out = [like(block_output), like(input_grad)]
    out += [like(a) for a in states]
    out += [jax.ShapeDtypeStruct((1, 1), f32), jax.ShapeDtypeStruct((2, 2, 9), f32)]
    near = [
        pltpu.VMEM(a.shape, a.dtype)
        for a in (*grads, *states, *states, block_output, input_grad)
    ]
    return pl.pallas_call(
        lamb_kernel,
        out_shape=out,
        in_specs=[far] * 23,
        out_specs=[far] * 20 + [whole] * 2,
        scratch_shapes=near + [pltpu.SemaphoreType.DMA((n,)) for n in (3, 18, 18, 4)],
        compiler_params=pltpu.CompilerParams(vmem_limit_bytes=60 * 1024 * 1024),
    )(*grads, block_output, input_grad, *states)


def body(mesh, features, cell_frame, cotangent, *rest):
    weights, firsts, seconds = rest[0:6], rest[6:12], rest[12:18]
    cols = features.shape[2]
    call = main_call(mesh.shape["strip"], cols // WIN, cols, mesh.shape["grid"])
    cell_frame = cell_frame.reshape(WIN, 1, cols)
    block_output, input_grad, *grads = call(features[0], cell_frame, cotangent[0], *weights)
    out = lamb_call(grads, block_output, input_grad, weights, firsts, seconds)
    norms = jnp.swapaxes(out[21], 1, 2)
    return (out[0][None], out[1][None], *out[2:20], out[20].reshape(()), norms)


def solution(mesh):
    cells = P("grid", "strip", None, None)
    return jax.shard_map(
        functools.partial(body, mesh),
        mesh=mesh,
        in_specs=(cells, P("grid", "strip", None), cells) + (P(),) * 18,
        out_specs=(cells, cells) + (P(),) * 20,
        check_vma=False,
    )
```

```python
import functools

import jax
import jax.numpy as jnp
import numpy as np
from jax import lax
from jax.experimental import pallas as pl
from jax.experimental.pallas import tpu as pltpu
from jax.sharding import PartitionSpec as P

bf16 = jnp.bfloat16
f32 = jnp.float32
MESH = pl.DeviceIdType.MESH

HEADS = 8
HEAD = 16
D = 128
FF = 256
WIN = 12
SLOTS = WIN * WIN
LANES = HEADS * SLOTS
STEP = 10
beta_one = 0.9
beta_two = 0.999
learn_rate = 0.2
weight_decay = 0.01
epsilon = 1e-06
clip_bound = 1.0

L1 = dict(q=0, k=128, v=256, o=384, e=512, r=768, p=1024, n=1168)
L0_FF = dict(e=0, r=256)
L0_REST = dict(q=0, k=128, v=256, o=384, p=512, n=656)
SET_ROWS = (1176, 512, 664)

FORWARD_ZERO = ((0, 2), (2, 4), (4, 6))
FORWARD_ONE = ((0, 3), (3, 6))
BACKWARD_ONE = ((0, 2), (2, 4), (4, 6))
BACKWARD_ZERO = (((1, 4),), ((4, 6), (0, 1)))
COPIES = 9

TILES = tuple((a, a + 128) for a in range(0, LANES, 128))


def nt(a, b):
    return lax.dot_general(a, b, (((1,), (1,)), ((), ())), preferred_element_type=f32)


def tn(a, b):
    return lax.dot_general(a, b, (((0,), (0,)), ((), ())), preferred_element_type=f32)


def nn(a, b):
    return jnp.dot(a, b, preferred_element_type=f32)


def head_blocks(block):
    lane = lax.broadcasted_iota(jnp.int32, block.shape, 1)
    parts = []
    for h in range(HEADS):
        keep = (lane >= h * HEAD) & (lane < (h + 1) * HEAD)
        parts.append(jnp.where(keep, block, jnp.zeros_like(block)))
    return jnp.concatenate(parts, axis=0)


def merged(full):
    lane = lax.broadcasted_iota(jnp.int32, (SLOTS, D), 1)
    block = full[0:SLOTS]
    for h in range(1, HEADS):
        block = jnp.where(lane >= h * HEAD, full[h * SLOTS : (h + 1) * SLOTS], block)
    return block


def diagonal(full):
    return jnp.concatenate(
        [full[h * HEAD : (h + 1) * HEAD, h * SLOTS : (h + 1) * SLOTS] for h in range(HEADS)], axis=0
    )


def chunk_rows(rows, parts):
    return (-(-rows // parts) + 7) // 8 * 8


def main_kernel(
    strips,
    windows,
    n_grid,
    feat_in,
    codes_in,
    cot_in,
    attend_in,
    output_in,
    expand_in,
    reduce_in,
    position_in,
    norms_in,
    *refs,
):
    states_in, refs = refs[:12], refs[12:]
    outs, refs = refs[:23], refs[23:]
    run(strips, windows, n_grid, feat_in, codes_in, cot_in, attend_in, output_in, expand_in,
        reduce_in, position_in, norms_in, states_in, outs, *refs)


def run(
    strips,
    windows,
    n_grid,
    feat_in,
    codes_in,
    cot_in,
    attend_in,
    output_in,
    expand_in,
    reduce_in,
    position_in,
    norms_in,
    states_in,
    outs,
    feat,
    codes_v,
    cot,
    wa,
    wo,
    we,
    wr,
    xt,
    mi,
    qs,
    ks,
    vs,
    probs,
    att,
    first_b,
    xh1,
    rs1,
    act,
    dgelu,
    xh2,
    rs2,
    crow,
    ccol,
    ctab,
    field_a,
    field_b,
    field_c,
    field_d,
    wide_a,
    wide_b,
    wide_c,
    wide_d,
    wide_e,
    wide_f,
    wide_g,
    wide_h,
    scores_s,
    d_br2,
    d_hid,
    d_br,
    d_att,
    d_res,
    ds_s,
    d_q,
    d_k,
    d_v,
    csend,
    crecv,
    hsend,
    hrecv,
    osend,
    orecv,
    grecv,
    bsend,
    brecv,
    *sums_and_sems,
):
    send_sem, recv_sem, in_sem, out_sem = sums_and_sems[-4:]
    T = windows * SLOTS
    cols = windows * WIN
    stride = cols + 8
    hw = WIN // 2
    hs = hw * WIN
    gi = lax.axis_index("grid")
    si = lax.axis_index("strip")
    core = lax.rem(si, 2)
    zi = lax.div(si, 2)
    n_z = strips // 2
    chips = n_grid * n_z
    chip = gi * n_z + zi
    prev = lax.rem(si + strips - 1, strips)
    nxt = lax.rem(si + 1, strips)
    sib = si + 1 - 2 * core
    others = []
    for dz in sorted(range(n_z), key=lambda d: -min(d, n_z - d)):
        for dg in reversed(range(n_grid)):
            if (dz, dg) != (0, 0):
                g_p, z_p = lax.rem(gi + dg, n_grid), lax.rem(zi + dz, n_z)
                others.append((g_p * n_z + z_p, (g_p, z_p * 2 + core)))

    block_v, input_v = outs[0:2]
    attend_w, output_w, expand_w, reduce_w, position, norms = outs[5:11]
    loads = {}
    for i, (src, dst) in enumerate(
        (
            (feat_in, feat),
            (codes_in, codes_v),
            (attend_in, attend_w),
            (position_in, position),
            (output_in, output_w),
            (expand_in, expand_w),
            (reduce_in, reduce_w),
            (norms_in, norms),
            (cot_in, cot),
        )
    ):
        loads[i] = pltpu.make_async_copy(src, dst, in_sem.at[i])
        loads[i].start()

    state_loads = []
    for i, (src, dst) in enumerate(zip(states_in, outs[11:23])):
        state_loads.append(pltpu.make_async_copy(src, dst, out_sem.at[i]))

    barrier = pltpu.get_barrier_semaphore()
    peers = [(gi, prev), (gi, nxt), (gi, sib)] + [device for _, device in others]
    for peer in peers:
        pl.semaphore_signal(barrier, inc=1, device_id=peer, device_id_type=MESH)

    def remote(src, dst, index, device):
        return pltpu.make_async_remote_copy(
            src_ref=src,
            dst_ref=dst,
            send_sem=send_sem.at[index],
            recv_sem=recv_sem.at[index],
            device_id=device,
            device_id_type=MESH,
        )

    class Total:
        def __init__(self, number):
            self.g, self.s1, self.r1, self.s2, self.r2 = sums_and_sems[
                number * 5 : number * 5 + 5
            ]
            self.out = outs[2 + number]
            self.c = chunk_rows(SET_ROWS[number], 2 * chips)
            self.sem = COPIES + number * 2 * chips

        def rows(self, half, j):
            return pl.ds(pl.multiple_of((half * chips + j) * self.c, 8), self.c)

        def to_sibling(self):
            used = SET_ROWS[number_of(self)]
            if used < 2 * chips * self.c:
                self.g[used:] = jnp.zeros((2 * chips * self.c - used, D), f32)
            for j in range(chips):
                self.s1[j] = self.g[self.rows(1 - core, j)].astype(bf16)
            self.first = remote(self.s1, self.r1, self.sem, (gi, sib))
            self.first.start()

        def to_chips(self):
            self.first.wait()
            for j in range(chips):
                both = self.g[self.rows(core, j)] + self.r1[j].astype(f32)
                self.s2[j] = both.astype(bf16)
            self.copies = []
            for i, (number, device) in enumerate(others):
                copy = remote(self.s2.at[number], self.r2.at[chip], self.sem + 1 + i, device)
                copy.start()
                self.copies.append(copy)
            self.r2[chip] = self.s2[chip]

        def spread(self):
            for copy in self.copies:
                copy.wait()
            total = self.r2[0].astype(f32)
            for j in range(1, chips):
                total = total + self.r2[j].astype(f32)
            self.out[core, chip] = total.astype(bf16)
            self.copies = []
            for i, (number, device) in enumerate(others):
                mine = self.out.at[core, chip]
                copy = remote(mine, mine, self.sem + chips + i, device)
                copy.start()
                self.copies.append(copy)

        def share(self):
            for copy in self.copies:
                copy.wait()
            mine = self.out.at[core]
            self.last = remote(mine, mine, self.sem + 2 * chips - 1, (gi, sib))
            self.last.start()

        def done(self):
            self.last.wait()

    totals = [Total(n) for n in range(3)]
    number_of = totals.index
    homes = (
        {"e": (totals[1], L0_FF), "r": (totals[1], L0_FF)},
        {},
    )

    def put(l, name, value, rows):
        total, table = homes[l].get(name, (totals[2], L0_REST) if l == 0 else (totals[0], L1))
        total.g[table[name] : table[name] + rows] = value

    def code_tables(l, table):
        low = table.astype(bf16)
        lane = lax.broadcasted_iota(jnp.int32, (16, LANES), 1).astype(f32)
        row = lax.broadcasted_iota(jnp.int32, (16, LANES), 0).astype(f32)
        slot = lane - SLOTS * jnp.floor((lane + 0.5) * (1.0 / SLOTS))
        slot_r = jnp.floor((slot + 0.5) * (1.0 / WIN))
        slot_c = slot - WIN * slot_r
        pick_r = (slot_r == row).astype(bf16)
        ctab[...] = tn(low, pick_r)
        pick_c = (slot_c == row).astype(f32)[0:WIN]
        for w in range(windows):
            part = ctab[w * WIN : (w + 1) * WIN, :]
            crow[l, w] = jnp.sum(part * pick_c, axis=0, keepdims=True)
        token = lax.broadcasted_iota(jnp.int32, (SLOTS, 128), 0).astype(f32)
        place = lax.broadcasted_iota(jnp.int32, (SLOTS, 128), 1).astype(f32)
        token_r = jnp.floor((token + 0.5) * (1.0 / WIN))
        token_c = token - WIN * token_r
        row_of = (token_r == place).astype(bf16)[:, 0:16]
        spread = nn(row_of, low)
        for w in range(windows):
            chosen = jnp.where(place == token_c + w * WIN, spread, 0.0)
            value = jnp.sum(chosen, axis=1, keepdims=True)
            ccol[l, w * SLOTS : (w + 1) * SLOTS] = jnp.broadcast_to(value, (SLOTS, 128))

    def window_rows(w):
        return slice(w * SLOTS, (w + 1) * SLOTS)

    def layer_forward(l, first_window, end, out):
        rows = slice(first_window * SLOTS, end * SLOTS)
        x = xt[l, rows]
        places = jnp.concatenate([position[l]] * (end - first_window), axis=0)
        m = (x.astype(f32) + places).astype(bf16)
        mi[l, rows] = m
        qk = nn(m, wa[l, :, 0 : 2 * D])
        qs[l, rows] = (qk[:, 0:D] * HEAD ** (-0.5)).astype(bf16)
        ks[l, rows] = qk[:, D : 2 * D].astype(bf16)
        vs[l, rows] = nn(x, wa[l, :, 2 * D : 3 * D]).astype(bf16)

        for w in range(first_window, end):
            one = window_rows(w)
            qb = head_blocks(qs[l, one])
            scores_s[w % 2] = nt(ks[l, one], qb)
            cc = ccol[l, one]
            cr = crow[l, w]
            for a, b in TILES:
                scores = jnp.where(cc == cr[:, a:b], scores_s[w % 2, :, a:b], -1000000000.0)
                top = jnp.max(scores, axis=0, keepdims=True)
                weights = jnp.exp(scores - top)
                total = jnp.sum(weights, axis=0, keepdims=True)
                probs[l, one, a:b] = (weights * (1.0 / total)).astype(bf16)
            att[l, one] = merged(tn(probs[l, one], vs[l, one])).astype(bf16)

        r = xt[l, rows].astype(f32) + nn(att[l, rows], wo[l])
        c = r - jnp.mean(r, axis=1, keepdims=True)
        s = lax.rsqrt(jnp.mean(c * c, axis=1, keepdims=True) + 1e-05)
        n = c * s
        xh1[l, rows] = n
        rs1[l, rows] = jnp.broadcast_to(s, n.shape)
        first = n * norms[l, 0:1] + norms[l, 1:2]
        fb = first.astype(bf16)
        first_b[l, rows] = fb
        h = nn(fb, we[l])
        h2 = h * h
        t = jnp.tanh(0.7978845608028654 * h * (1.0 + 0.044715 * h2))
        act_b = (0.5 * h * (1.0 + t)).astype(bf16)
        act[l, rows] = act_b
        dgelu[l, rows] = 0.5 * (1.0 + t) + 0.5 * h * (1.0 - t * t) * (
            0.7978845608028654 * (1.0 + 3.0 * 0.044715 * h2)
        )
        r = first + nn(act_b, wr[l])
        c = r - jnp.mean(r, axis=1, keepdims=True)
        s = lax.rsqrt(jnp.mean(c * c, axis=1, keepdims=True) + 1e-05)
        n = c * s
        xh2[l, rows] = n
        rs2[l, rows] = jnp.broadcast_to(s, n.shape)
        second = n * norms[l, 2:3] + norms[l, 3:4]
        second = jnp.where(ccol[l, rows] > 0.0, second, 0.0)
        out[rows] = second.astype(bf16).astype(f32)

    def norm_back(d, gain, n, s):
        dn = d * gain
        m1 = jnp.mean(dn, axis=1, keepdims=True)
        m2 = jnp.mean(dn * n, axis=1, keepdims=True)
        return s * (dn - m1 - n * m2)

    def dense_backward(l, first_window, end, grad_out):
        rows = slice(first_window * SLOTS, end * SLOTS)
        d = jnp.where(ccol[l, rows] > 0.0, grad_out[rows], 0.0)
        n2 = xh2[l, rows]
        bias2 = jnp.sum(d, axis=0, keepdims=True)
        gain2 = jnp.sum(d * n2, axis=0, keepdims=True)
        d2 = norm_back(d, norms[l, 2:3], n2, rs2[l, rows])
        b2 = d2.astype(bf16)
        d_br2[rows] = b2
        dh = (nt(b2, wr[l]) * dgelu[l, rows]).astype(bf16)
        d_hid[rows] = dh
        d1 = d2 + nt(dh, we[l])
        n1 = xh1[l, rows]
        bias1 = jnp.sum(d1, axis=0, keepdims=True)
        gain1 = jnp.sum(d1 * n1, axis=0, keepdims=True)
        dr = norm_back(d1, norms[l, 0:1], n1, rs1[l, rows])
        d_res[rows] = dr
        b1 = dr.astype(bf16)
        d_br[rows] = b1
        d_att[rows] = nt(b1, wo[l]).astype(bf16)
        return [gain1, bias1, gain2, bias2]

    def norm_grads(l, parts):
        lines = [sum(lines) for lines in zip(*parts)] + [jnp.zeros((4, D), f32)]
        put(l, "n", jnp.concatenate(lines, axis=0), 8)

    def feed_forward_grads(l):
        put(l, "r", tn(act[l], d_br2[...]), FF)
        d_expand = tn(first_b[l], d_hid[...])
        put(l, "e", jnp.concatenate([d_expand[:, 0:D], d_expand[:, D : 2 * D]], axis=0), FF)

    def attention_backward(l, first_window, end):
        for w in range(first_window, end):
            rows = window_rows(w)
            db = head_blocks(d_att[rows])
            qb = head_blocks(qs[l, rows])
            d_probs = nt(vs[l, rows], db)
            for a, b in TILES:
                dp = d_probs[:, a:b]
                p = probs[l, rows, a:b].astype(f32)
                ds = p * (dp - jnp.sum(dp * p, axis=0, keepdims=True))
                ds_s[rows, a:b] = ds.astype(bf16)
            d_v[rows] = nn(probs[l, rows], db).astype(bf16)
            ds = ds_s[rows]
            d_k[rows] = nn(ds, qb).astype(bf16)
            full = nn(ks[l, rows].T, ds)
            d_q[rows] = (diagonal(full).T * HEAD ** (-0.5)).astype(bf16)

    def attention_grads(l):
        put(l, "o", tn(att[l], d_br[...]), D)
        put(l, "q", tn(mi[l], d_q[...]), D)
        put(l, "k", tn(mi[l], d_k[...]), D)
        put(l, "v", tn(xt[l], d_v[...]), D)
        d_pos = jnp.zeros((SLOTS, D), f32)
        for part, columns in ((d_q, slice(0, D)), (d_k, slice(D, 2 * D))):
            total = part[0:SLOTS].astype(f32)
            for w in range(1, windows):
                total = total + part[window_rows(w)].astype(f32)
            high = total.astype(bf16)
            low = (total - high.astype(f32)).astype(bf16)
            d_pos = d_pos + nt(high, wa[l, :, columns]) + nt(low, wa[l, :, columns])
        put(l, "p", d_pos, SLOTS)

    def input_gradient(l, first_window, end, out):
        rows = slice(first_window * SLOTS, end * SLOTS)
        d = nt(d_q[rows], wa[l, :, 0:D]) + nt(d_k[rows], wa[l, :, D : 2 * D])
        out[rows] = d_res[rows] + d + nt(d_v[rows], wa[l, :, 2 * D : 3 * D])

    def lower(l):
        wa[l] = attend_w[l].astype(bf16)
        wo[l] = output_w[l].astype(bf16)
        we[l] = expand_w[l].astype(bf16)
        wr[l] = reduce_w[l].astype(bf16)

    def to_windows(source, target, chosen):
        for w in chosen:
            for r in range(WIN):
                a = w * SLOTS + r * WIN
                target[a : a + WIN] = source[r * stride + w * WIN : r * stride + (w + 1) * WIN]

    def wrap_ends(field, rows):
        for r in rows:
            field[r * stride + cols : r * stride + cols + hw] = field[r * stride : r * stride + hw]

    def wrap_starts(field, rows):
        for r in rows:
            field[r * stride : r * stride + hw] = field[r * stride + cols : r * stride + cols + hw]

    def to_shifted(source, target, chosen, rows):
        for w in chosen:
            for r in rows:
                a = w * SLOTS + r * WIN
                b = r * stride + w * WIN + hw
                target[a : a + WIN] = source[b : b + WIN]

    def from_shifted(source, source_rows, field, first_row, chosen):
        for w in chosen:
            for r in range(hw):
                a = w * source_rows + r * WIN
                b = (r + first_row) * stride + w * WIN + hw
                field[b : b + WIN] = source[a : a + WIN]

    every = range(windows)
    top, bottom = range(hw), range(hw, WIN)

    loads[0].wait()
    for r in range(WIN):
        field_a[r * stride : r * stride + cols] = feat[r].astype(f32)
    to_windows(field_a, wide_a, every)
    xt[0] = wide_a[...].astype(bf16)
    loads[1].wait()
    csend[...] = jnp.zeros((16, 128), f32)
    for r in range(WIN):
        csend[r : r + 1, 0:cols] = codes_v[r].astype(f32)
    code_tables(0, csend[...])
    for i in range(2, 8):
        loads[i].wait()
    lower(0)
    halo_copies = []
    for i, (a, b) in enumerate(FORWARD_ZERO):
        layer_forward(0, a, b, wide_b)
        for w in range(a, b):
            hsend[w] = wide_b[w * SLOTS : w * SLOTS + hs].astype(bf16)
        if i == 0:
            pl.semaphore_wait(barrier, len(peers))
            codes_copy = remote(csend, crecv, 0, (gi, prev))
            codes_copy.start()
            cot_copy = remote(cot_in.at[pl.ds(0, hw)], grecv, 1, (gi, prev))
            cot_copy.start()
        halo_copies.append(remote(hsend.at[a:b], hrecv.at[a:b], 3 + i, (gi, prev)))
        halo_copies[-1].start()
        if i == 0:
            for load in state_loads:
                load.start()
            lower(1)

    for w in every:
        for r in top:
            a = w * SLOTS + (r + hw) * WIN
            field_b[r * stride + w * WIN : r * stride + (w + 1) * WIN] = wide_b[a : a + WIN]
    wrap_ends(field_b, top)
    to_shifted(field_b, wide_c, every, top)
    codes_copy.wait()
    own = csend[...]
    other = crecv[...]
    table = jnp.concatenate([own[hw:WIN], other[0:hw], jnp.zeros((4, 128), f32)], axis=0)
    table = jnp.concatenate(
        [table[:, hw:cols], table[:, 0:hw], jnp.zeros((16, 128 - cols), f32)], axis=1
    )
    code_tables(1, table)

    arrived = 0
    for a, b in FORWARD_ONE:
        for i, (c, e) in enumerate(FORWARD_ZERO):
            if i >= arrived and c <= b % windows + (windows if b == windows else 0):
                halo_copies[i].wait()
                arrived += 1
                for w in range(c, e):
                    wide_d[w * hs : (w + 1) * hs] = hrecv[w].astype(f32)
                    for r in top:
                        x = w * hs + r * WIN
                        y = (r + hw) * stride + w * WIN
                        field_b[y : y + WIN] = wide_d[x : x + WIN]
                if c == 0:
                    wrap_ends(field_b, bottom)
        to_shifted(field_b, wide_c, range(a, b), bottom)
        rows = slice(a * SLOTS, b * SLOTS)
        xt[1, rows] = wide_c[rows].astype(bf16)
        layer_forward(1, a, b, wide_e)

    for w in every:
        osend[w] = wide_e[w * SLOTS + hs : (w + 1) * SLOTS].astype(bf16)
    out_copy = remote(osend, orecv, 2, (gi, nxt))
    out_copy.start()

    loads[8].wait()
    cot_copy.wait()
    for r in top:
        field_c[r * stride : r * stride + cols] = cot[r + hw].astype(f32)
        field_c[(r + hw) * stride : (r + hw) * stride + cols] = grecv[r].astype(f32)
    wrap_ends(field_c, range(WIN))
    to_shifted(field_c, wide_f, every, range(WIN))
    parts = []
    back_copies = []
    for i, (a, b) in enumerate(BACKWARD_ONE):
        parts.append(dense_backward(1, a, b, wide_f))
        attention_backward(1, a, b)
        input_gradient(1, a, b, wide_g)
        for w in range(a, b):
            bsend[w] = wide_g[w * SLOTS + hs : (w + 1) * SLOTS].astype(bf16)
        back_copies.append(remote(bsend.at[a:b], brecv.at[a:b], 6 + i, (gi, nxt)))
        back_copies[-1].start()
        from_shifted(wide_g, SLOTS, field_d, hw, range(a, b))
    wrap_starts(field_d, bottom)
    norm_grads(1, parts)
    feed_forward_grads(1)
    attention_grads(1)
    totals[0].to_sibling()

    parts = []
    arrived = 0
    for i, ranges in enumerate(BACKWARD_ZERO):
        for j, (c, e) in enumerate(BACKWARD_ONE):
            if j >= arrived and (i == len(BACKWARD_ZERO) - 1 or c < ranges[0][1]):
                back_copies[j].wait()
                arrived += 1
                for w in range(c, e):
                    wide_d[w * hs : (w + 1) * hs] = brecv[w].astype(f32)
                from_shifted(wide_d, hs, field_d, 0, range(c, e))
                if e == windows:
                    wrap_starts(field_d, top)
        if i == 0:
            totals[0].to_chips()
        for a, b in ranges:
            to_windows(field_d, wide_h, range(a, b))
            rows = slice(a * SLOTS, b * SLOTS)
            wide_h[rows] = wide_h[rows].astype(bf16).astype(f32)
            parts.append(dense_backward(0, a, b, wide_h))
        if i == len(BACKWARD_ZERO) - 1:
            feed_forward_grads(0)
            totals[1].to_sibling()
        for a, b in ranges:
            attention_backward(0, a, b)
    norm_grads(0, parts)
    attention_grads(0)
    totals[2].to_sibling()
    totals[1].to_chips()
    totals[2].to_chips()
    totals[0].spread()
    input_gradient(0, 0, windows, wide_a)
    totals[1].spread()
    for w in every:
        for r in range(WIN):
            a = w * SLOTS + r * WIN
            field_a[r * stride + w * WIN : r * stride + (w + 1) * WIN] = wide_a[a : a + WIN]
    for r in range(WIN):
        input_v[r] = field_a[r * stride : r * stride + cols]
    out_copy.wait()
    for w in every:
        wide_d[w * hs : (w + 1) * hs] = orecv[w].astype(f32)
    from_shifted(wide_d, hs, field_c, 0, every)
    from_shifted(wide_e, SLOTS, field_c, hw, every)
    wrap_starts(field_c, range(WIN))
    for r in range(WIN):
        block_v[r] = field_c[r * stride : r * stride + cols].astype(bf16)
    totals[2].spread()
    totals[0].share()
    totals[1].share()
    totals[2].share()
    for load in state_loads:
        load.wait()
    for total in totals:
        total.done()


def main_call(strips, windows, cols, n_grid):
    T = windows * SLOTS
    hw = WIN // 2
    chips = n_grid * strips // 2
    vm = pltpu.VMEM
    hs = hw * WIN
    scratch = [
        vm((WIN, cols, D), bf16),
        vm((WIN, 1, cols), jnp.int32),
        vm((WIN, cols, D), bf16),
        vm((2, D, 3 * D), bf16),
        vm((2, D, D), bf16),
        vm((2, D, FF), bf16),
        vm((2, FF, D), bf16),
        vm((2, T, D), bf16),
        vm((2, T, D), bf16),
        vm((2, T, D), bf16),
        vm((2, T, D), bf16),
        vm((2, T, D), bf16),
        vm((2, T, LANES), bf16),
        vm((2, T, D), bf16),
        vm((2, T, D), bf16),
        vm((2, T, D), f32),
        vm((2, T, D), f32),
        vm((2, T, FF), bf16),
        vm((2, T, FF), f32),
        vm((2, T, D), f32),
        vm((2, T, D), f32),
        vm((2, windows, 1, LANES), f32),
        vm((2, T, D), f32),
        vm((128, LANES), f32),
        *[vm((WIN * (cols + 8), D), f32) for _ in range(4)],
        *[vm((T, D), f32) for _ in range(8)],
        vm((2, SLOTS, LANES), f32),
        vm((T, D), bf16),
        vm((T, FF), bf16),
        vm((T, D), bf16),
        vm((T, D), bf16),
        vm((T, D), f32),
        vm((T, LANES), bf16),
        vm((T, D), bf16),
        vm((T, D), bf16),
        vm((T, D), bf16),
        vm((16, 128), f32),
        vm((16, 128), f32),
        vm((windows, hs, D), bf16),
        vm((windows, hs, D), bf16),
        vm((windows, hs, D), bf16),
        vm((windows, hs, D), bf16),
        vm((hw, cols, D), bf16),
        vm((windows, hs, D), bf16),
        vm((windows, hs, D), bf16),
    ]
    outs = []
    for rows in SET_ROWS:
        c = chunk_rows(rows, 2 * chips)
        scratch += [
            vm((2 * chips * c, D), f32),
            vm((chips, c, D), bf16),
            vm((chips, c, D), bf16),
            vm((chips, c, D), bf16),
            vm((chips, c, D), bf16),
        ]
        outs.append(vm((2, chips, c, D), bf16))
    copies = COPIES + 3 * 2 * chips
    scratch += [pltpu.SemaphoreType.DMA((n,)) for n in (copies, copies, 9, 12)]
    params = [(2, D, 3 * D), (2, D, D), (2, D, FF), (2, FF, D), (2, SLOTS, D), (2, 4, D)]
    outs += [vm(shape, f32) for shape in params * 3]
    near = pl.BlockSpec(memory_space=pltpu.VMEM)
    far = pl.BlockSpec(memory_space=pl.ANY)
    return pl.pallas_call(
        functools.partial(main_kernel, strips, windows, n_grid),
        out_shape=(
            vm((WIN, cols, D), bf16),
            vm((WIN, cols, D), f32),
            *outs,
        ),
        in_specs=[far] * 21,
        out_specs=(near,) * 23,
        scratch_shapes=scratch,
        compiler_params=pltpu.CompilerParams(
            collective_id=0, has_side_effects=True, vmem_limit_bytes=40 * 1024 * 1024
        ),
    )


def lamb_kernel(*refs):
    grads_near = refs[0:3]
    block_near, input_near = refs[3:5]
    states = refs[5:23]
    block_out, input_out = refs[23:25]
    results_far = refs[25:43]
    clip_out, norms_out = refs[43:45]
    results = refs[45:63]
    out_sem, cell_sem = refs[63:65]
    cells = [
        pltpu.make_async_copy(block_near, block_out, cell_sem.at[0]),
        pltpu.make_async_copy(input_near, input_out, cell_sem.at[1]),
    ]
    for copy in cells:
        copy.start()
    stores = [
        pltpu.make_async_copy(results[i], results_far[i], out_sem.at[i]) for i in range(18)
    ]
    grads = [g[...].astype(f32).reshape(-1, D) for g in grads_near]
    clip_norm = jnp.sqrt(sum(jnp.sum(g * g, keepdims=True) for g in grads))
    clip_out[...] = clip_norm
    factor = clip_bound / jnp.maximum(clip_norm, clip_bound)
    fix_one = 1.0 / (1.0 - beta_one**STEP)
    fix_two = 1.0 / (1.0 - beta_two**STEP)

    def grad_rows(l, name, start, rows):
        if l == 1:
            number, table = 0, L1
        elif name in L0_FF:
            number, table = 1, L0_FF
        else:
            number, table = 2, L0_REST
        return grads[number][table[name] + start : table[name] + start + rows]

    def step(index, where, grad, decay):
        grad = grad * factor
        old = states[index][where]
        moment = beta_one * states[6 + index][where] + (1.0 - beta_one) * grad
        square = beta_two * states[12 + index][where] + (1.0 - beta_two) * grad * grad
        results[6 + index][where] = moment
        results[12 + index][where] = square
        direction = moment * fix_one / (jnp.sqrt(square * fix_two) + epsilon)
        if decay:
            direction = direction + weight_decay * old
        return old, direction

    found = {}
    for index, names, height in (
        (0, "qkv", D),
        (1, "o", D),
        (2, "ee", D),
        (3, "r", FF),
        (4, "p", SLOTS),
    ):
        for l in range(2):
            parts = []
            for b, name in enumerate(names):
                where = (l, slice(None), slice(b * D, (b + 1) * D))
                grad = grad_rows(l, name, b * D if name == "e" else 0, height)
                parts.append((where,) + step(index, where, grad, True))
            weight_norm = jnp.sqrt(sum(jnp.sum(old * old, keepdims=True) for _, old, _ in parts))
            step_norm = jnp.sqrt(sum(jnp.sum(d * d, keepdims=True) for _, _, d in parts))
            scale = learn_rate * weight_norm / (step_norm + epsilon)
            for where, old, direction in parts:
                results[index][where] = old - scale * direction
            found[l, index] = (weight_norm, step_norm)
        for kind in range(3):
            stores[6 * kind + index].start()
    for l in range(2):
        old, direction = step(5, (l,), grad_rows(l, "n", 0, 4), False)
        weight_norm = jnp.sqrt(jnp.sum(old * old, axis=1, keepdims=True))
        step_norm = jnp.sqrt(jnp.sum(direction * direction, axis=1, keepdims=True))
        results[5][l] = old - learn_rate * weight_norm / (step_norm + epsilon) * direction
        for r in range(4):
            found[l, 5 + r] = (weight_norm[r : r + 1], step_norm[r : r + 1])
        row = lax.broadcasted_iota(jnp.int32, (2, 9), 0)
        lane = lax.broadcasted_iota(jnp.int32, (2, 9), 1)
        table = jnp.zeros((2, 9), f32)
        for t in range(9):
            for j in range(2):
                value = jnp.broadcast_to(found[l, t][j], (2, 9))
                table = jnp.where((row == j) & (lane == t), value, table)
        norms_out[l] = table
    for kind in range(3):
        stores[6 * kind + 5].start()
    for copy in stores + cells:
        copy.wait()


def lamb_call(grads, block_output, input_grad, states):
    whole = pl.BlockSpec(memory_space=pltpu.VMEM)
    far = pl.BlockSpec(memory_space=pl.ANY)
    like = lambda a: jax.ShapeDtypeStruct(a.shape, a.dtype)
    out = [like(block_output), like(input_grad)]
    out += [like(a) for a in states]
    out += [jax.ShapeDtypeStruct((1, 1), f32), jax.ShapeDtypeStruct((2, 2, 9), f32)]
    near = [pltpu.VMEM(a.shape, a.dtype) for a in states]
    return pl.pallas_call(
        lamb_kernel,
        out_shape=out,
        in_specs=[whole] * 23,
        out_specs=[far] * 20 + [whole] * 2,
        scratch_shapes=near + [pltpu.SemaphoreType.DMA((n,)) for n in (18, 2)],
        compiler_params=pltpu.CompilerParams(vmem_limit_bytes=32 * 1024 * 1024),
    )(*grads, block_output, input_grad, *states)


def body(mesh, features, cell_frame, cotangent, *rest):
    cols = features.shape[2]
    call = main_call(mesh.shape["strip"], cols // WIN, cols, mesh.shape["grid"])
    cell_frame = cell_frame.reshape(WIN, 1, cols)
    held = [
        pltpu.with_memory_space_constraint(a, pltpu.HBM)
        for a in (features[0], cell_frame, cotangent[0], *rest)
    ]
    found = call(*held)
    out = lamb_call(found[2:5], found[0], found[1], found[5:23])
    norms = jnp.swapaxes(out[21], 1, 2)
    return (out[0][None], out[1][None], *out[2:20], out[20].reshape(()), norms)


def solution(mesh):
    cells = P("grid", "strip", None, None)
    return jax.shard_map(
        functools.partial(body, mesh),
        mesh=mesh,
        in_specs=(cells, P("grid", "strip", None), cells) + (P(),) * 18,
        out_specs=(cells, cells) + (P(),) * 20,
        check_vma=False,
    )
```

```python
import functools

import jax
import jax.numpy as jnp
import numpy as np
from jax import lax
from jax.experimental import pallas as pl
from jax.experimental.pallas import tpu as pltpu
from jax.sharding import PartitionSpec as P

bf16 = jnp.bfloat16
f32 = jnp.float32
MESH = pl.DeviceIdType.MESH

HEADS = 8
HEAD = 16
D = 128
FF = 256
WIN = 12
SLOTS = WIN * WIN
LANES = HEADS * SLOTS
STEP = 10
beta_one = 0.9
beta_two = 0.999
learn_rate = 0.2
weight_decay = 0.01
epsilon = 1e-06
clip_bound = 1.0

L1 = dict(q=0, k=128, v=256, o=384, e=512, r=768, p=1024, n=1168)
L0_FF = dict(e=0, r=256)
L0_REST = dict(q=0, k=128, v=256, o=384, p=512, n=656)
SET_ROWS = (1176, 512, 664)

FORWARD_ZERO = ((0, 6),)
FORWARD_ONE = ((0, 6),)
BACKWARD_ONE = ((0, 6),)
BACKWARD_ZERO = (((0, 6),),)
COPIES = 9

TILES = tuple((a, min(a + 256, LANES)) for a in range(0, LANES, 256))


def nt(a, b):
    return lax.dot_general(a, b, (((1,), (1,)), ((), ())), preferred_element_type=f32)


def tn(a, b):
    return lax.dot_general(a, b, (((0,), (0,)), ((), ())), preferred_element_type=f32)


def nn(a, b):
    return jnp.dot(a, b, preferred_element_type=f32)


def head_blocks(block):
    lane = lax.broadcasted_iota(jnp.int32, block.shape, 1)
    parts = []
    for h in range(HEADS):
        keep = (lane >= h * HEAD) & (lane < (h + 1) * HEAD)
        parts.append(jnp.where(keep, block, jnp.zeros_like(block)))
    return jnp.concatenate(parts, axis=0)


def diagonal(full):
    return jnp.concatenate(
        [full[h * HEAD : (h + 1) * HEAD, h * SLOTS : (h + 1) * SLOTS] for h in range(HEADS)], axis=0
    )


def chunk_rows(rows, parts):
    return (-(-rows // parts) + 7) // 8 * 8


def main_kernel(
    strips,
    windows,
    n_grid,
    feat_in,
    codes_in,
    cot_in,
    attend_in,
    output_in,
    expand_in,
    reduce_in,
    position_in,
    norms_in,
    *refs,
):
    states_in, refs = refs[:12], refs[12:]
    outs, refs = refs[:23], refs[23:]
    run(strips, windows, n_grid, feat_in, codes_in, cot_in, attend_in, output_in, expand_in,
        reduce_in, position_in, norms_in, states_in, outs, *refs)


def run(
    strips,
    windows,
    n_grid,
    feat_in,
    codes_in,
    cot_in,
    attend_in,
    output_in,
    expand_in,
    reduce_in,
    position_in,
    norms_in,
    states_in,
    outs,
    feat,
    codes_v,
    cot,
    wa,
    wo,
    we,
    wr,
    xt,
    mi,
    qs,
    ks,
    vs,
    probs,
    att,
    first_b,
    xh1,
    rs1,
    act,
    dgelu,
    xh2,
    rs2,
    crow,
    ccol,
    ctab,
    field_a,
    field_b,
    field_c,
    field_d,
    wide_a,
    wide_b,
    wide_c,
    wide_d,
    wide_e,
    wide_f,
    wide_g,
    wide_h,
    scores_s,
    d_br2,
    d_hid,
    d_br,
    d_att,
    d_res,
    ds_s,
    d_q,
    d_k,
    d_v,
    csend,
    crecv,
    hsend,
    hrecv,
    osend,
    orecv,
    grecv,
    bsend,
    brecv,
    *sums_and_sems,
):
    send_sem, recv_sem, in_sem, out_sem = sums_and_sems[-4:]
    T = windows * SLOTS
    cols = windows * WIN
    stride = cols + 8
    hw = WIN // 2
    hs = hw * WIN
    gi = lax.axis_index("grid")
    si = lax.axis_index("strip")
    core = lax.rem(si, 2)
    zi = lax.div(si, 2)
    n_z = strips // 2
    chips = n_grid * n_z
    chip = gi * n_z + zi
    prev = lax.rem(si + strips - 1, strips)
    nxt = lax.rem(si + 1, strips)
    sib = si + 1 - 2 * core
    others = []
    for dz in sorted(range(n_z), key=lambda d: -min(d, n_z - d)):
        for dg in reversed(range(n_grid)):
            if (dz, dg) != (0, 0):
                g_p, z_p = lax.rem(gi + dg, n_grid), lax.rem(zi + dz, n_z)
                others.append((g_p * n_z + z_p, (g_p, z_p * 2 + core)))

    block_v, input_v = outs[0:2]
    attend_w, output_w, expand_w, reduce_w, position, norms = outs[5:11]
    loads = {}
    for i, (src, dst) in enumerate(
        (
            (feat_in, feat),
            (codes_in, codes_v),
            (attend_in, attend_w),
            (position_in, position),
            (output_in, output_w),
            (expand_in, expand_w),
            (reduce_in, reduce_w),
            (norms_in, norms),
            (cot_in, cot),
        )
    ):
        loads[i] = pltpu.make_async_copy(src, dst, in_sem.at[i])
        loads[i].start()

    state_loads = []
    for i, (src, dst) in enumerate(zip(states_in, outs[11:23])):
        state_loads.append(pltpu.make_async_copy(src, dst, out_sem.at[i]))

    barrier = pltpu.get_barrier_semaphore()
    peers = [(gi, prev), (gi, nxt), (gi, sib)] + [device for _, device in others]
    for peer in peers:
        pl.semaphore_signal(barrier, inc=1, device_id=peer, device_id_type=MESH)

    def remote(src, dst, index, device):
        return pltpu.make_async_remote_copy(
            src_ref=src,
            dst_ref=dst,
            send_sem=send_sem.at[index],
            recv_sem=recv_sem.at[index],
            device_id=device,
            device_id_type=MESH,
        )

    class Total:
        def __init__(self, number):
            self.g, self.s1, self.r1, self.s2, self.r2 = sums_and_sems[
                number * 5 : number * 5 + 5
            ]
            self.out = outs[2 + number]
            self.c = chunk_rows(SET_ROWS[number], 2 * chips)
            self.sem = COPIES + number * 4

        def rows(self, half, j):
            return pl.ds(pl.multiple_of((half * chips + j) * self.c, 8), self.c)

        def to_sibling(self):
            used = SET_ROWS[number_of(self)]
            if used < 2 * chips * self.c:
                self.g[used:] = jnp.zeros((2 * chips * self.c - used, D), f32)
            for j in range(chips):
                self.s1[j] = self.g[self.rows(1 - core, j)].astype(bf16)
            self.first = remote(self.s1, self.r1, self.sem, (gi, sib))
            self.first.start()

        def to_chips(self):
            self.first.wait()
            for j in range(chips):
                both = self.g[self.rows(core, j)] + self.r1[j].astype(f32)
                self.s2[j] = both.astype(bf16)
            for number, device in others:
                remote(self.s2.at[number], self.r2.at[chip], self.sem + 1, device).start()
            self.r2[chip] = self.s2[chip]

        def all_arrived(self, buffer, index):
            bytes_of = buffer.at[pl.ds(0, chips - 1)]
            remote(bytes_of, bytes_of, index, (gi, sib)).wait()

        def spread(self):
            self.all_arrived(self.r2, self.sem + 1)
            total = self.r2[0].astype(f32)
            for j in range(1, chips):
                total = total + self.r2[j].astype(f32)
            self.out[core, chip] = total.astype(bf16)
            mine = self.out.at[core, chip]
            for number, device in others:
                remote(mine, mine, self.sem + 2, device).start()

        def share(self):
            self.all_arrived(self.r2, self.sem + 2)
            mine = self.out.at[core]
            self.last = remote(mine, mine, self.sem + 3, (gi, sib))
            self.last.start()

        def done(self):
            self.last.wait()

    totals = [Total(n) for n in range(3)]
    number_of = totals.index
    homes = (
        {"e": (totals[1], L0_FF), "r": (totals[1], L0_FF)},
        {},
    )

    def put(l, name, value, rows):
        total, table = homes[l].get(name, (totals[2], L0_REST) if l == 0 else (totals[0], L1))
        total.g[table[name] : table[name] + rows] = value

    def code_tables(l, table):
        low = table.astype(bf16)
        lane = lax.broadcasted_iota(jnp.int32, (16, LANES), 1).astype(f32)
        row = lax.broadcasted_iota(jnp.int32, (16, LANES), 0).astype(f32)
        slot = lane - SLOTS * jnp.floor((lane + 0.5) * (1.0 / SLOTS))
        slot_r = jnp.floor((slot + 0.5) * (1.0 / WIN))
        slot_c = slot - WIN * slot_r
        pick_r = (slot_r == row).astype(bf16)
        ctab[...] = tn(low, pick_r)
        pick_c = (slot_c == row).astype(f32)[0:WIN]
        for w in range(windows):
            part = ctab[w * WIN : (w + 1) * WIN, :]
            crow[l, w] = jnp.sum(part * pick_c, axis=0, keepdims=True)
        token = lax.broadcasted_iota(jnp.int32, (SLOTS, 128), 0).astype(f32)
        place = lax.broadcasted_iota(jnp.int32, (SLOTS, 128), 1).astype(f32)
        token_r = jnp.floor((token + 0.5) * (1.0 / WIN))
        token_c = token - WIN * token_r
        row_of = (token_r == place).astype(bf16)[:, 0:16]
        spread = nn(row_of, low)
        for w in range(windows):
            chosen = jnp.where(place == token_c + w * WIN, spread, 0.0)
            value = jnp.sum(chosen, axis=1, keepdims=True)
            ccol[l, w * SLOTS : (w + 1) * SLOTS] = jnp.broadcast_to(value, (SLOTS, 128))

    def window_rows(w):
        return slice(w * SLOTS, (w + 1) * SLOTS)

    def in_turn(chosen, before, middle, after):
        before(chosen[0])
        for i, w in enumerate(chosen):
            if i + 1 < len(chosen):
                before(chosen[i + 1])
            middle(w)
            if i > 0:
                after(chosen[i - 1])
        after(chosen[-1])

    def layer_forward(l, first_window, end, out):
        rows = slice(first_window * SLOTS, end * SLOTS)
        x = xt[l, rows]
        places = jnp.concatenate([position[l]] * (end - first_window), axis=0)
        m = (x.astype(f32) + places).astype(bf16)
        mi[l, rows] = m
        qk = nn(m, wa[l, :, 0 : 2 * D])
        qs[l, rows] = (qk[:, 0:D] * HEAD ** (-0.5)).astype(bf16)
        ks[l, rows] = qk[:, D : 2 * D].astype(bf16)
        vs[l, rows] = nn(x, wa[l, :, 2 * D : 3 * D]).astype(bf16)

        def scores_of(w):
            one = window_rows(w)
            scores_s[w] = nt(ks[l, one], head_blocks(qs[l, one]))

        def soften(w):
            one = window_rows(w)
            cc = ccol[l, one]
            cr = crow[l, w]
            for a, b in TILES:
                same = jnp.concatenate([cc] * ((b - a) // 128), axis=1) == cr[:, a:b]
                scores = jnp.where(same, scores_s[w, :, a:b], -1000000000.0)
                top = jnp.max(scores, axis=0, keepdims=True)
                weights = jnp.exp(scores - top)
                total = jnp.sum(weights, axis=0, keepdims=True)
                probs[l, one, a:b] = (weights * (1.0 / total)).astype(bf16)

        def mix(w):
            one = window_rows(w)
            att[l, one] = diagonal(nn(vs[l, one].T, probs[l, one])).T.astype(bf16)

        in_turn(range(first_window, end), scores_of, soften, mix)

        r = xt[l, rows].astype(f32) + nn(att[l, rows], wo[l])
        c = r - jnp.mean(r, axis=1, keepdims=True)
        s = lax.rsqrt(jnp.mean(c * c, axis=1, keepdims=True) + 1e-05)
        n = c * s
        xh1[l, rows] = n
        rs1[l, rows] = jnp.broadcast_to(s, n.shape)
        first = n * norms[l, 0:1] + norms[l, 1:2]
        fb = first.astype(bf16)
        first_b[l, rows] = fb
        h = nn(fb, we[l])
        h2 = h * h
        t = jnp.tanh(0.7978845608028654 * h * (1.0 + 0.044715 * h2))
        act_b = (0.5 * h * (1.0 + t)).astype(bf16)
        act[l, rows] = act_b
        dgelu[l, rows] = 0.5 * (1.0 + t) + 0.5 * h * (1.0 - t * t) * (
            0.7978845608028654 * (1.0 + 3.0 * 0.044715 * h2)
        )
        r = first + nn(act_b, wr[l])
        c = r - jnp.mean(r, axis=1, keepdims=True)
        s = lax.rsqrt(jnp.mean(c * c, axis=1, keepdims=True) + 1e-05)
        n = c * s
        xh2[l, rows] = n
        rs2[l, rows] = jnp.broadcast_to(s, n.shape)
        second = n * norms[l, 2:3] + norms[l, 3:4]
        second = jnp.where(ccol[l, rows] > 0.0, second, 0.0)
        out[rows] = second.astype(bf16).astype(f32)

    def norm_back(d, gain, n, s):
        dn = d * gain
        m1 = jnp.mean(dn, axis=1, keepdims=True)
        m2 = jnp.mean(dn * n, axis=1, keepdims=True)
        return s * (dn - m1 - n * m2)

    def dense_backward(l, first_window, end, grad_out):
        rows = slice(first_window * SLOTS, end * SLOTS)
        d = jnp.where(ccol[l, rows] > 0.0, grad_out[rows], 0.0)
        n2 = xh2[l, rows]
        bias2 = jnp.sum(d, axis=0, keepdims=True)
        gain2 = jnp.sum(d * n2, axis=0, keepdims=True)
        d2 = norm_back(d, norms[l, 2:3], n2, rs2[l, rows])
        b2 = d2.astype(bf16)
        d_br2[rows] = b2
        dh = (nt(b2, wr[l]) * dgelu[l, rows]).astype(bf16)
        d_hid[rows] = dh
        d1 = d2 + nt(dh, we[l])
        n1 = xh1[l, rows]
        bias1 = jnp.sum(d1, axis=0, keepdims=True)
        gain1 = jnp.sum(d1 * n1, axis=0, keepdims=True)
        dr = norm_back(d1, norms[l, 0:1], n1, rs1[l, rows])
        d_res[rows] = dr
        b1 = dr.astype(bf16)
        d_br[rows] = b1
        d_att[rows] = nt(b1, wo[l]).astype(bf16)
        return [gain1, bias1, gain2, bias2]

    def norm_grads(l, parts):
        lines = [sum(lines) for lines in zip(*parts)] + [jnp.zeros((4, D), f32)]
        put(l, "n", jnp.concatenate(lines, axis=0), 8)

    def feed_forward_grads(l):
        put(l, "r", tn(act[l], d_br2[...]), FF)
        d_expand = tn(first_b[l], d_hid[...])
        put(l, "e", jnp.concatenate([d_expand[:, 0:D], d_expand[:, D : 2 * D]], axis=0), FF)

    def attention_backward(l, chosen):
        def d_probs_of(w):
            rows = window_rows(w)
            db = head_blocks(d_att[rows])
            d_v[rows] = nn(probs[l, rows], db).astype(bf16)
            scores_s[w] = nt(vs[l, rows], db)

        def d_soften(w):
            rows = window_rows(w)
            for a, b in TILES:
                dp = scores_s[w, :, a:b]
                p = probs[l, rows, a:b].astype(f32)
                ds = p * (dp - jnp.sum(dp * p, axis=0, keepdims=True))
                ds_s[rows, a:b] = ds.astype(bf16)

        def d_mix(w):
            rows = window_rows(w)
            ds = ds_s[rows]
            d_k[rows] = nn(ds, head_blocks(qs[l, rows])).astype(bf16)
            full = nn(ks[l, rows].T, ds)
            d_q[rows] = (diagonal(full).T * HEAD ** (-0.5)).astype(bf16)

        in_turn(chosen, d_probs_of, d_soften, d_mix)

    def attention_grads(l):
        put(l, "o", tn(att[l], d_br[...]), D)
        put(l, "q", tn(mi[l], d_q[...]), D)
        put(l, "k", tn(mi[l], d_k[...]), D)
        put(l, "v", tn(xt[l], d_v[...]), D)
        d_pos = jnp.zeros((SLOTS, D), f32)
        for part, columns in ((d_q, slice(0, D)), (d_k, slice(D, 2 * D))):
            total = part[0:SLOTS].astype(f32)
            for w in range(1, windows):
                total = total + part[window_rows(w)].astype(f32)
            high = total.astype(bf16)
            low = (total - high.astype(f32)).astype(bf16)
            d_pos = d_pos + nt(high, wa[l, :, columns]) + nt(low, wa[l, :, columns])
        put(l, "p", d_pos, SLOTS)

    def input_gradient(l, first_window, end, out):
        rows = slice(first_window * SLOTS, end * SLOTS)
        d = nt(d_q[rows], wa[l, :, 0:D]) + nt(d_k[rows], wa[l, :, D : 2 * D])
        out[rows] = d_res[rows] + d + nt(d_v[rows], wa[l, :, 2 * D : 3 * D])

    def lower(l):
        wa[l] = attend_w[l].astype(bf16)
        wo[l] = output_w[l].astype(bf16)
        we[l] = expand_w[l].astype(bf16)
        wr[l] = reduce_w[l].astype(bf16)

    def to_windows(source, target, chosen):
        for w in chosen:
            for r in range(WIN):
                a = w * SLOTS + r * WIN
                target[a : a + WIN] = source[r * stride + w * WIN : r * stride + (w + 1) * WIN]

    def wrap_ends(field, rows):
        for r in rows:
            field[r * stride + cols : r * stride + cols + hw] = field[r * stride : r * stride + hw]

    def wrap_starts(field, rows):
        for r in rows:
            field[r * stride : r * stride + hw] = field[r * stride + cols : r * stride + cols + hw]

    def to_shifted(source, target, chosen, rows):
        for w in chosen:
            for r in rows:
                a = w * SLOTS + r * WIN
                b = r * stride + w * WIN + hw
                target[a : a + WIN] = source[b : b + WIN]

    def from_shifted(source, source_rows, field, first_row, chosen):
        for w in chosen:
            for r in range(hw):
                a = w * source_rows + r * WIN
                b = (r + first_row) * stride + w * WIN + hw
                field[b : b + WIN] = source[a : a + WIN]

    every = range(windows)
    top, bottom = range(hw), range(hw, WIN)

    loads[0].wait()
    for r in range(WIN):
        field_a[r * stride : r * stride + cols] = feat[r].astype(f32)
    to_windows(field_a, wide_a, every)
    xt[0] = wide_a[...].astype(bf16)
    loads[1].wait()
    csend[...] = jnp.zeros((16, 128), f32)
    for r in range(WIN):
        csend[r : r + 1, 0:cols] = codes_v[r].astype(f32)
    code_tables(0, csend[...])
    for i in range(2, 8):
        loads[i].wait()
    lower(0)
    halo_copies = []
    for i, (a, b) in enumerate(FORWARD_ZERO):
        layer_forward(0, a, b, wide_b)
        for w in range(a, b):
            hsend[w] = wide_b[w * SLOTS : w * SLOTS + hs].astype(bf16)
        if i == 0:
            pl.semaphore_wait(barrier, len(peers))
            codes_copy = remote(csend, crecv, 0, (gi, prev))
            codes_copy.start()
        halo_copies.append(remote(hsend.at[a:b], hrecv.at[a:b], 3 + i, (gi, prev)))
        halo_copies[-1].start()
        if i == 0:
            for load in state_loads:
                load.start()
            lower(1)

    for w in every:
        for r in top:
            a = w * SLOTS + (r + hw) * WIN
            field_b[r * stride + w * WIN : r * stride + (w + 1) * WIN] = wide_b[a : a + WIN]
    wrap_ends(field_b, top)
    to_shifted(field_b, wide_c, every, top)
    loads[8].wait()
    for r in top:
        field_c[r * stride : r * stride + cols] = cot[r + hw].astype(f32)
    wrap_ends(field_c, top)
    to_shifted(field_c, wide_f, every, top)
    codes_copy.wait()
    own = csend[...]
    other = crecv[...]
    table = jnp.concatenate([own[hw:WIN], other[0:hw], jnp.zeros((4, 128), f32)], axis=0)
    table = jnp.concatenate(
        [table[:, hw:cols], table[:, 0:hw], jnp.zeros((16, 128 - cols), f32)], axis=1
    )
    code_tables(1, table)
    arrived = 0
    for a, b in FORWARD_ONE:
        for i, (c, e) in enumerate(FORWARD_ZERO):
            if i >= arrived and c <= b % windows + (windows if b == windows else 0):
                halo_copies[i].wait()
                arrived += 1
                for w in range(c, e):
                    wide_d[w * hs : (w + 1) * hs] = hrecv[w].astype(f32)
                    for r in top:
                        x = w * hs + r * WIN
                        y = (r + hw) * stride + w * WIN
                        field_b[y : y + WIN] = wide_d[x : x + WIN]
                if c == 0:
                    wrap_ends(field_b, bottom)
        if arrived == len(halo_copies):
            cot_copy = remote(cot_in.at[pl.ds(0, hw)], grecv, 1, (gi, prev))
            cot_copy.start()
        to_shifted(field_b, wide_c, range(a, b), bottom)
        rows = slice(a * SLOTS, b * SLOTS)
        xt[1, rows] = wide_c[rows].astype(bf16)
        layer_forward(1, a, b, wide_e)

    for w in every:
        osend[w] = wide_e[w * SLOTS + hs : (w + 1) * SLOTS].astype(bf16)
    out_copy = remote(osend, orecv, 2, (gi, nxt))
    out_copy.start()

    cot_copy.wait()
    for r in top:
        field_c[(r + hw) * stride : (r + hw) * stride + cols] = grecv[r].astype(f32)
    wrap_ends(field_c, bottom)
    to_shifted(field_c, wide_f, every, bottom)
    parts = []
    back_copies = []
    for i, (a, b) in enumerate(BACKWARD_ONE):
        parts.append(dense_backward(1, a, b, wide_f))
        attention_backward(1, range(a, b))
        input_gradient(1, a, b, wide_g)
        for w in range(a, b):
            bsend[w] = wide_g[w * SLOTS + hs : (w + 1) * SLOTS].astype(bf16)
        back_copies.append(remote(bsend.at[a:b], brecv.at[a:b], 6 + i, (gi, nxt)))
        back_copies[-1].start()
        from_shifted(wide_g, SLOTS, field_d, hw, range(a, b))
    wrap_starts(field_d, bottom)
    norm_grads(1, parts)
    feed_forward_grads(1)
    attention_grads(1)
    totals[0].to_sibling()

    parts = []
    arrived = 0
    for i, ranges in enumerate(BACKWARD_ZERO):
        for j, (c, e) in enumerate(BACKWARD_ONE):
            if j >= arrived and (i == len(BACKWARD_ZERO) - 1 or c < ranges[0][1]):
                back_copies[j].wait()
                arrived += 1
                for w in range(c, e):
                    wide_d[w * hs : (w + 1) * hs] = brecv[w].astype(f32)
                from_shifted(wide_d, hs, field_d, 0, range(c, e))
                if e == windows:
                    wrap_starts(field_d, top)
        if i == 0:
            totals[0].to_chips()
        for a, b in ranges:
            to_windows(field_d, wide_h, range(a, b))
            rows = slice(a * SLOTS, b * SLOTS)
            wide_h[rows] = wide_h[rows].astype(bf16).astype(f32)
            parts.append(dense_backward(0, a, b, wide_h))
        if i == len(BACKWARD_ZERO) - 1:
            feed_forward_grads(0)
            totals[1].to_sibling()
        attention_backward(0, [w for a, b in ranges for w in range(a, b)])
    norm_grads(0, parts)
    attention_grads(0)
    totals[2].to_sibling()
    totals[0].spread()
    totals[2].to_chips()
    totals[1].to_chips()
    input_gradient(0, 0, windows, wide_a)
    for w in every:
        for r in range(WIN):
            a = w * SLOTS + r * WIN
            field_a[r * stride + w * WIN : r * stride + (w + 1) * WIN] = wide_a[a : a + WIN]
    for r in range(WIN):
        input_v[r] = field_a[r * stride : r * stride + cols]
    out_copy.wait()
    for w in every:
        wide_d[w * hs : (w + 1) * hs] = orecv[w].astype(f32)
    from_shifted(wide_d, hs, field_c, 0, every)
    from_shifted(wide_e, SLOTS, field_c, hw, every)
    wrap_starts(field_c, range(WIN))
    for r in range(WIN):
        block_v[r] = field_c[r * stride : r * stride + cols].astype(bf16)
    totals[2].spread()
    totals[1].spread()
    totals[0].share()
    totals[2].share()
    totals[1].share()
    for load in state_loads:
        load.wait()
    for total in totals:
        total.done()


def main_call(strips, windows, cols, n_grid):
    T = windows * SLOTS
    hw = WIN // 2
    chips = n_grid * strips // 2
    vm = pltpu.VMEM
    hs = hw * WIN
    scratch = [
        vm((WIN, cols, D), bf16),
        vm((WIN, 1, cols), jnp.int32),
        vm((WIN, cols, D), bf16),
        vm((2, D, 3 * D), bf16),
        vm((2, D, D), bf16),
        vm((2, D, FF), bf16),
        vm((2, FF, D), bf16),
        vm((2, T, D), bf16),
        vm((2, T, D), bf16),
        vm((2, T, D), bf16),
        vm((2, T, D), bf16),
        vm((2, T, D), bf16),
        vm((2, T, LANES), bf16),
        vm((2, T, D), bf16),
        vm((2, T, D), bf16),
        vm((2, T, D), f32),
        vm((2, T, D), f32),
        vm((2, T, FF), bf16),
        vm((2, T, FF), f32),
        vm((2, T, D), f32),
        vm((2, T, D), f32),
        vm((2, windows, 1, LANES), f32),
        vm((2, T, D), f32),
        vm((128, LANES), f32),
        *[vm((WIN * (cols + 8), D), f32) for _ in range(4)],
        *[vm((T, D), f32) for _ in range(8)],
        vm((windows, SLOTS, LANES), f32),
        vm((T, D), bf16),
        vm((T, FF), bf16),
        vm((T, D), bf16),
        vm((T, D), bf16),
        vm((T, D), f32),
        vm((T, LANES), bf16),
        vm((T, D), bf16),
        vm((T, D), bf16),
        vm((T, D), bf16),
        vm((16, 128), f32),
        vm((16, 128), f32),
        vm((windows, hs, D), bf16),
        vm((windows, hs, D), bf16),
        vm((windows, hs, D), bf16),
        vm((windows, hs, D), bf16),
        vm((hw, cols, D), bf16),
        vm((windows, hs, D), bf16),
        vm((windows, hs, D), bf16),
    ]
    outs = []
    for rows in SET_ROWS:
        c = chunk_rows(rows, 2 * chips)
        scratch += [
            vm((2 * chips * c, D), f32),
            vm((chips, c, D), bf16),
            vm((chips, c, D), bf16),
            vm((chips, c, D), bf16),
            vm((chips, c, D), bf16),
        ]
        outs.append(vm((2, chips, c, D), bf16))
    copies = COPIES + 3 * 4
    scratch += [pltpu.SemaphoreType.DMA((n,)) for n in (copies, copies, 9, 12)]
    params = [(2, D, 3 * D), (2, D, D), (2, D, FF), (2, FF, D), (2, SLOTS, D), (2, 4, D)]
    outs += [vm(shape, f32) for shape in params * 3]
    near = pl.BlockSpec(memory_space=pltpu.VMEM)
    far = pl.BlockSpec(memory_space=pl.ANY)
    return pl.pallas_call(
        functools.partial(main_kernel, strips, windows, n_grid),
        out_shape=(
            vm((WIN, cols, D), bf16),
            vm((WIN, cols, D), f32),
            *outs,
        ),
        in_specs=[far] * 21,
        out_specs=(near,) * 23,
        scratch_shapes=scratch,
        compiler_params=pltpu.CompilerParams(
            collective_id=0, has_side_effects=True, vmem_limit_bytes=40 * 1024 * 1024
        ),
    )


def lamb_kernel(*refs):
    grads_near = refs[0:3]
    block_near, input_near = refs[3:5]
    states = refs[5:23]
    block_out, input_out = refs[23:25]
    results_far = refs[25:43]
    clip_out, norms_out = refs[43:45]
    results = refs[45:63]
    out_sem, cell_sem = refs[63:65]
    cells = [
        pltpu.make_async_copy(block_near, block_out, cell_sem.at[0]),
        pltpu.make_async_copy(input_near, input_out, cell_sem.at[1]),
    ]
    for copy in cells:
        copy.start()
    stores = [
        pltpu.make_async_copy(results[i], results_far[i], out_sem.at[i]) for i in range(18)
    ]
    grads = [g[...].astype(f32).reshape(-1, D) for g in grads_near]
    clip_norm = jnp.sqrt(sum(jnp.sum(g * g, keepdims=True) for g in grads))
    clip_out[...] = clip_norm
    factor = clip_bound / jnp.maximum(clip_norm, clip_bound)
    fix_one = 1.0 / (1.0 - beta_one**STEP)
    fix_two = 1.0 / (1.0 - beta_two**STEP)

    def grad_rows(l, name, start, rows):
        if l == 1:
            number, table = 0, L1
        elif name in L0_FF:
            number, table = 1, L0_FF
        else:
            number, table = 2, L0_REST
        return grads[number][table[name] + start : table[name] + start + rows]

    def step(index, where, grad, decay):
        grad = grad * factor
        old = states[index][where]
        moment = beta_one * states[6 + index][where] + (1.0 - beta_one) * grad
        square = beta_two * states[12 + index][where] + (1.0 - beta_two) * grad * grad
        results[6 + index][where] = moment
        results[12 + index][where] = square
        direction = moment * fix_one / (jnp.sqrt(square * fix_two) + epsilon)
        if decay:
            direction = direction + weight_decay * old
        results[index][where] = direction
        return old, direction

    found = {}
    order = ((0, "qkv", D), (2, "ee", D), (3, "r", FF), (4, "p", SLOTS), (1, "o", D))
    for index, names, height in order:
        for l in range(2):
            weight_sum, step_sum = [], []
            for b, name in enumerate(names):
                where = (l, slice(None), slice(b * D, (b + 1) * D))
                grad = grad_rows(l, name, b * D if name == "e" else 0, height)
                old, direction = step(index, where, grad, True)
                weight_sum.append(jnp.sum(old * old, axis=0, keepdims=True))
                step_sum.append(jnp.sum(direction * direction, axis=0, keepdims=True))
            found[l, index] = tuple(
                jnp.sqrt(jnp.sum(sum(parts), axis=1, keepdims=True))
                for parts in (weight_sum, step_sum)
            )
        for kind in (1, 2):
            stores[6 * kind + index].start()
    for index, names, _ in order:
        for l in range(2):
            weight_norm, step_norm = found[l, index]
            scale = learn_rate * weight_norm / (step_norm + epsilon)
            results[index][l] = states[index][l] - scale * results[index][l]
        stores[index].start()
    for l in range(2):
        old, direction = step(5, (l,), grad_rows(l, "n", 0, 4), False)
        weight_norm = jnp.sqrt(jnp.sum(old * old, axis=1, keepdims=True))
        step_norm = jnp.sqrt(jnp.sum(direction * direction, axis=1, keepdims=True))
        results[5][l] = old - learn_rate * weight_norm / (step_norm + epsilon) * direction
        for r in range(4):
            found[l, 5 + r] = (weight_norm[r : r + 1], step_norm[r : r + 1])
        row = lax.broadcasted_iota(jnp.int32, (2, 9), 0)
        lane = lax.broadcasted_iota(jnp.int32, (2, 9), 1)
        table = jnp.zeros((2, 9), f32)
        for t in range(9):
            for j in range(2):
                value = jnp.broadcast_to(found[l, t][j], (2, 9))
                table = jnp.where((row == j) & (lane == t), value, table)
        norms_out[l] = table
    for kind in range(3):
        stores[6 * kind + 5].start()
    for copy in stores + cells:
        copy.wait()


def lamb_call(grads, block_output, input_grad, states):
    whole = pl.BlockSpec(memory_space=pltpu.VMEM)
    far = pl.BlockSpec(memory_space=pl.ANY)
    like = lambda a: jax.ShapeDtypeStruct(a.shape, a.dtype)
    out = [like(block_output), like(input_grad)]
    out += [like(a) for a in states]
    out += [jax.ShapeDtypeStruct((1, 1), f32), jax.ShapeDtypeStruct((2, 2, 9), f32)]
    near = [pltpu.VMEM(a.shape, a.dtype) for a in states]
    return pl.pallas_call(
        lamb_kernel,
        out_shape=out,
        in_specs=[whole] * 23,
        out_specs=[far] * 20 + [whole] * 2,
        scratch_shapes=near + [pltpu.SemaphoreType.DMA((n,)) for n in (18, 2)],
        compiler_params=pltpu.CompilerParams(vmem_limit_bytes=32 * 1024 * 1024),
    )(*grads, block_output, input_grad, *states)


def body(mesh, features, cell_frame, cotangent, *rest):
    cols = features.shape[2]
    call = main_call(mesh.shape["strip"], cols // WIN, cols, mesh.shape["grid"])
    cell_frame = cell_frame.reshape(WIN, 1, cols)
    held = [
        pltpu.with_memory_space_constraint(a, pltpu.HBM)
        for a in (features[0], cell_frame, cotangent[0], *rest)
    ]
    found = call(*held)
    out = lamb_call(found[2:5], found[0], found[1], found[5:23])
    norms = jnp.swapaxes(out[21], 1, 2)
    return (out[0][None], out[1][None], *out[2:20], out[20].reshape(()), norms)


def solution(mesh):
    cells = P("grid", "strip", None, None)
    return jax.shard_map(
        functools.partial(body, mesh),
        mesh=mesh,
        in_specs=(cells, P("grid", "strip", None), cells) + (P(),) * 18,
        out_specs=(cells, cells) + (P(),) * 20,
        check_vma=False,
    )
```

```python
import functools

import jax
import jax.numpy as jnp
import numpy as np
from jax import lax
from jax.experimental import pallas as pl
from jax.experimental.pallas import tpu as pltpu
from jax.sharding import PartitionSpec as P

bf16 = jnp.bfloat16
f32 = jnp.float32
MESH = pl.DeviceIdType.MESH

HEADS = 8
HEAD = 16
D = 128
FF = 256
WIN = 12
SLOTS = WIN * WIN
LANES = HEADS * SLOTS
STEP = 10
beta_one = 0.9
beta_two = 0.999
learn_rate = 0.2
weight_decay = 0.01
epsilon = 1e-06
clip_bound = 1.0

L1 = dict(q=0, k=128, v=256, o=384, e=512, r=768, p=1024, n=1168)
L0_FF = dict(e=0, r=256)
L0_REST = dict(q=0, k=128, v=256, o=384, p=512, n=656)
SET_ROWS = (1176, 512, 664)

PARTS = ((0, 80), (80, SLOTS))
BOTH = (0, 1)
COPIES = 5


def lanes_of(parts):
    return HEADS * PARTS[parts[0]][0], HEADS * PARTS[parts[-1]][1]


def tiles_of(parts):
    first, end = lanes_of(parts)
    return [(a, min(a + 256, end)) for a in range(first, end, 256)]


def nt(a, b):
    return lax.dot_general(a, b, (((1,), (1,)), ((), ())), preferred_element_type=f32)


def tn(a, b):
    return lax.dot_general(a, b, (((0,), (0,)), ((), ())), preferred_element_type=f32)


def nn(a, b):
    return jnp.dot(a, b, preferred_element_type=f32)


def head_blocks(block):
    lane = lax.broadcasted_iota(jnp.int32, block.shape, 1)
    parts = []
    for h in range(HEADS):
        keep = (lane >= h * HEAD) & (lane < (h + 1) * HEAD)
        parts.append(jnp.where(keep, block, jnp.zeros_like(block)))
    return jnp.concatenate(parts, axis=0)


def diagonal(full):
    n = full.shape[1] // HEADS
    return jnp.concatenate(
        [full[h * HEAD : (h + 1) * HEAD, h * n : (h + 1) * n] for h in range(HEADS)], axis=0
    ).T


def chunk_rows(rows, parts):
    return (-(-rows // parts) + 7) // 8 * 8


def main_kernel(
    strips,
    windows,
    n_grid,
    feat_in,
    codes_in,
    cot_in,
    attend_in,
    output_in,
    expand_in,
    reduce_in,
    position_in,
    norms_in,
    *refs,
):
    states_in, refs = refs[:12], refs[12:]
    outs, refs = refs[:23], refs[23:]
    run(strips, windows, n_grid, feat_in, codes_in, cot_in, attend_in, output_in, expand_in,
        reduce_in, position_in, norms_in, states_in, outs, *refs)


def run(
    strips,
    windows,
    n_grid,
    feat_in,
    codes_in,
    cot_in,
    attend_in,
    output_in,
    expand_in,
    reduce_in,
    position_in,
    norms_in,
    states_in,
    outs,
    feat,
    codes_v,
    cot,
    wa,
    wo,
    we,
    wr,
    xt,
    mi,
    qs,
    ks,
    vs,
    probs,
    att,
    first_b,
    xh1,
    rs1,
    act,
    dgelu,
    xh2,
    rs2,
    crow,
    ccol,
    ctab,
    field_a,
    field_b,
    field_c,
    field_d,
    wide_a,
    wide_b,
    wide_c,
    wide_d,
    wide_e,
    wide_f,
    wide_g,
    wide_h,
    kept_v,
    kept_k,
    scores_s,
    d_br2,
    d_hid,
    d_br,
    d_att,
    d_res,
    ds_s,
    d_q,
    d_k,
    d_v,
    csend,
    crecv,
    hsend,
    hrecv,
    osend,
    orecv,
    grecv,
    bsend,
    brecv,
    *sums_and_sems,
):
    send_sem, recv_sem, in_sem, out_sem = sums_and_sems[-4:]
    T = windows * SLOTS
    cols = windows * WIN
    stride = cols + 8
    hw = WIN // 2
    hs = hw * WIN
    gi = lax.axis_index("grid")
    si = lax.axis_index("strip")
    core = lax.rem(si, 2)
    zi = lax.div(si, 2)
    n_z = strips // 2
    chips = n_grid * n_z
    chip = gi * n_z + zi
    prev = lax.rem(si + strips - 1, strips)
    nxt = lax.rem(si + 1, strips)
    sib = si + 1 - 2 * core
    others = []
    for dz in sorted(range(n_z), key=lambda d: -min(d, n_z - d)):
        for dg in reversed(range(n_grid)):
            if (dz, dg) != (0, 0):
                g_p, z_p = lax.rem(gi + dg, n_grid), lax.rem(zi + dz, n_z)
                others.append((g_p * n_z + z_p, (g_p, z_p * 2 + core)))

    block_v, input_v = outs[0:2]
    attend_w, output_w, expand_w, reduce_w, position, norms = outs[5:11]
    loads = {}
    for i, (src, dst) in enumerate(
        (
            (feat_in, feat),
            (codes_in, codes_v),
            (attend_in, attend_w),
            (position_in, position),
            (output_in, output_w),
            (expand_in, expand_w),
            (reduce_in, reduce_w),
            (norms_in, norms),
            (cot_in, cot),
        )
    ):
        loads[i] = pltpu.make_async_copy(src, dst, in_sem.at[i])
        loads[i].start()

    state_loads = []
    for i, (src, dst) in enumerate(zip(states_in, outs[11:23])):
        state_loads.append(pltpu.make_async_copy(src, dst, out_sem.at[i]))

    barrier = pltpu.get_barrier_semaphore()
    peers = [(gi, prev), (gi, nxt), (gi, sib)] + [device for _, device in others]
    for peer in peers:
        pl.semaphore_signal(barrier, inc=1, device_id=peer, device_id_type=MESH)

    def remote(src, dst, index, device):
        return pltpu.make_async_remote_copy(
            src_ref=src,
            dst_ref=dst,
            send_sem=send_sem.at[index],
            recv_sem=recv_sem.at[index],
            device_id=device,
            device_id_type=MESH,
        )

    class Total:
        def __init__(self, number):
            self.g, self.s1, self.r1, self.s2, self.r2 = sums_and_sems[
                number * 5 : number * 5 + 5
            ]
            self.out = outs[2 + number]
            self.c = chunk_rows(SET_ROWS[number], 2 * chips)
            self.sem = COPIES + number * 4

        def rows(self, half, j):
            return pl.ds(pl.multiple_of((half * chips + j) * self.c, 8), self.c)

        def to_sibling(self):
            used = SET_ROWS[number_of(self)]
            if used < 2 * chips * self.c:
                self.g[used:] = jnp.zeros((2 * chips * self.c - used, D), f32)
            for j in range(chips):
                self.s1[j] = self.g[self.rows(1 - core, j)].astype(bf16)
            self.first = remote(self.s1, self.r1, self.sem, (gi, sib))
            self.first.start()

        def to_chips(self):
            self.first.wait()
            for j in range(chips):
                both = self.g[self.rows(core, j)] + self.r1[j].astype(f32)
                self.s2[j] = both.astype(bf16)
            for number, device in others:
                remote(self.s2.at[number], self.r2.at[chip], self.sem + 1, device).start()
            self.r2[chip] = self.s2[chip]

        def all_arrived(self, buffer, index):
            bytes_of = buffer.at[pl.ds(0, chips - 1)]
            remote(bytes_of, bytes_of, index, (gi, sib)).wait()

        def spread(self):
            self.all_arrived(self.r2, self.sem + 1)
            total = self.r2[0].astype(f32)
            for j in range(1, chips):
                total = total + self.r2[j].astype(f32)
            self.out[core, chip] = total.astype(bf16)
            mine = self.out.at[core, chip]
            for number, device in others:
                remote(mine, mine, self.sem + 2, device).start()

        def share(self):
            self.all_arrived(self.r2, self.sem + 2)
            mine = self.out.at[core]
            self.last = remote(mine, mine, self.sem + 3, (gi, sib))
            self.last.start()

        def done(self):
            self.last.wait()

    totals = [Total(n) for n in range(3)]
    number_of = totals.index
    homes = (
        {"e": (totals[1], L0_FF), "r": (totals[1], L0_FF)},
        {},
    )

    def put(l, name, value, rows):
        total, table = homes[l].get(name, (totals[2], L0_REST) if l == 0 else (totals[0], L1))
        total.g[table[name] : table[name] + rows] = value

    def code_tables(l, table):
        low = table.astype(bf16)
        lane = lax.broadcasted_iota(jnp.int32, (16, LANES), 1).astype(f32)
        row = lax.broadcasted_iota(jnp.int32, (16, LANES), 0).astype(f32)
        cut, end = PARTS[0][1], PARTS[1][1]
        lane_b = lane - HEADS * cut
        slot_a = lane - cut * jnp.floor((lane + 0.5) * (1.0 / cut))
        slot_b = lane_b - (end - cut) * jnp.floor((lane_b + 0.5) * (1.0 / (end - cut))) + cut
        slot = jnp.where(lane_b < 0.0, slot_a, slot_b)
        slot_r = jnp.floor((slot + 0.5) * (1.0 / WIN))
        slot_c = slot - WIN * slot_r
        pick_r = (slot_r == row).astype(bf16)
        ctab[...] = tn(low, pick_r)
        pick_c = (slot_c == row).astype(f32)[0:WIN]
        for w in range(windows):
            part = ctab[w * WIN : (w + 1) * WIN, :]
            crow[l, w] = jnp.sum(part * pick_c, axis=0, keepdims=True)
        token = lax.broadcasted_iota(jnp.int32, (SLOTS, 128), 0).astype(f32)
        place = lax.broadcasted_iota(jnp.int32, (SLOTS, 128), 1).astype(f32)
        token_r = jnp.floor((token + 0.5) * (1.0 / WIN))
        token_c = token - WIN * token_r
        row_of = (token_r == place).astype(bf16)[:, 0:16]
        spread = nn(row_of, low)
        for w in range(windows):
            chosen = jnp.where(place == token_c + w * WIN, spread, 0.0)
            value = jnp.sum(chosen, axis=1, keepdims=True)
            ccol[l, w * SLOTS : (w + 1) * SLOTS] = jnp.broadcast_to(value, (SLOTS, 128))

    every = range(windows)

    def window_rows(w):
        return slice(w * SLOTS, (w + 1) * SLOTS)

    def in_turn(chosen, before, middle, after):
        before(chosen[0])
        for i, w in enumerate(chosen):
            if i + 1 < len(chosen):
                before(chosen[i + 1])
            middle(w)
            if i > 0:
                after(chosen[i - 1])
        after(chosen[-1])

    def rows_of(w, p):
        return slice(w * SLOTS + PARTS[p][0], w * SLOTS + PARTS[p][1])

    def take(ref, parts):
        if parts == BOTH:
            return ref[...]
        return jnp.concatenate([ref[rows_of(w, p)] for w in every for p in parts], axis=0)

    def give(ref, parts, value):
        if parts == BOTH:
            ref[...] = value
            return
        n = value.shape[0] // windows
        for w in every:
            ref[rows_of(w, parts[0])] = value[w * n : (w + 1) * n]

    def blocks(ref, w, parts):
        return jnp.concatenate([head_blocks(ref[rows_of(w, p)]) for p in parts], axis=0)

    def diagonals(full, parts):
        first, _ = lanes_of(parts)
        found = []
        for p in parts:
            a, b = lanes_of((p,))
            found.append(diagonal(full[:, a - first : b - first]))
        return found

    def project(l):
        x = xt[l]
        m = (x.astype(f32) + jnp.concatenate([position[l]] * windows, axis=0)).astype(bf16)
        mi[l] = m
        qk = nn(m, wa[l, :, 0 : 2 * D])
        qs[l] = (qk[:, 0:D] * HEAD ** (-0.5)).astype(bf16)
        ks[l] = qk[:, D : 2 * D].astype(bf16)
        vs[l] = nn(x, wa[l, :, 2 * D : 3 * D]).astype(bf16)

    def attend(l, parts):
        first, end = lanes_of(parts)

        def scores_of(w):
            scores_s[w, :, first:end] = nt(ks[l, window_rows(w)], blocks(qs.at[l], w, parts))

        def soften(w):
            one = window_rows(w)
            cc = ccol[l, one]
            cr = crow[l, w]
            for a, b in tiles_of(parts):
                same = jnp.concatenate([cc] * ((b - a) // 128), axis=1) == cr[:, a:b]
                scores = jnp.where(same, scores_s[w, :, a:b], -1000000000.0)
                top = jnp.max(scores, axis=0, keepdims=True)
                weights = jnp.exp(scores - top)
                total = jnp.sum(weights, axis=0, keepdims=True)
                probs[l, one, a:b] = (weights * (1.0 / total)).astype(bf16)

        def mix(w):
            one = window_rows(w)
            full = nn(vs[l, one].T, probs[l, one, first:end])
            for p, value in zip(parts, diagonals(full, parts)):
                att[l, rows_of(w, p)] = value.astype(bf16)

        in_turn(every, scores_of, soften, mix)

    def feed_forward(l, parts, out):
        r = take(xt.at[l], parts).astype(f32) + nn(take(att.at[l], parts), wo[l])
        c = r - jnp.mean(r, axis=1, keepdims=True)
        s = lax.rsqrt(jnp.mean(c * c, axis=1, keepdims=True) + 1e-05)
        n = c * s
        give(xh1.at[l], parts, n)
        give(rs1.at[l], parts, jnp.broadcast_to(s, n.shape))
        first = n * norms[l, 0:1] + norms[l, 1:2]
        fb = first.astype(bf16)
        give(first_b.at[l], parts, fb)
        h = nn(fb, we[l])
        h2 = h * h
        t = jnp.tanh(0.7978845608028654 * h * (1.0 + 0.044715 * h2))
        act_b = (0.5 * h * (1.0 + t)).astype(bf16)
        give(act.at[l], parts, act_b)
        slope = 0.7978845608028654 * (1.0 + 3.0 * 0.044715 * h2)
        give(dgelu.at[l], parts, 0.5 * (1.0 + t) + 0.5 * h * (1.0 - t * t) * slope)
        r = first + nn(act_b, wr[l])
        c = r - jnp.mean(r, axis=1, keepdims=True)
        s = lax.rsqrt(jnp.mean(c * c, axis=1, keepdims=True) + 1e-05)
        n = c * s
        give(xh2.at[l], parts, n)
        give(rs2.at[l], parts, jnp.broadcast_to(s, n.shape))
        second = n * norms[l, 2:3] + norms[l, 3:4]
        second = jnp.where(take(ccol.at[l], parts) > 0.0, second, 0.0)
        give(out, parts, second.astype(bf16).astype(f32))

    def norm_back(d, gain, n, s):
        dn = d * gain
        m1 = jnp.mean(dn, axis=1, keepdims=True)
        m2 = jnp.mean(dn * n, axis=1, keepdims=True)
        return s * (dn - m1 - n * m2)

    def dense_backward(l, parts, grad_out):
        d = jnp.where(take(ccol.at[l], parts) > 0.0, take(grad_out, parts), 0.0)
        n2 = take(xh2.at[l], parts)
        bias2 = jnp.sum(d, axis=0, keepdims=True)
        gain2 = jnp.sum(d * n2, axis=0, keepdims=True)
        d2 = norm_back(d, norms[l, 2:3], n2, take(rs2.at[l], parts))
        b2 = d2.astype(bf16)
        give(d_br2, parts, b2)
        dh = (nt(b2, wr[l]) * take(dgelu.at[l], parts)).astype(bf16)
        give(d_hid, parts, dh)
        d1 = d2 + nt(dh, we[l])
        n1 = take(xh1.at[l], parts)
        bias1 = jnp.sum(d1, axis=0, keepdims=True)
        gain1 = jnp.sum(d1 * n1, axis=0, keepdims=True)
        dr = norm_back(d1, norms[l, 0:1], n1, take(rs1.at[l], parts))
        give(d_res, parts, dr)
        b1 = dr.astype(bf16)
        give(d_br, parts, b1)
        give(d_att, parts, nt(b1, wo[l]).astype(bf16))
        return [gain1, bias1, gain2, bias2]

    def norm_grads(l, parts):
        lines = [sum(lines) for lines in zip(*parts)] + [jnp.zeros((4, D), f32)]
        put(l, "n", jnp.concatenate(lines, axis=0), 8)

    def feed_forward_grads(l):
        put(l, "r", tn(act[l], d_br2[...]), FF)
        d_expand = tn(first_b[l], d_hid[...])
        put(l, "e", jnp.concatenate([d_expand[:, 0:D], d_expand[:, D : 2 * D]], axis=0), FF)

    def attention_backward(l, parts, add_to=None, keep=None):
        first, end = lanes_of(parts)

        def put_rows(which, target, rows, value):
            if keep is not None:
                keep[which][rows] = value
                return
            if add_to is not None:
                value = value + add_to[which][rows]
            target[rows] = value.astype(bf16)

        def d_probs_of(w):
            rows = window_rows(w)
            db = blocks(d_att, w, parts)
            put_rows(0, d_v, rows, nn(probs[l, rows, first:end], db))
            scores_s[w, :, first:end] = nt(vs[l, rows], db)

        def d_soften(w):
            rows = window_rows(w)
            for a, b in tiles_of(parts):
                dp = scores_s[w, :, a:b]
                p = probs[l, rows, a:b].astype(f32)
                ds = p * (dp - jnp.sum(dp * p, axis=0, keepdims=True))
                ds_s[rows, a:b] = ds.astype(bf16)

        def d_mix(w):
            rows = window_rows(w)
            ds = ds_s[rows, first:end]
            put_rows(1, d_k, rows, nn(ds, blocks(qs.at[l], w, parts)))
            full = nn(ks[l, rows].T, ds)
            for p, value in zip(parts, diagonals(full, parts)):
                d_q[rows_of(w, p)] = (value * HEAD ** (-0.5)).astype(bf16)

        in_turn(every, d_probs_of, d_soften, d_mix)

    def attention_grads(l):
        put(l, "o", tn(att[l], d_br[...]), D)
        put(l, "q", tn(mi[l], d_q[...]), D)
        put(l, "k", tn(mi[l], d_k[...]), D)
        put(l, "v", tn(xt[l], d_v[...]), D)
        d_pos = jnp.zeros((SLOTS, D), f32)
        for part, columns in ((d_q, slice(0, D)), (d_k, slice(D, 2 * D))):
            total = part[0:SLOTS].astype(f32)
            for w in range(1, windows):
                total = total + part[window_rows(w)].astype(f32)
            high = total.astype(bf16)
            low = (total - high.astype(f32)).astype(bf16)
            d_pos = d_pos + nt(high, wa[l, :, columns]) + nt(low, wa[l, :, columns])
        put(l, "p", d_pos, SLOTS)

    def input_gradient(l, out):
        d = nt(d_q[...], wa[l, :, 0:D]) + nt(d_k[...], wa[l, :, D : 2 * D])
        out[...] = d_res[...] + d + nt(d_v[...], wa[l, :, 2 * D : 3 * D])

    def lower(l):
        wa[l] = attend_w[l].astype(bf16)
        wo[l] = output_w[l].astype(bf16)
        we[l] = expand_w[l].astype(bf16)
        wr[l] = reduce_w[l].astype(bf16)

    def to_windows(source, target, rows):
        for w in every:
            for r in rows:
                a = w * SLOTS + r * WIN
                target[a : a + WIN] = source[r * stride + w * WIN : r * stride + (w + 1) * WIN]

    def wrap_ends(field, rows):
        for r in rows:
            field[r * stride + cols : r * stride + cols + hw] = field[r * stride : r * stride + hw]

    def wrap_starts(field, rows):
        for r in rows:
            field[r * stride : r * stride + hw] = field[r * stride + cols : r * stride + cols + hw]

    def to_shifted(source, target, rows):
        for w in every:
            for r in rows:
                a = w * SLOTS + r * WIN
                b = r * stride + w * WIN + hw
                target[a : a + WIN] = source[b : b + WIN]

    def from_shifted(source, source_rows, field, first_row):
        for w in every:
            for r in range(hw):
                a = w * source_rows + r * WIN
                b = (r + first_row) * stride + w * WIN + hw
                field[b : b + WIN] = source[a : a + WIN]

    top, bottom = range(hw), range(hw, WIN)

    loads[0].wait()
    for r in range(WIN):
        field_a[r * stride : r * stride + cols] = feat[r].astype(f32)
    to_windows(field_a, wide_a, range(WIN))
    xt[0] = wide_a[...].astype(bf16)
    loads[1].wait()
    csend[...] = jnp.zeros((16, 128), f32)
    for r in range(WIN):
        csend[r : r + 1, 0:cols] = codes_v[r].astype(f32)
    code_tables(0, csend[...])
    for i in range(2, 8):
        loads[i].wait()
    lower(0)
    project(0)
    attend(0, (0,))
    feed_forward(0, (0,), wide_b)
    for w in every:
        hsend[w] = wide_b[w * SLOTS : w * SLOTS + hs].astype(bf16)
    pl.semaphore_wait(barrier, len(peers))
    codes_copy = remote(csend, crecv, 0, (gi, prev))
    codes_copy.start()
    halo_copy = remote(hsend, hrecv, 1, (gi, prev))
    halo_copy.start()
    for load in state_loads:
        load.start()

    attend(0, (1,))
    feed_forward(0, (1,), wide_b)
    lower(1)
    for w in every:
        for r in top:
            a = w * SLOTS + (r + hw) * WIN
            field_b[r * stride + w * WIN : r * stride + (w + 1) * WIN] = wide_b[a : a + WIN]
    wrap_ends(field_b, top)
    to_shifted(field_b, wide_c, top)
    loads[8].wait()
    for r in top:
        field_c[r * stride : r * stride + cols] = cot[r + hw].astype(f32)
    wrap_ends(field_c, top)
    to_shifted(field_c, wide_f, top)
    codes_copy.wait()
    own = csend[...]
    other = crecv[...]
    table = jnp.concatenate([own[hw:WIN], other[0:hw], jnp.zeros((4, 128), f32)], axis=0)
    table = jnp.concatenate(
        [table[:, hw:cols], table[:, 0:hw], jnp.zeros((16, 128 - cols), f32)], axis=1
    )
    code_tables(1, table)

    halo_copy.wait()
    cot_copy = remote(cot_in.at[pl.ds(0, hw)], grecv, 2, (gi, prev))
    cot_copy.start()
    for w in every:
        wide_d[w * hs : (w + 1) * hs] = hrecv[w].astype(f32)
        for r in top:
            x = w * hs + r * WIN
            y = (r + hw) * stride + w * WIN
            field_b[y : y + WIN] = wide_d[x : x + WIN]
    wrap_ends(field_b, bottom)
    to_shifted(field_b, wide_c, bottom)
    xt[1] = wide_c[...].astype(bf16)
    project(1)
    attend(1, BOTH)
    feed_forward(1, BOTH, wide_e)

    for w in every:
        osend[w] = wide_e[w * SLOTS + hs : (w + 1) * SLOTS].astype(bf16)
    out_copy = remote(osend, orecv, 3, (gi, nxt))
    out_copy.start()

    cot_copy.wait()
    for r in top:
        field_c[(r + hw) * stride : (r + hw) * stride + cols] = grecv[r].astype(f32)
    wrap_ends(field_c, bottom)
    to_shifted(field_c, wide_f, bottom)
    norm_parts = [dense_backward(1, BOTH, wide_f)]
    attention_backward(1, BOTH)
    input_gradient(1, wide_g)
    for w in every:
        bsend[w] = wide_g[w * SLOTS + hs : (w + 1) * SLOTS].astype(bf16)
    back_copy = remote(bsend, brecv, 4, (gi, nxt))
    back_copy.start()

    norm_grads(1, norm_parts)
    feed_forward_grads(1)
    attention_grads(1)
    totals[0].to_sibling()
    from_shifted(wide_g, SLOTS, field_d, hw)
    wrap_starts(field_d, bottom)
    to_windows(field_d, wide_h, bottom)
    for w in every:
        late = slice(w * SLOTS + hs, (w + 1) * SLOTS)
        wide_h[late] = wide_h[late].astype(bf16).astype(f32)
    norm_parts = [dense_backward(0, (1,), wide_h)]
    attention_backward(0, (1,), keep=(kept_v, kept_k))

    back_copy.wait()
    totals[0].to_chips()
    for w in every:
        wide_d[w * hs : (w + 1) * hs] = brecv[w].astype(f32)
    from_shifted(wide_d, hs, field_d, 0)
    wrap_starts(field_d, top)
    to_windows(field_d, wide_h, top)
    norm_parts.append(dense_backward(0, (0,), wide_h))
    feed_forward_grads(0)
    totals[1].to_sibling()
    attention_backward(0, (0,), add_to=(kept_v, kept_k))
    norm_grads(0, norm_parts)
    attention_grads(0)
    totals[2].to_sibling()
    totals[1].to_chips()
    totals[2].to_chips()
    input_gradient(0, wide_a)
    for w in every:
        for r in range(WIN):
            a = w * SLOTS + r * WIN
            field_a[r * stride + w * WIN : r * stride + (w + 1) * WIN] = wide_a[a : a + WIN]
    for r in range(WIN):
        input_v[r] = field_a[r * stride : r * stride + cols]
    out_copy.wait()
    for w in every:
        wide_d[w * hs : (w + 1) * hs] = orecv[w].astype(f32)
    from_shifted(wide_d, hs, field_c, 0)
    from_shifted(wide_e, SLOTS, field_c, hw)
    wrap_starts(field_c, range(WIN))
    for r in range(WIN):
        block_v[r] = field_c[r * stride : r * stride + cols].astype(bf16)
    totals[0].spread()
    totals[1].spread()
    totals[2].spread()
    totals[0].share()
    totals[1].share()
    totals[2].share()
    for load in state_loads:
        load.wait()
    for total in totals:
        total.done()


def main_call(strips, windows, cols, n_grid):
    T = windows * SLOTS
    hw = WIN // 2
    chips = n_grid * strips // 2
    vm = pltpu.VMEM
    hs = hw * WIN
    scratch = [
        vm((WIN, cols, D), bf16),
        vm((WIN, 1, cols), jnp.int32),
        vm((WIN, cols, D), bf16),
        vm((2, D, 3 * D), bf16),
        vm((2, D, D), bf16),
        vm((2, D, FF), bf16),
        vm((2, FF, D), bf16),
        vm((2, T, D), bf16),
        vm((2, T, D), bf16),
        vm((2, T, D), bf16),
        vm((2, T, D), bf16),
        vm((2, T, D), bf16),
        vm((2, T, LANES), bf16),
        vm((2, T, D), bf16),
        vm((2, T, D), bf16),
        vm((2, T, D), f32),
        vm((2, T, D), f32),
        vm((2, T, FF), bf16),
        vm((2, T, FF), f32),
        vm((2, T, D), f32),
        vm((2, T, D), f32),
        vm((2, windows, 1, LANES), f32),
        vm((2, T, D), f32),
        vm((128, LANES), f32),
        *[vm((WIN * (cols + 8), D), f32) for _ in range(4)],
        *[vm((T, D), f32) for _ in range(10)],
        vm((windows, SLOTS, LANES), f32),
        vm((T, D), bf16),
        vm((T, FF), bf16),
        vm((T, D), bf16),
        vm((T, D), bf16),
        vm((T, D), f32),
        vm((T, LANES), bf16),
        vm((T, D), bf16),
        vm((T, D), bf16),
        vm((T, D), bf16),
        vm((16, 128), f32),
        vm((16, 128), f32),
        vm((windows, hs, D), bf16),
        vm((windows, hs, D), bf16),
        vm((windows, hs, D), bf16),
        vm((windows, hs, D), bf16),
        vm((hw, cols, D), bf16),
        vm((windows, hs, D), bf16),
        vm((windows, hs, D), bf16),
    ]
    outs = []
    for rows in SET_ROWS:
        c = chunk_rows(rows, 2 * chips)
        scratch += [
            vm((2 * chips * c, D), f32),
            vm((chips, c, D), bf16),
            vm((chips, c, D), bf16),
            vm((chips, c, D), bf16),
            vm((chips, c, D), bf16),
        ]
        outs.append(vm((2, chips, c, D), bf16))
    copies = COPIES + 3 * 4
    scratch += [pltpu.SemaphoreType.DMA((n,)) for n in (copies, copies, 9, 12)]
    params = [(2, D, 3 * D), (2, D, D), (2, D, FF), (2, FF, D), (2, SLOTS, D), (2, 4, D)]
    outs += [vm(shape, f32) for shape in params * 3]
    near = pl.BlockSpec(memory_space=pltpu.VMEM)
    far = pl.BlockSpec(memory_space=pl.ANY)
    return pl.pallas_call(
        functools.partial(main_kernel, strips, windows, n_grid),
        out_shape=(
            vm((WIN, cols, D), bf16),
            vm((WIN, cols, D), f32),
            *outs,
        ),
        in_specs=[far] * 21,
        out_specs=(near,) * 23,
        scratch_shapes=scratch,
        compiler_params=pltpu.CompilerParams(
            collective_id=0, has_side_effects=True, vmem_limit_bytes=40 * 1024 * 1024
        ),
    )


def lamb_kernel(*refs):
    grads_near = refs[0:3]
    block_near, input_near = refs[3:5]
    states = refs[5:23]
    block_out, input_out = refs[23:25]
    results_far = refs[25:43]
    clip_out, norms_out = refs[43:45]
    results = refs[45:63]
    out_sem, cell_sem = refs[63:65]
    cells = [
        pltpu.make_async_copy(block_near, block_out, cell_sem.at[0]),
        pltpu.make_async_copy(input_near, input_out, cell_sem.at[1]),
    ]
    for copy in cells:
        copy.start()
    stores = [
        pltpu.make_async_copy(results[i], results_far[i], out_sem.at[i]) for i in range(18)
    ]
    grads = [g[...].astype(f32).reshape(-1, D) for g in grads_near]
    clip_norm = jnp.sqrt(sum(jnp.sum(g * g, keepdims=True) for g in grads))
    clip_out[...] = clip_norm
    factor = clip_bound / jnp.maximum(clip_norm, clip_bound)
    fix_one = 1.0 / (1.0 - beta_one**STEP)
    fix_two = 1.0 / (1.0 - beta_two**STEP)

    def grad_rows(l, name, start, rows):
        if l == 1:
            number, table = 0, L1
        elif name in L0_FF:
            number, table = 1, L0_FF
        else:
            number, table = 2, L0_REST
        return grads[number][table[name] + start : table[name] + start + rows]

    def step(index, where, grad, decay):
        grad = grad * factor
        old = states[index][where]
        moment = beta_one * states[6 + index][where] + (1.0 - beta_one) * grad
        square = beta_two * states[12 + index][where] + (1.0 - beta_two) * grad * grad
        results[6 + index][where] = moment
        results[12 + index][where] = square
        direction = moment * fix_one / (jnp.sqrt(square * fix_two) + epsilon)
        if decay:
            direction = direction + weight_decay * old
        results[index][where] = direction
        return old, direction

    found = {}
    order = ((0, "qkv", D), (2, "ee", D), (3, "r", FF), (4, "p", SLOTS), (1, "o", D))
    for index, names, height in order:
        for l in range(2):
            weight_sum, step_sum = [], []
            for b, name in enumerate(names):
                where = (l, slice(None), slice(b * D, (b + 1) * D))
                grad = grad_rows(l, name, b * D if name == "e" else 0, height)
                old, direction = step(index, where, grad, True)
                weight_sum.append(jnp.sum(old * old, axis=0, keepdims=True))
                step_sum.append(jnp.sum(direction * direction, axis=0, keepdims=True))
            found[l, index] = tuple(
                jnp.sqrt(jnp.sum(sum(parts), axis=1, keepdims=True))
                for parts in (weight_sum, step_sum)
            )
        for kind in (1, 2):
            stores[6 * kind + index].start()
    for index, names, _ in order:
        for l in range(2):
            weight_norm, step_norm = found[l, index]
            scale = learn_rate * weight_norm / (step_norm + epsilon)
            results[index][l] = states[index][l] - scale * results[index][l]
        stores[index].start()
    for l in range(2):
        old, direction = step(5, (l,), grad_rows(l, "n", 0, 4), False)
        weight_norm = jnp.sqrt(jnp.sum(old * old, axis=1, keepdims=True))
        step_norm = jnp.sqrt(jnp.sum(direction * direction, axis=1, keepdims=True))
        results[5][l] = old - learn_rate * weight_norm / (step_norm + epsilon) * direction
        for r in range(4):
            found[l, 5 + r] = (weight_norm[r : r + 1], step_norm[r : r + 1])
        row = lax.broadcasted_iota(jnp.int32, (2, 9), 0)
        lane = lax.broadcasted_iota(jnp.int32, (2, 9), 1)
        table = jnp.zeros((2, 9), f32)
        for t in range(9):
            for j in range(2):
                value = jnp.broadcast_to(found[l, t][j], (2, 9))
                table = jnp.where((row == j) & (lane == t), value, table)
        norms_out[l] = table
    for kind in range(3):
        stores[6 * kind + 5].start()
    for copy in stores + cells:
        copy.wait()


def lamb_call(grads, block_output, input_grad, states):
    whole = pl.BlockSpec(memory_space=pltpu.VMEM)
    far = pl.BlockSpec(memory_space=pl.ANY)
    like = lambda a: jax.ShapeDtypeStruct(a.shape, a.dtype)
    out = [like(block_output), like(input_grad)]
    out += [like(a) for a in states]
    out += [jax.ShapeDtypeStruct((1, 1), f32), jax.ShapeDtypeStruct((2, 2, 9), f32)]
    near = [pltpu.VMEM(a.shape, a.dtype) for a in states]
    return pl.pallas_call(
        lamb_kernel,
        out_shape=out,
        in_specs=[whole] * 23,
        out_specs=[far] * 20 + [whole] * 2,
        scratch_shapes=near + [pltpu.SemaphoreType.DMA((n,)) for n in (18, 2)],
        compiler_params=pltpu.CompilerParams(vmem_limit_bytes=32 * 1024 * 1024),
    )(*grads, block_output, input_grad, *states)


def body(mesh, features, cell_frame, cotangent, *rest):
    cols = features.shape[2]
    call = main_call(mesh.shape["strip"], cols // WIN, cols, mesh.shape["grid"])
    cell_frame = cell_frame.reshape(WIN, 1, cols)
    held = [
        pltpu.with_memory_space_constraint(a, pltpu.HBM)
        for a in (features[0], cell_frame, cotangent[0], *rest)
    ]
    found = call(*held)
    out = lamb_call(found[2:5], found[0], found[1], found[5:23])
    norms = jnp.swapaxes(out[21], 1, 2)
    return (out[0][None], out[1][None], *out[2:20], out[20].reshape(()), norms)


def solution(mesh):
    cells = P("grid", "strip", None, None)
    return jax.shard_map(
        functools.partial(body, mesh),
        mesh=mesh,
        in_specs=(cells, P("grid", "strip", None), cells) + (P(),) * 18,
        out_specs=(cells, cells) + (P(),) * 20,
        check_vma=False,
    )
```

```python
import functools

import jax
import jax.numpy as jnp
import numpy as np
from jax import lax
from jax.experimental import pallas as pl
from jax.experimental.pallas import tpu as pltpu
from jax.sharding import PartitionSpec as P

bf16 = jnp.bfloat16
f32 = jnp.float32
MESH = pl.DeviceIdType.MESH

HEADS = 8
HEAD = 16
D = 128
FF = 256
WIN = 12
SLOTS = WIN * WIN
LANES = HEADS * SLOTS
STEP = 10
beta_one = 0.9
beta_two = 0.999
learn_rate = 0.2
weight_decay = 0.01
epsilon = 1e-06
clip_bound = 1.0

FEED = dict(e=0, r=256)
REST = dict(q=0, k=128, v=256, o=384, p=512, n=656)
SET_ROWS = (664, 512, 664, 512)

PARTS = ((0, 80), (80, SLOTS))
BOTH = (0, 1)
COPIES = 5


def lanes_of(parts):
    return HEADS * PARTS[parts[0]][0], HEADS * PARTS[parts[-1]][1]


def tiles_of(parts):
    first, end = lanes_of(parts)
    return [(a, min(a + 256, end)) for a in range(first, end, 256)]


def nt(a, b):
    return lax.dot_general(a, b, (((1,), (1,)), ((), ())), preferred_element_type=f32)


def tn(a, b):
    return lax.dot_general(a, b, (((0,), (0,)), ((), ())), preferred_element_type=f32)


def nn(a, b):
    return jnp.dot(a, b, preferred_element_type=f32)


def head_blocks(block):
    lane = lax.broadcasted_iota(jnp.int32, block.shape, 1)
    parts = []
    for h in range(HEADS):
        keep = (lane >= h * HEAD) & (lane < (h + 1) * HEAD)
        parts.append(jnp.where(keep, block, jnp.zeros_like(block)))
    return jnp.concatenate(parts, axis=0)


def diagonal(full):
    n = full.shape[1] // HEADS
    return jnp.concatenate(
        [full[h * HEAD : (h + 1) * HEAD, h * n : (h + 1) * n] for h in range(HEADS)], axis=0
    ).T


def chunk_rows(rows, parts):
    return (-(-rows // parts) + 7) // 8 * 8


def main_kernel(
    strips,
    windows,
    n_grid,
    feat_in,
    codes_in,
    cot_in,
    attend_in,
    output_in,
    expand_in,
    reduce_in,
    position_in,
    norms_in,
    *refs,
):
    states_in, refs = refs[:12], refs[12:]
    outs, refs = refs[:24], refs[24:]
    run(strips, windows, n_grid, feat_in, codes_in, cot_in, attend_in, output_in, expand_in,
        reduce_in, position_in, norms_in, states_in, outs, *refs)


def run(
    strips,
    windows,
    n_grid,
    feat_in,
    codes_in,
    cot_in,
    attend_in,
    output_in,
    expand_in,
    reduce_in,
    position_in,
    norms_in,
    states_in,
    outs,
    feat,
    codes_v,
    cot,
    wa,
    wo,
    we,
    wr,
    xt,
    mi,
    qs,
    ks,
    vs,
    probs,
    att,
    first_b,
    xh1,
    rs1,
    act,
    dgelu,
    xh2,
    rs2,
    crow,
    ccol,
    ctab,
    field_a,
    field_b,
    field_c,
    field_d,
    wide_a,
    wide_b,
    wide_c,
    wide_d,
    wide_e,
    wide_f,
    wide_g,
    wide_h,
    kept_v,
    kept_k,
    scores_s,
    d_br2,
    d_hid,
    d_br,
    d_att,
    d_res,
    ds_s,
    d_q,
    d_k,
    d_v,
    csend,
    crecv,
    hsend,
    hrecv,
    osend,
    orecv,
    grecv,
    bsend,
    brecv,
    *sums_and_sems,
):
    send_sem, recv_sem, in_sem, out_sem = sums_and_sems[-4:]
    T = windows * SLOTS
    cols = windows * WIN
    stride = cols + 8
    hw = WIN // 2
    hs = hw * WIN
    gi = lax.axis_index("grid")
    si = lax.axis_index("strip")
    core = lax.rem(si, 2)
    zi = lax.div(si, 2)
    n_z = strips // 2
    chips = n_grid * n_z
    chip = gi * n_z + zi
    prev = lax.rem(si + strips - 1, strips)
    nxt = lax.rem(si + 1, strips)
    sib = si + 1 - 2 * core
    others = []
    for dz in sorted(range(n_z), key=lambda d: -min(d, n_z - d)):
        for dg in reversed(range(n_grid)):
            if (dz, dg) != (0, 0):
                g_p, z_p = lax.rem(gi + dg, n_grid), lax.rem(zi + dz, n_z)
                others.append((g_p * n_z + z_p, (g_p, z_p * 2 + core)))

    block_v, input_v = outs[0:2]
    attend_w, output_w, expand_w, reduce_w, position, norms = outs[6:12]
    loads = {}
    for i, (src, dst) in enumerate(
        (
            (feat_in, feat),
            (codes_in, codes_v),
            (attend_in, attend_w),
            (position_in, position),
            (output_in, output_w),
            (expand_in, expand_w),
            (reduce_in, reduce_w),
            (norms_in, norms),
            (cot_in, cot),
        )
    ):
        loads[i] = pltpu.make_async_copy(src, dst, in_sem.at[i])
        loads[i].start()

    state_loads = []
    for i, (src, dst) in enumerate(zip(states_in, outs[12:24])):
        state_loads.append(pltpu.make_async_copy(src, dst, out_sem.at[i]))

    barrier = pltpu.get_barrier_semaphore()
    peers = [(gi, prev), (gi, nxt), (gi, sib)] + [device for _, device in others]
    for peer in peers:
        pl.semaphore_signal(barrier, inc=1, device_id=peer, device_id_type=MESH)

    def remote(src, dst, index, device):
        return pltpu.make_async_remote_copy(
            src_ref=src,
            dst_ref=dst,
            send_sem=send_sem.at[index],
            recv_sem=recv_sem.at[index],
            device_id=device,
            device_id_type=MESH,
        )

    class Total:
        def __init__(self, number):
            self.g, self.s1, self.r1, self.s2, self.r2 = sums_and_sems[
                number * 5 : number * 5 + 5
            ]
            self.out = outs[2 + number]
            self.c = chunk_rows(SET_ROWS[number], 2 * chips)
            self.sem = COPIES + number * 4

        def rows(self, half, j):
            return pl.ds(pl.multiple_of((half * chips + j) * self.c, 8), self.c)

        def to_sibling(self):
            used = SET_ROWS[number_of(self)]
            if used < 2 * chips * self.c:
                self.g[used:] = jnp.zeros((2 * chips * self.c - used, D), f32)
            for j in range(chips):
                self.s1[j] = self.g[self.rows(1 - core, j)].astype(bf16)
            self.first = remote(self.s1, self.r1, self.sem, (gi, sib))
            self.first.start()

        def to_chips(self):
            self.first.wait()
            for j in range(chips):
                both = self.g[self.rows(core, j)] + self.r1[j].astype(f32)
                self.s2[j] = both.astype(bf16)
            for number, device in others:
                remote(self.s2.at[number], self.r2.at[chip], self.sem + 1, device).start()
            self.r2[chip] = self.s2[chip]

        def all_arrived(self, buffer, index):
            bytes_of = buffer.at[pl.ds(0, chips - 1)]
            remote(bytes_of, bytes_of, index, (gi, sib)).wait()

        def spread(self):
            self.all_arrived(self.r2, self.sem + 1)
            total = self.r2[0].astype(f32)
            for j in range(1, chips):
                total = total + self.r2[j].astype(f32)
            self.out[core, chip] = total.astype(bf16)
            mine = self.out.at[core, chip]
            for number, device in others:
                remote(mine, mine, self.sem + 2, device).start()

        def share(self):
            self.all_arrived(self.r2, self.sem + 2)
            mine = self.out.at[core]
            self.last = remote(mine, mine, self.sem + 3, (gi, sib))
            self.last.start()

        def done(self):
            self.last.wait()

    totals = [Total(n) for n in range(4)]
    number_of = totals.index
    def put(l, name, value, rows):
        total, table = (totals[3 if l else 1], FEED) if name in FEED else (totals[0 if l else 2], REST)
        total.g[table[name] : table[name] + rows] = value

    def code_tables(l, table):
        low = table.astype(bf16)
        lane = lax.broadcasted_iota(jnp.int32, (16, LANES), 1).astype(f32)
        row = lax.broadcasted_iota(jnp.int32, (16, LANES), 0).astype(f32)
        cut, end = PARTS[0][1], PARTS[1][1]
        lane_b = lane - HEADS * cut
        slot_a = lane - cut * jnp.floor((lane + 0.5) * (1.0 / cut))
        slot_b = lane_b - (end - cut) * jnp.floor((lane_b + 0.5) * (1.0 / (end - cut))) + cut
        slot = jnp.where(lane_b < 0.0, slot_a, slot_b)
        slot_r = jnp.floor((slot + 0.5) * (1.0 / WIN))
        slot_c = slot - WIN * slot_r
        pick_r = (slot_r == row).astype(bf16)
        ctab[...] = tn(low, pick_r)
        pick_c = (slot_c == row).astype(f32)[0:WIN]
        for w in range(windows):
            part = ctab[w * WIN : (w + 1) * WIN, :]
            crow[l, w] = jnp.sum(part * pick_c, axis=0, keepdims=True)
        token = lax.broadcasted_iota(jnp.int32, (SLOTS, 128), 0).astype(f32)
        place = lax.broadcasted_iota(jnp.int32, (SLOTS, 128), 1).astype(f32)
        token_r = jnp.floor((token + 0.5) * (1.0 / WIN))
        token_c = token - WIN * token_r
        row_of = (token_r == place).astype(bf16)[:, 0:16]
        spread = nn(row_of, low)
        for w in range(windows):
            chosen = jnp.where(place == token_c + w * WIN, spread, 0.0)
            value = jnp.sum(chosen, axis=1, keepdims=True)
            ccol[l, w * SLOTS : (w + 1) * SLOTS] = jnp.broadcast_to(value, (SLOTS, 128))

    every = range(windows)

    def window_rows(w):
        return slice(w * SLOTS, (w + 1) * SLOTS)

    def in_turn(chosen, before, middle, after):
        before(chosen[0])
        for i, w in enumerate(chosen):
            if i + 1 < len(chosen):
                before(chosen[i + 1])
            middle(w)
            if i > 0:
                after(chosen[i - 1])
        after(chosen[-1])

    def rows_of(w, p):
        return slice(w * SLOTS + PARTS[p][0], w * SLOTS + PARTS[p][1])

    def take(ref, parts):
        if parts == BOTH:
            return ref[...]
        return jnp.concatenate([ref[rows_of(w, p)] for w in every for p in parts], axis=0)

    def give(ref, parts, value):
        if parts == BOTH:
            ref[...] = value
            return
        n = value.shape[0] // windows
        for w in every:
            ref[rows_of(w, parts[0])] = value[w * n : (w + 1) * n]

    def blocks(ref, w, parts):
        return jnp.concatenate([head_blocks(ref[rows_of(w, p)]) for p in parts], axis=0)

    def diagonals(full, parts):
        first, _ = lanes_of(parts)
        found = []
        for p in parts:
            a, b = lanes_of((p,))
            found.append(diagonal(full[:, a - first : b - first]))
        return found

    def project(l):
        x = xt[l]
        m = (x.astype(f32) + jnp.concatenate([position[l]] * windows, axis=0)).astype(bf16)
        mi[l] = m
        qk = nn(m, wa[l, :, 0 : 2 * D])
        qs[l] = (qk[:, 0:D] * HEAD ** (-0.5)).astype(bf16)
        ks[l] = qk[:, D : 2 * D].astype(bf16)
        vs[l] = nn(x, wa[l, :, 2 * D : 3 * D]).astype(bf16)

    def attend(l, parts):
        first, end = lanes_of(parts)

        def scores_of(w):
            scores_s[w, :, first:end] = nt(ks[l, window_rows(w)], blocks(qs.at[l], w, parts))

        def soften(w):
            one = window_rows(w)
            cc = ccol[l, one]
            cr = crow[l, w]
            for a, b in tiles_of(parts):
                same = jnp.concatenate([cc] * ((b - a) // 128), axis=1) == cr[:, a:b]
                scores = jnp.where(same, scores_s[w, :, a:b], -1000000000.0)
                top = jnp.max(scores, axis=0, keepdims=True)
                weights = jnp.exp(scores - top)
                total = jnp.sum(weights, axis=0, keepdims=True)
                probs[l, one, a:b] = (weights * (1.0 / total)).astype(bf16)

        def mix(w):
            one = window_rows(w)
            full = nn(vs[l, one].T, probs[l, one, first:end])
            for p, value in zip(parts, diagonals(full, parts)):
                att[l, rows_of(w, p)] = value.astype(bf16)

        in_turn(every, scores_of, soften, mix)

    def feed_forward(l, parts, out):
        r = take(xt.at[l], parts).astype(f32) + nn(take(att.at[l], parts), wo[l])
        c = r - jnp.mean(r, axis=1, keepdims=True)
        s = lax.rsqrt(jnp.mean(c * c, axis=1, keepdims=True) + 1e-05)
        n = c * s
        give(xh1.at[l], parts, n)
        give(rs1.at[l], parts, jnp.broadcast_to(s, n.shape))
        first = n * norms[l, 0:1] + norms[l, 1:2]
        fb = first.astype(bf16)
        give(first_b.at[l], parts, fb)
        h = nn(fb, we[l])
        h2 = h * h
        t = jnp.tanh(0.7978845608028654 * h * (1.0 + 0.044715 * h2))
        act_b = (0.5 * h * (1.0 + t)).astype(bf16)
        give(act.at[l], parts, act_b)
        slope = 0.7978845608028654 * (1.0 + 3.0 * 0.044715 * h2)
        give(dgelu.at[l], parts, 0.5 * (1.0 + t) + 0.5 * h * (1.0 - t * t) * slope)
        r = first + nn(act_b, wr[l])
        c = r - jnp.mean(r, axis=1, keepdims=True)
        s = lax.rsqrt(jnp.mean(c * c, axis=1, keepdims=True) + 1e-05)
        n = c * s
        give(xh2.at[l], parts, n)
        give(rs2.at[l], parts, jnp.broadcast_to(s, n.shape))
        second = n * norms[l, 2:3] + norms[l, 3:4]
        second = jnp.where(take(ccol.at[l], parts) > 0.0, second, 0.0)
        give(out, parts, second.astype(bf16).astype(f32))

    def norm_back(d, gain, n, s):
        dn = d * gain
        m1 = jnp.mean(dn, axis=1, keepdims=True)
        m2 = jnp.mean(dn * n, axis=1, keepdims=True)
        return s * (dn - m1 - n * m2)

    def dense_backward(l, parts, grad_out):
        d = jnp.where(take(ccol.at[l], parts) > 0.0, take(grad_out, parts), 0.0)
        n2 = take(xh2.at[l], parts)
        bias2 = jnp.sum(d, axis=0, keepdims=True)
        gain2 = jnp.sum(d * n2, axis=0, keepdims=True)
        d2 = norm_back(d, norms[l, 2:3], n2, take(rs2.at[l], parts))
        b2 = d2.astype(bf16)
        give(d_br2, parts, b2)
        dh = (nt(b2, wr[l]) * take(dgelu.at[l], parts)).astype(bf16)
        give(d_hid, parts, dh)
        d1 = d2 + nt(dh, we[l])
        n1 = take(xh1.at[l], parts)
        bias1 = jnp.sum(d1, axis=0, keepdims=True)
        gain1 = jnp.sum(d1 * n1, axis=0, keepdims=True)
        dr = norm_back(d1, norms[l, 0:1], n1, take(rs1.at[l], parts))
        give(d_res, parts, dr)
        b1 = dr.astype(bf16)
        give(d_br, parts, b1)
        give(d_att, parts, nt(b1, wo[l]).astype(bf16))
        return [gain1, bias1, gain2, bias2]

    def norm_grads(l, parts):
        lines = [sum(lines) for lines in zip(*parts)] + [jnp.zeros((4, D), f32)]
        put(l, "n", jnp.concatenate(lines, axis=0), 8)

    def feed_forward_grads(l):
        put(l, "r", tn(act[l], d_br2[...]), FF)
        d_expand = tn(first_b[l], d_hid[...])
        put(l, "e", jnp.concatenate([d_expand[:, 0:D], d_expand[:, D : 2 * D]], axis=0), FF)

    def attention_backward(l, parts, add_to=None, keep=None):
        first, end = lanes_of(parts)

        def put_rows(which, target, rows, value):
            if keep is not None:
                keep[which][rows] = value
                return
            if add_to is not None:
                value = value + add_to[which][rows]
            target[rows] = value.astype(bf16)

        def d_probs_of(w):
            rows = window_rows(w)
            db = blocks(d_att, w, parts)
            put_rows(0, d_v, rows, nn(probs[l, rows, first:end], db))
            scores_s[w, :, first:end] = nt(vs[l, rows], db)

        def d_soften(w):
            rows = window_rows(w)
            for a, b in tiles_of(parts):
                dp = scores_s[w, :, a:b]
                p = probs[l, rows, a:b].astype(f32)
                ds = p * (dp - jnp.sum(dp * p, axis=0, keepdims=True))
                ds_s[rows, a:b] = ds.astype(bf16)

        def d_mix(w):
            rows = window_rows(w)
            ds = ds_s[rows, first:end]
            put_rows(1, d_k, rows, nn(ds, blocks(qs.at[l], w, parts)))
            full = nn(ks[l, rows].T, ds)
            for p, value in zip(parts, diagonals(full, parts)):
                d_q[rows_of(w, p)] = (value * HEAD ** (-0.5)).astype(bf16)

        in_turn(every, d_probs_of, d_soften, d_mix)

    def attention_grads(l):
        put(l, "o", tn(att[l], d_br[...]), D)
        put(l, "q", tn(mi[l], d_q[...]), D)
        put(l, "k", tn(mi[l], d_k[...]), D)
        put(l, "v", tn(xt[l], d_v[...]), D)
        d_pos = jnp.zeros((SLOTS, D), f32)
        for part, columns in ((d_q, slice(0, D)), (d_k, slice(D, 2 * D))):
            total = part[0:SLOTS].astype(f32)
            for w in range(1, windows):
                total = total + part[window_rows(w)].astype(f32)
            high = total.astype(bf16)
            low = (total - high.astype(f32)).astype(bf16)
            d_pos = d_pos + nt(high, wa[l, :, columns]) + nt(low, wa[l, :, columns])
        put(l, "p", d_pos, SLOTS)

    def input_gradient(l, out):
        d = nt(d_q[...], wa[l, :, 0:D]) + nt(d_k[...], wa[l, :, D : 2 * D])
        out[...] = d_res[...] + d + nt(d_v[...], wa[l, :, 2 * D : 3 * D])

    def lower(l):
        wa[l] = attend_w[l].astype(bf16)
        wo[l] = output_w[l].astype(bf16)
        we[l] = expand_w[l].astype(bf16)
        wr[l] = reduce_w[l].astype(bf16)

    def to_windows(source, target, rows):
        for w in every:
            for r in rows:
                a = w * SLOTS + r * WIN
                target[a : a + WIN] = source[r * stride + w * WIN : r * stride + (w + 1) * WIN]

    def wrap_ends(field, rows):
        for r in rows:
            field[r * stride + cols : r * stride + cols + hw] = field[r * stride : r * stride + hw]

    def wrap_starts(field, rows):
        for r in rows:
            field[r * stride : r * stride + hw] = field[r * stride + cols : r * stride + cols + hw]

    def to_shifted(source, target, rows):
        for w in every:
            for r in rows:
                a = w * SLOTS + r * WIN
                b = r * stride + w * WIN + hw
                target[a : a + WIN] = source[b : b + WIN]

    def from_shifted(source, source_rows, field, first_row):
        for w in every:
            for r in range(hw):
                a = w * source_rows + r * WIN
                b = (r + first_row) * stride + w * WIN + hw
                field[b : b + WIN] = source[a : a + WIN]

    top, bottom = range(hw), range(hw, WIN)

    loads[0].wait()
    for r in range(WIN):
        field_a[r * stride : r * stride + cols] = feat[r].astype(f32)
    to_windows(field_a, wide_a, range(WIN))
    xt[0] = wide_a[...].astype(bf16)
    loads[1].wait()
    csend[...] = jnp.zeros((16, 128), f32)
    for r in range(WIN):
        csend[r : r + 1, 0:cols] = codes_v[r].astype(f32)
    code_tables(0, csend[...])
    for i in range(2, 8):
        loads[i].wait()
    lower(0)
    project(0)
    attend(0, (0,))
    feed_forward(0, (0,), wide_b)
    for w in every:
        hsend[w] = wide_b[w * SLOTS : w * SLOTS + hs].astype(bf16)
    pl.semaphore_wait(barrier, len(peers))
    codes_copy = remote(csend, crecv, 0, (gi, prev))
    codes_copy.start()
    halo_copy = remote(hsend, hrecv, 1, (gi, prev))
    halo_copy.start()
    for load in state_loads:
        load.start()

    attend(0, (1,))
    feed_forward(0, (1,), wide_b)
    lower(1)
    for w in every:
        for r in top:
            a = w * SLOTS + (r + hw) * WIN
            field_b[r * stride + w * WIN : r * stride + (w + 1) * WIN] = wide_b[a : a + WIN]
    wrap_ends(field_b, top)
    to_shifted(field_b, wide_c, top)
    loads[8].wait()
    for r in top:
        field_c[r * stride : r * stride + cols] = cot[r + hw].astype(f32)
    wrap_ends(field_c, top)
    to_shifted(field_c, wide_f, top)
    codes_copy.wait()
    own = csend[...]
    other = crecv[...]
    table = jnp.concatenate([own[hw:WIN], other[0:hw], jnp.zeros((4, 128), f32)], axis=0)
    table = jnp.concatenate(
        [table[:, hw:cols], table[:, 0:hw], jnp.zeros((16, 128 - cols), f32)], axis=1
    )
    code_tables(1, table)

    halo_copy.wait()
    cot_copy = remote(cot_in.at[pl.ds(0, hw)], grecv, 2, (gi, prev))
    cot_copy.start()
    for w in every:
        wide_d[w * hs : (w + 1) * hs] = hrecv[w].astype(f32)
        for r in top:
            x = w * hs + r * WIN
            y = (r + hw) * stride + w * WIN
            field_b[y : y + WIN] = wide_d[x : x + WIN]
    wrap_ends(field_b, bottom)
    to_shifted(field_b, wide_c, bottom)
    xt[1] = wide_c[...].astype(bf16)
    project(1)
    attend(1, BOTH)
    feed_forward(1, BOTH, wide_e)

    for w in every:
        osend[w] = wide_e[w * SLOTS + hs : (w + 1) * SLOTS].astype(bf16)
    out_copy = remote(osend, orecv, 3, (gi, nxt))
    out_copy.start()

    cot_copy.wait()
    for r in top:
        field_c[(r + hw) * stride : (r + hw) * stride + cols] = grecv[r].astype(f32)
    wrap_ends(field_c, bottom)
    to_shifted(field_c, wide_f, bottom)
    norm_parts = [dense_backward(1, BOTH, wide_f)]
    feed_forward_grads(1)
    totals[3].to_sibling()
    attention_backward(1, BOTH)
    input_gradient(1, wide_g)
    for w in every:
        bsend[w] = wide_g[w * SLOTS + hs : (w + 1) * SLOTS].astype(bf16)
    back_copy = remote(bsend, brecv, 4, (gi, nxt))
    back_copy.start()

    totals[3].to_chips()
    norm_grads(1, norm_parts)
    attention_grads(1)
    totals[0].to_sibling()
    from_shifted(wide_g, SLOTS, field_d, hw)
    wrap_starts(field_d, bottom)
    to_windows(field_d, wide_h, bottom)
    for w in every:
        late = slice(w * SLOTS + hs, (w + 1) * SLOTS)
        wide_h[late] = wide_h[late].astype(bf16).astype(f32)
    norm_parts = [dense_backward(0, (1,), wide_h)]
    attention_backward(0, (1,), keep=(kept_v, kept_k))

    back_copy.wait()
    totals[0].to_chips()
    for w in every:
        wide_d[w * hs : (w + 1) * hs] = brecv[w].astype(f32)
    from_shifted(wide_d, hs, field_d, 0)
    wrap_starts(field_d, top)
    to_windows(field_d, wide_h, top)
    norm_parts.append(dense_backward(0, (0,), wide_h))
    feed_forward_grads(0)
    totals[1].to_sibling()
    totals[3].spread()
    attention_backward(0, (0,), add_to=(kept_v, kept_k))
    norm_grads(0, norm_parts)
    attention_grads(0)
    totals[2].to_sibling()
    totals[1].to_chips()
    totals[2].to_chips()
    input_gradient(0, wide_a)
    for w in every:
        for r in range(WIN):
            a = w * SLOTS + r * WIN
            field_a[r * stride + w * WIN : r * stride + (w + 1) * WIN] = wide_a[a : a + WIN]
    for r in range(WIN):
        input_v[r] = field_a[r * stride : r * stride + cols]
    out_copy.wait()
    for w in every:
        wide_d[w * hs : (w + 1) * hs] = orecv[w].astype(f32)
    from_shifted(wide_d, hs, field_c, 0)
    from_shifted(wide_e, SLOTS, field_c, hw)
    wrap_starts(field_c, range(WIN))
    for r in range(WIN):
        block_v[r] = field_c[r * stride : r * stride + cols].astype(bf16)
    totals[0].spread()
    totals[1].spread()
    totals[2].spread()
    totals[3].share()
    totals[0].share()
    totals[1].share()
    totals[2].share()
    for load in state_loads:
        load.wait()
    for total in totals:
        total.done()


def main_call(strips, windows, cols, n_grid):
    T = windows * SLOTS
    hw = WIN // 2
    chips = n_grid * strips // 2
    vm = pltpu.VMEM
    hs = hw * WIN
    scratch = [
        vm((WIN, cols, D), bf16),
        vm((WIN, 1, cols), jnp.int32),
        vm((WIN, cols, D), bf16),
        vm((2, D, 3 * D), bf16),
        vm((2, D, D), bf16),
        vm((2, D, FF), bf16),
        vm((2, FF, D), bf16),
        vm((2, T, D), bf16),
        vm((2, T, D), bf16),
        vm((2, T, D), bf16),
        vm((2, T, D), bf16),
        vm((2, T, D), bf16),
        vm((2, T, LANES), bf16),
        vm((2, T, D), bf16),
        vm((2, T, D), bf16),
        vm((2, T, D), f32),
        vm((2, T, D), f32),
        vm((2, T, FF), bf16),
        vm((2, T, FF), f32),
        vm((2, T, D), f32),
        vm((2, T, D), f32),
        vm((2, windows, 1, LANES), f32),
        vm((2, T, D), f32),
        vm((128, LANES), f32),
        *[vm((WIN * (cols + 8), D), f32) for _ in range(4)],
        *[vm((T, D), f32) for _ in range(10)],
        vm((windows, SLOTS, LANES), f32),
        vm((T, D), bf16),
        vm((T, FF), bf16),
        vm((T, D), bf16),
        vm((T, D), bf16),
        vm((T, D), f32),
        vm((T, LANES), bf16),
        vm((T, D), bf16),
        vm((T, D), bf16),
        vm((T, D), bf16),
        vm((16, 128), f32),
        vm((16, 128), f32),
        vm((windows, hs, D), bf16),
        vm((windows, hs, D), bf16),
        vm((windows, hs, D), bf16),
        vm((windows, hs, D), bf16),
        vm((hw, cols, D), bf16),
        vm((windows, hs, D), bf16),
        vm((windows, hs, D), bf16),
    ]
    outs = []
    for rows in SET_ROWS:
        c = chunk_rows(rows, 2 * chips)
        scratch += [
            vm((2 * chips * c, D), f32),
            vm((chips, c, D), bf16),
            vm((chips, c, D), bf16),
            vm((chips, c, D), bf16),
            vm((chips, c, D), bf16),
        ]
        outs.append(vm((2, chips, c, D), bf16))
    copies = COPIES + 4 * 4
    scratch += [pltpu.SemaphoreType.DMA((n,)) for n in (copies, copies, 9, 12)]
    params = [(2, D, 3 * D), (2, D, D), (2, D, FF), (2, FF, D), (2, SLOTS, D), (2, 4, D)]
    outs += [vm(shape, f32) for shape in params * 3]
    near = pl.BlockSpec(memory_space=pltpu.VMEM)
    far = pl.BlockSpec(memory_space=pl.ANY)
    return pl.pallas_call(
        functools.partial(main_kernel, strips, windows, n_grid),
        out_shape=(
            vm((WIN, cols, D), bf16),
            vm((WIN, cols, D), f32),
            *outs,
        ),
        in_specs=[far] * 21,
        out_specs=(near,) * 24,
        scratch_shapes=scratch,
        compiler_params=pltpu.CompilerParams(
            collective_id=0, has_side_effects=True, vmem_limit_bytes=40 * 1024 * 1024
        ),
    )


def lamb_kernel(*refs):
    grads_near = refs[0:4]
    block_near, input_near = refs[4:6]
    states = refs[6:24]
    block_out, input_out = refs[24:26]
    results_far = refs[26:44]
    clip_out, norms_out = refs[44:46]
    results = refs[46:64]
    out_sem, cell_sem = refs[64:66]
    cells = [
        pltpu.make_async_copy(block_near, block_out, cell_sem.at[0]),
        pltpu.make_async_copy(input_near, input_out, cell_sem.at[1]),
    ]
    for copy in cells:
        copy.start()
    stores = [
        pltpu.make_async_copy(results[i], results_far[i], out_sem.at[i]) for i in range(18)
    ]
    grads = [g[...].astype(f32).reshape(-1, D) for g in grads_near]
    clip_norm = jnp.sqrt(sum(jnp.sum(g * g, keepdims=True) for g in grads))
    clip_out[...] = clip_norm
    factor = clip_bound / jnp.maximum(clip_norm, clip_bound)
    fix_one = 1.0 / (1.0 - beta_one**STEP)
    fix_two = 1.0 / (1.0 - beta_two**STEP)

    def grad_rows(l, name, start, rows):
        if name in FEED:
            number, table = (3 if l else 1), FEED
        else:
            number, table = (0 if l else 2), REST
        return grads[number][table[name] + start : table[name] + start + rows]

    def step(index, where, grad, decay):
        grad = grad * factor
        old = states[index][where]
        moment = beta_one * states[6 + index][where] + (1.0 - beta_one) * grad
        square = beta_two * states[12 + index][where] + (1.0 - beta_two) * grad * grad
        results[6 + index][where] = moment
        results[12 + index][where] = square
        direction = moment * fix_one / (jnp.sqrt(square * fix_two) + epsilon)
        if decay:
            direction = direction + weight_decay * old
        results[index][where] = direction
        return old, direction

    found = {}
    order = ((0, "qkv", D), (2, "ee", D), (3, "r", FF), (4, "p", SLOTS), (1, "o", D))
    for index, names, height in order:
        for l in range(2):
            weight_sum, step_sum = [], []
            for b, name in enumerate(names):
                where = (l, slice(None), slice(b * D, (b + 1) * D))
                grad = grad_rows(l, name, b * D if name == "e" else 0, height)
                old, direction = step(index, where, grad, True)
                weight_sum.append(jnp.sum(old * old, axis=0, keepdims=True))
                step_sum.append(jnp.sum(direction * direction, axis=0, keepdims=True))
            found[l, index] = tuple(
                jnp.sqrt(jnp.sum(sum(parts), axis=1, keepdims=True))
                for parts in (weight_sum, step_sum)
            )
        for kind in (1, 2):
            stores[6 * kind + index].start()
    for index, names, _ in order:
        for l in range(2):
            weight_norm, step_norm = found[l, index]
            scale = learn_rate * weight_norm / (step_norm + epsilon)
            results[index][l] = states[index][l] - scale * results[index][l]
        stores[index].start()
    for l in range(2):
        old, direction = step(5, (l,), grad_rows(l, "n", 0, 4), False)
        weight_norm = jnp.sqrt(jnp.sum(old * old, axis=1, keepdims=True))
        step_norm = jnp.sqrt(jnp.sum(direction * direction, axis=1, keepdims=True))
        results[5][l] = old - learn_rate * weight_norm / (step_norm + epsilon) * direction
        for r in range(4):
            found[l, 5 + r] = (weight_norm[r : r + 1], step_norm[r : r + 1])
        row = lax.broadcasted_iota(jnp.int32, (2, 9), 0)
        lane = lax.broadcasted_iota(jnp.int32, (2, 9), 1)
        table = jnp.zeros((2, 9), f32)
        for t in range(9):
            for j in range(2):
                value = jnp.broadcast_to(found[l, t][j], (2, 9))
                table = jnp.where((row == j) & (lane == t), value, table)
        norms_out[l] = table
    for kind in range(3):
        stores[6 * kind + 5].start()
    for copy in stores + cells:
        copy.wait()


def lamb_call(grads, block_output, input_grad, states):
    whole = pl.BlockSpec(memory_space=pltpu.VMEM)
    far = pl.BlockSpec(memory_space=pl.ANY)
    like = lambda a: jax.ShapeDtypeStruct(a.shape, a.dtype)
    out = [like(block_output), like(input_grad)]
    out += [like(a) for a in states]
    out += [jax.ShapeDtypeStruct((1, 1), f32), jax.ShapeDtypeStruct((2, 2, 9), f32)]
    near = [pltpu.VMEM(a.shape, a.dtype) for a in states]
    return pl.pallas_call(
        lamb_kernel,
        out_shape=out,
        in_specs=[whole] * 24,
        out_specs=[far] * 20 + [whole] * 2,
        scratch_shapes=near + [pltpu.SemaphoreType.DMA((n,)) for n in (18, 2)],
        compiler_params=pltpu.CompilerParams(vmem_limit_bytes=32 * 1024 * 1024),
    )(*grads, block_output, input_grad, *states)


def body(mesh, features, cell_frame, cotangent, *rest):
    cols = features.shape[2]
    call = main_call(mesh.shape["strip"], cols // WIN, cols, mesh.shape["grid"])
    cell_frame = cell_frame.reshape(WIN, 1, cols)
    held = [
        pltpu.with_memory_space_constraint(a, pltpu.HBM)
        for a in (features[0], cell_frame, cotangent[0], *rest)
    ]
    found = call(*held)
    out = lamb_call(found[2:6], found[0], found[1], found[6:24])
    norms = jnp.swapaxes(out[21], 1, 2)
    return (out[0][None], out[1][None], *out[2:20], out[20].reshape(()), norms)


def solution(mesh):
    cells = P("grid", "strip", None, None)
    return jax.shard_map(
        functools.partial(body, mesh),
        mesh=mesh,
        in_specs=(cells, P("grid", "strip", None), cells) + (P(),) * 18,
        out_specs=(cells, cells) + (P(),) * 20,
        check_vma=False,
    )
```
